32 devices in a mesh: wide: 16 (over z, y, core), narrow: 2 (over x).
Axes of the slice: x: 2, y: 2, z: 4, core: 2. Of those that a mesh axis runs over, the one named last changes fastest.
Arguments:
- inputs: bfloat16 [2, 24576, 768], P(None, ('wide', 'narrow')), may hold values from -6 to 6
- coords: float32 [2, 2, 24576], P(None, None, ('wide', 'narrow')), may hold values from 0 to 1
- neighbours: int32 [2, 40, 24576], P(None, None, ('wide', 'narrow')), may hold values from 0 to 767, as said below
- counts: int32 [2, 24576], P(None, ('wide', 'narrow')), may hold values from 1 to 40, as said below
- doc_length: int32 [2, 32], P(None, ('wide', 'narrow')), may hold values from 384 to 768, as said below
- self_one: bfloat16 [768, 768], P(('wide', 'narrow')), may hold values from -0.21875 to 0.21875
- near_one: bfloat16 [768, 768], P(('wide', 'narrow')), may hold values from -0.4375 to 0.4375
- self_two: bfloat16 [768, 768], P(('wide', 'narrow')), may hold values from -0.21875 to 0.21875
- near_two: bfloat16 [768, 768], P(('wide', 'narrow')), may hold values from -0.4375 to 0.4375
- edge_proj: float32 [2, 768], replicated, may hold values from -4 to 4
- qkv_proj: bfloat16 [768, 2304], P(('wide', 'narrow')), may hold values from -0.21875 to 0.21875
- out_proj: bfloat16 [768, 768], P(('wide', 'narrow')), may hold values from -0.875 to 0.875
- up_proj: bfloat16 [768, 3072], P(('wide', 'narrow')), may hold values from -0.21875 to 0.21875
- down_proj: bfloat16 [3072, 768], P(('wide', 'narrow')), may hold values from -0.109375 to 0.109375
- norm_gains: float32 [3, 768], replicated, may hold values from 0.5 to 1.5
- norm_shifts: float32 [3, 768], replicated, may hold values from -1.5 to 1.5
- distance_rate: float32 [12], replicated, may hold values from 0.2 to 1
- order_rate: float32 [12], replicated, may hold values from -1 to 1
- cotangent: bfloat16 [2, 24576, 768], P(None, ('wide', 'narrow')), may hold values from -6 to 6
Outputs:
- outputs: bfloat16 [2, 24576, 768], P(None, ('wide', 'narrow'))
- input_grad: float32 [2, 24576, 768], P(None, ('wide', 'narrow'))
- grad_self_one: float32 [768, 768], P(('wide', 'narrow'))
- grad_near_one: float32 [768, 768], P(('wide', 'narrow'))
- grad_self_two: float32 [768, 768], P(('wide', 'narrow'))
- grad_near_two: float32 [768, 768], P(('wide', 'narrow'))
- grad_edge: float32 [2, 768], replicated
- grad_qkv: float32 [768, 2304], P(('wide', 'narrow'))
- grad_out: float32 [768, 768], P(('wide', 'narrow'))
- grad_up: float32 [768, 3072], P(('wide', 'narrow'))
- grad_down: float32 [3072, 768], P(('wide', 'narrow'))
- grad_gains: float32 [3, 768], replicated
- grad_shifts: float32 [3, 768], replicated
- grad_distance: float32 [12], replicated
- grad_order: float32 [12], replicated
The draws below stay inside these ranges and needn't reach their ends.
Inputs may be any that keep to these rules, and one draw needn't show every extreme that they name: A token's neighbours are positions in its own row of 768 tokens, within 64 of its own position. `counts`: slots at or beyond a token's count are padding. `doc_length`: the rest of the row after the document is padding.
All inputs are finite; a program needn't handle non-finite values.
Results may differ from the reference program's by a relative error of at most 0.015.
Values may be sent and summed in bfloat16 or wider, within the bound.
A program may use at most 256 MiB of HBM per device.

```python
import jax
import jax.numpy as jnp
from jax import lax

D = 768
HEADS = 12
HEAD = 64
FF = 3072
RADIUS = 128
RG = 64
K = 40
MICRO = 2
TOK_MB = 768
TOKENS = 24576


def draw_neighbours(key, part):
    key = jax.random.fold_in(key, 11)
    offsets = jax.random.randint(key, (MICRO, K, TOKENS), -RG, RG + 1)
    positions = jnp.arange(TOKENS, dtype=jnp.int32) % TOK_MB
    return jnp.clip(positions[None, None, :] + offsets, 0, TOK_MB - 1).astype(jnp.int32)


def draw_counts(key, part):
    key = jax.random.fold_in(key, 23)
    drawn = jax.random.randint(key, (MICRO, TOKENS), 1, K + 1)
    positions = jnp.arange(TOKENS, dtype=jnp.int32) % TOK_MB
    drawn = jnp.where(positions[None, :] == 0, K, drawn)
    drawn = jnp.where(positions[None, :] == 1, 1, drawn)
    return drawn.astype(jnp.int32)


def draw_doc_length(key, part):
    key = jax.random.fold_in(key, 37)
    drawn = jax.random.randint(key, (MICRO, TOKENS // TOK_MB), TOK_MB // 2, TOK_MB + 1)
    column = jnp.arange(TOKENS // TOK_MB, dtype=jnp.int32)
    drawn = jnp.where(column[None, :] == 0, TOK_MB, drawn)
    drawn = jnp.where(column[None, :] == 1, TOK_MB // 2, drawn)
    return drawn.astype(jnp.int32)


def block_scale(own_key, extent, cuts, smallest, largest):
    level = 1.0
    for dim, shards_of in cuts:
        heights = jax.random.uniform(jax.random.fold_in(jax.random.fold_in(own_key, 6), dim), (shards_of,), jnp.float32, smallest / len(cuts), largest / len(cuts))
        level = level * jnp.repeat(jnp.exp(heights), extent[dim] // shards_of).reshape((-1,) + (1,) * (len(extent) - 1 - dim))
    return level


def normal_values(rng, shape, scale, bound, pieces=(), held_as=jnp.bfloat16):
    values = scale * jax.random.normal(rng, shape, jnp.float32)
    if pieces:
        values = values * block_scale(rng, shape, pieces, -0.22, 0.18)
    return jnp.clip(values, -bound, bound).astype(held_as)


def setup_inputs(seed: int = 0) -> dict:
    key_of = jax.random.split(jax.random.key(seed), 20)
    return {
        "inputs": normal_values(key_of[0], (MICRO, TOKENS, D), 1.0, 6.0, ((1, 32),)),
        "coords": jnp.clip(1.0 * jax.random.uniform(key_of[1], (MICRO, 2, TOKENS), jnp.float32) ** block_scale(key_of[1], (MICRO, 2, TOKENS), ((2, 32),), -0.2, 0.2), 0.0, 1.0),
        "neighbours": draw_neighbours(jax.random.fold_in(key_of[19], 71), 0),
        "counts": draw_counts(jax.random.fold_in(key_of[19], 71), 0),
        "doc_length": draw_doc_length(jax.random.fold_in(key_of[19], 71), 0),
        "self_one": normal_values(key_of[5], (D, D), D ** -0.5, 0.21875, ((0, 32),)),
        "near_one": normal_values(key_of[6], (D, D), (D // 4) ** -0.5, 0.4375, ((0, 32),)),
        "self_two": normal_values(key_of[7], (D, D), D ** -0.5, 0.21875, ((0, 32),)),
        "near_two": normal_values(key_of[8], (D, D), (D // 4) ** -0.5, 0.4375, ((0, 32),)),
        "edge_proj": normal_values(key_of[9], (2, D), 1.0, 4.0, (), jnp.float32),
        "qkv_proj": normal_values(key_of[10], (D, 3 * D), D ** -0.5, 0.21875, ((0, 32),)),
        "out_proj": normal_values(key_of[11], (D, D), (D // 16) ** -0.5, 0.875, ((0, 32),)),
        "up_proj": normal_values(key_of[12], (D, FF), D ** -0.5, 0.21875, ((0, 32),)),
        "down_proj": normal_values(key_of[13], (FF, D), FF ** -0.5, 0.109375, ((0, 32),)),
        "norm_gains": jnp.clip(1.0 + 0.1 * jax.random.normal(key_of[14], (3, D), jnp.float32), 0.5, 1.5),
        "norm_shifts": normal_values(key_of[15], (3, D), 0.3, 1.5, (), jnp.float32),
        "distance_rate": jnp.clip(jax.random.uniform(key_of[16], (HEADS,), jnp.float32, 0.2, 1.0), 0.2, 1.0),
        "order_rate": jnp.clip(jax.random.uniform(key_of[17], (HEADS,), jnp.float32, -1.0, 1.0), -1.0, 1.0),
        "cotangent": normal_values(key_of[18], (MICRO, TOKENS, D), 1.0, 6.0, ((1, 32),)),
    }


@jax.custom_vjp
def low(v):
    return lax.optimization_barrier(v.astype(jnp.bfloat16)).astype(jnp.float32)

@jax.custom_vjp
def low_back(v):
    return v

def low_keep(v):
    return (low(v), None)

def low_pass(kept, grad):
    return (grad,)

def back_keep(v):
    return (v, None)

def back_low(kept, grad):
    return (low(grad),)
low.defvjp(low_keep, low_pass)
low_back.defvjp(back_keep, back_low)

def matmul(left, right):
    return jnp.dot(left, right, precision=lax.Precision.HIGHEST)

def layer_norm(values, gain, shift):
    centre = values - lax.optimization_barrier(jnp.mean(values, axis=-1, keepdims=True))
    spread = lax.optimization_barrier(jnp.mean(centre * centre, axis=-1, keepdims=True))
    return centre * lax.rsqrt(spread + 1e-05) * gain + shift

def build_graph(neighbours, counts, coords, length):
    tokens_row = counts.shape[0]
    positions = jnp.arange(tokens_row, dtype=jnp.int32)
    later = positions >= length
    slots = jnp.arange(neighbours.shape[0], dtype=jnp.int32)[:, None]
    valid = (slots < counts[None, :]) & ((neighbours >= length) == later[None, :])

    def add_slot(slot, total):
        hit = (neighbours[slot][:, None] == positions[None, :]) & valid[slot][:, None]
        return total + hit.astype(jnp.float32)
    adjacency = lax.fori_loop(0, neighbours.shape[0], add_slot, jnp.zeros((tokens_row, tokens_row), jnp.float32))
    inverse = 1.0 / counts.astype(jnp.float32)
    points = coords.T
    edge = (matmul(adjacency, points) - lax.optimization_barrier(jnp.sum(adjacency, axis=1))[:, None] * points) * inverse[:, None]
    delta_x = coords[0][None, :] - coords[0][:, None]
    delta_y = coords[1][None, :] - coords[1][:, None]
    distance = jnp.log(1.0 + 16.0 * (delta_x * delta_x + delta_y * delta_y))
    order = jnp.tanh(4.0 * delta_x)
    allowed = (jnp.abs(positions[:, None] - positions[None, :]) <= RADIUS) & (later[:, None] == later[None, :])
    return (adjacency, inverse, edge, distance, order, allowed)

def row_forward(inputs, graph, weights):
    adjacency, inverse, edge, distance, order, allowed = graph
    self_one, near_one, self_two, near_two, edge_proj, qkv_proj, out_proj, up_proj, down_proj, norm_gains, norm_shifts, distance_rate, order_rate = weights
    tokens_row = inputs.shape[0]
    agg_one = low(inverse[:, None] * low_back(matmul(adjacency, inputs)))
    pre_one = low_back(matmul(inputs, self_one) + matmul(agg_one, near_one)) + matmul(edge, edge_proj)
    hidden_one = low(jax.nn.gelu(pre_one))
    agg_two = low(inverse[:, None] * low_back(matmul(adjacency, hidden_one)))
    branch = low_back(matmul(hidden_one, self_two) + matmul(agg_two, near_two))
    normed_one = layer_norm(inputs + branch, norm_gains[0], norm_shifts[0])
    qkv = low(low_back(matmul(low(normed_one), qkv_proj)))
    split = qkv.reshape(tokens_row, 3, HEADS, HEAD)
    queries, keys_all, values = (split[:, 0], split[:, 1], split[:, 2])
    raw = jnp.einsum('thd,shd->hts', queries, keys_all, precision=lax.Precision.HIGHEST) * 0.125
    raw = raw - distance_rate[:, None, None] * distance[None] + order_rate[:, None, None] * order[None]
    scores = jnp.where(allowed[None], low_back(raw), -1000000000.0)
    probs = jax.nn.softmax(scores, axis=-1)
    attended = jnp.einsum('hts,shd->thd', low(probs), values, precision=lax.Precision.HIGHEST)
    attended = low(low_back(attended.reshape(tokens_row, HEADS * HEAD)))
    normed_two = layer_norm(normed_one + low_back(matmul(attended, out_proj)), norm_gains[1], norm_shifts[1])
    up_pre = low_back(matmul(low(normed_two), up_proj))
    activated = low(jax.nn.gelu(up_pre))
    resid_three = normed_two + low_back(matmul(activated, down_proj))
    return layer_norm(resid_three, norm_gains[2], norm_shifts[2])

def reference(inputs, coords, neighbours, counts, doc_length, self_one, near_one, self_two, near_two, edge_proj, qkv_proj, out_proj, up_proj, down_proj, norm_gains, norm_shifts, distance_rate, order_rate, cotangent):
    rows = inputs.shape[1] // TOK_MB
    total_rows = MICRO * rows
    input_rows = inputs.astype(jnp.float32).reshape(total_rows, TOK_MB, D)
    cot_rows = cotangent.astype(jnp.float32).reshape(total_rows, TOK_MB, D)
    coord_rows = coords.reshape(MICRO, 2, rows, TOK_MB).transpose(0, 2, 1, 3).reshape(total_rows, 2, TOK_MB)
    neighbour_rows = neighbours.reshape(MICRO, K, rows, TOK_MB).transpose(0, 2, 1, 3).reshape(total_rows, K, TOK_MB)
    count_rows = counts.reshape(total_rows, TOK_MB)
    length_rows = doc_length.reshape(total_rows)
    weights = tuple((weight.astype(jnp.float32) for weight in (self_one, near_one, self_two, near_two, edge_proj, qkv_proj, out_proj, up_proj, down_proj, norm_gains, norm_shifts, distance_rate, order_rate)))

    def whole(input_all, weight_all):

        def one_row(item):
            input_one, coord_one, neighbour_one, count_one, length_one = item
            graph = build_graph(neighbour_one, count_one, coord_one, length_one)
            return row_forward(input_one, graph, weight_all)
        return lax.map(jax.checkpoint(one_row), (input_all, coord_rows, neighbour_rows, count_rows, length_rows))
    result, pullback = jax.vjp(whole, input_rows, weights)
    input_back, weight_back = pullback(cot_rows)
    return (result.reshape(MICRO, rows * TOK_MB, D).astype(jnp.bfloat16), input_back.reshape(MICRO, rows * TOK_MB, D), weight_back[0], weight_back[1], weight_back[2], weight_back[3], weight_back[4], weight_back[5], weight_back[6], weight_back[7], weight_back[8], weight_back[9], weight_back[10], weight_back[11], weight_back[12])
```

```python
import functools
import jax
import jax.numpy as jnp
from jax import lax
from jax.experimental import pallas as pl
from jax.experimental.pallas import tpu as pltpu
from jax.sharding import PartitionSpec as P

RADIUS = 128
REACH = 64
BLOCK = 128
WIDE = BLOCK + 2 * REACH
SPAN = BLOCK + 2 * RADIUS
FAR = 1e10
F32 = jnp.float32
LOW = jnp.bfloat16
VMEM = 60 * 2**20


def dot(left, right, dims):
    return lax.dot_general(left, right, ((dims[:1], dims[1:]), ((), ())), preferred_element_type=F32)


def nn(left, right):
    return dot(left, right, (1, 0))


def nt(left, right):
    return dot(left, right, (1, 1))


def tn(left, right):
    return dot(left, right, (0, 0))


def gelu_pair(pre):
    slope = 0.7978845608028654
    square = pre * pre
    half = 0.5 + 0.5 * jnp.tanh(pre * (slope + (slope * 0.044715) * square))
    act = pre * half
    deriv = half + act * (1.0 - half) * (2.0 * slope + (6.0 * slope * 0.044715) * square)
    return act, deriv


def norm_parts(values):
    centre = values - jnp.mean(values, axis=-1, keepdims=True)
    rstd = lax.rsqrt(jnp.mean(centre * centre, axis=-1, keepdims=True) + 1e-05)
    return centre * rstd, rstd


def norm_back(grad, unit, rstd, gain):
    scaled = grad * gain
    mean = jnp.mean(scaled, axis=-1, keepdims=True)
    along = jnp.mean(scaled * unit, axis=-1, keepdims=True)
    return rstd * (scaled - mean - unit * along)


def fold(values):
    rows, cols = values.shape
    return jnp.sum(values.reshape(rows // 8, 8, cols), axis=0)


def whole(shape, space=None):
    return pl.BlockSpec(shape, lambda *_: (0,) * len(shape), pipeline_mode=pl.Buffered(1))


def params(grid_rank, **more):
    return pltpu.CompilerParams(
        vmem_limit_bytes=VMEM, dimension_semantics=("arbitrary",) * grid_rank, **more
    )


def graph_kernel(
    length_ref, near_ref, count_ref, point_ref, x_ref, graph_ref, edge_w_ref, gain_ref, shift_ref,
    qkv_w_ref,
    adj_ref, cols_ref, agg1_ref, slope_ref, hidden_ref, agg2_ref, unit_ref, rstd_ref, normed_ref,
    low_ref, qkv_ref,
    pad_ref, point_pad, rel_ref,
):
    row = pl.program_id(0)
    slots, tokens = near_ref.shape[1:]
    width = x_ref.shape[2]
    blocks = tokens // BLOCK
    length = length_ref[row]
    zeros = jnp.zeros((REACH, width), LOW)
    pad_ref[pl.ds(0, REACH), :] = zeros
    pad_ref[pl.ds(tokens + REACH, REACH), :] = zeros
    pad_ref[pl.ds(REACH, tokens), :] = x_ref[0]
    points = point_ref[0]
    high = points.astype(LOW)
    rest = points - high.astype(F32)
    mid = rest.astype(LOW)
    tail = (rest - mid.astype(F32)).astype(LOW)
    split = jnp.concatenate(
        [high.astype(F32), mid.astype(F32), tail.astype(F32), jnp.ones((1, tokens), F32), jnp.zeros((9, tokens), F32)], axis=0
    )
    side = jnp.zeros((16, REACH), F32)
    point_pad[...] = jnp.concatenate([side, split, side], axis=1).astype(LOW)

    for b in range(blocks):
        lanes = slice(b * BLOCK, (b + 1) * BLOCK)
        near = near_ref[0, :, lanes]
        count = count_ref[0, :, lanes]
        place = lax.broadcasted_iota(jnp.int32, (1, BLOCK), 1) + b * BLOCK
        slot = lax.broadcasted_iota(jnp.int32, (slots, BLOCK), 0)
        same = (near >= length) == (place >= length)
        rel_ref[...] = jnp.where((slot < count) & same, near - (b * BLOCK - REACH), -1)
        spot = lax.broadcasted_iota(jnp.int32, (WIDE, BLOCK), 0)
        total = jnp.zeros((WIDE, BLOCK), F32)
        for s in range(slots):
            total = total + jnp.where(rel_ref[s : s + 1, :] == spot, 1.0, 0.0)
        adj = total.astype(LOW)
        adj_ref[0, b] = adj
        sums = nn(point_pad[:, b * BLOCK : b * BLOCK + WIDE], adj)
        inverse = 1.0 / count.astype(F32)
        here = points[:, lanes]
        edge = (sums[0:2] + sums[2:4] + sums[4:6] - sums[6:7] * here) * inverse
        lines = jnp.concatenate([edge, inverse, jnp.zeros((5, BLOCK), F32)], axis=0)
        cols = lines.T
        cols_ref[0, lanes, :] = cols
        agg = tn(adj, pad_ref[b * BLOCK : b * BLOCK + WIDE, :])
        agg1_ref[0, lanes, :] = (agg * cols[:, 2:3]).astype(LOW)

    chunk = 2 * BLOCK
    for c in range(tokens // chunk):
        part = slice(c * chunk, (c + 1) * chunk)
        pre = nn(x_ref[0, part, :], graph_ref[:, 0:width])
        pre = pre + nn(agg1_ref[0, part, :], graph_ref[:, width : 2 * width])
        pre = pre + cols_ref[0, part, 0:1] * edge_w_ref[0:1, :] + cols_ref[0, part, 1:2] * edge_w_ref[1:2, :]
        act, deriv = gelu_pair(pre)
        slope_ref[0, part, :] = deriv.astype(LOW)
        hidden_ref[0, part, :] = act.astype(LOW)
        pad_ref[REACH + c * chunk : REACH + (c + 1) * chunk, :] = act.astype(LOW)

    for b in range(blocks):
        lanes = slice(b * BLOCK, (b + 1) * BLOCK)
        agg = tn(adj_ref[0, b], pad_ref[b * BLOCK : b * BLOCK + WIDE, :])
        agg2_ref[0, lanes, :] = (agg * cols_ref[0, lanes, 2:3]).astype(LOW)

    for c in range(tokens // chunk):
        part = slice(c * chunk, (c + 1) * chunk)
        resid = x_ref[0, part, :].astype(F32) + nn(hidden_ref[0, part, :], graph_ref[:, 2 * width : 3 * width])
        resid = resid + nn(agg2_ref[0, part, :], graph_ref[:, 3 * width : 4 * width])
        unit, rstd = norm_parts(resid)
        unit_ref[0, part, :] = unit.astype(LOW)
        rstd_ref[0, part, :] = rstd
        normed = unit * gain_ref[0:1, :] + shift_ref[0:1, :]
        normed_ref[0, part, :] = normed
        low = normed.astype(LOW)
        low_ref[0, part, :] = low
        qkv_ref[0, part, :] = nn(low, qkv_w_ref[...]).astype(LOW)


def graph_forward(length, near, count, point, x, graph_w, edge_w, gains, shifts, qkv_w):
    rows, tokens, width = x.shape
    slots = near.shape[1]
    blocks = tokens // BLOCK
    wide = 3 * width
    per_row = lambda *shape: pl.BlockSpec((1,) + shape, lambda r: (r,) + (0,) * len(shape))
    out = lambda dtype, *shape: jax.ShapeDtypeStruct((rows,) + shape, dtype)
    return pl.pallas_call(
        graph_kernel,
        grid=(rows,),
        in_specs=[
            pl.BlockSpec(memory_space=pltpu.SMEM),
            per_row(slots, tokens),
            per_row(1, tokens),
            per_row(2, tokens),
            per_row(tokens, width),
            whole((width, 4 * width)),
            whole((2, width)),
            whole(gains.shape),
            whole(shifts.shape),
            whole((width, wide)),
        ],
        out_specs=[
            per_row(blocks, WIDE, BLOCK),
            per_row(tokens, 8),
            per_row(tokens, width),
            per_row(tokens, width),
            per_row(tokens, width),
            per_row(tokens, width),
            per_row(tokens, width),
            per_row(tokens, 1),
            per_row(tokens, width),
            per_row(tokens, width),
            per_row(tokens, wide),
        ],
        out_shape=[
            out(LOW, blocks, WIDE, BLOCK),
            out(F32, tokens, 8),
            out(LOW, tokens, width),
            out(LOW, tokens, width),
            out(LOW, tokens, width),
            out(LOW, tokens, width),
            out(LOW, tokens, width),
            out(F32, tokens, 1),
            out(F32, tokens, width),
            out(LOW, tokens, width),
            out(LOW, tokens, wide),
        ],
        scratch_shapes=[
            pltpu.VMEM((tokens + 2 * REACH, width), LOW),
            pltpu.VMEM((16, tokens + 2 * REACH), LOW),
            pltpu.VMEM((slots, BLOCK), jnp.int32),
        ],
        compiler_params=params(1),
        name="graph_forward",
    )(length, near, count, point, x, graph_w, edge_w, gains, shifts, qkv_w)


def fill_bias(length, point_ref, far_ref, order_ref):
    tokens = point_ref.shape[2]
    side = jnp.zeros((2, RADIUS), F32)
    padded = jnp.concatenate([side, point_ref[0], side], axis=1)
    tall = jnp.concatenate([padded, jnp.zeros((6, tokens + 2 * RADIUS), F32)], axis=0)
    for b in range(tokens // BLOCK):
        window = tall[:, b * BLOCK : b * BLOCK + SPAN].T
        key_x, key_y = window[:, 0:1], window[:, 1:2]
        lanes = slice(b * BLOCK, (b + 1) * BLOCK)
        delta_x = key_x - point_ref[0, 0:1, lanes]
        delta_y = key_y - point_ref[0, 1:2, lanes]
        dist = jnp.log(1.0 + 16.0 * (delta_x * delta_x + delta_y * delta_y))
        query = lax.broadcasted_iota(jnp.int32, (SPAN, BLOCK), 1) + b * BLOCK
        key = lax.broadcasted_iota(jnp.int32, (SPAN, BLOCK), 0) + (b * BLOCK - RADIUS)
        allowed = (jnp.abs(query - key) <= RADIUS) & ((query >= length) == (key >= length))
        allowed = allowed & (key >= 0) & (key < tokens)
        far_ref[b] = jnp.where(allowed, dist, FAR)
        order_ref[b] = jnp.tanh(4.0 * delta_x)


def pair_rows(values):
    lane = lax.broadcasted_iota(jnp.int32, values.shape, 1)
    zero = jnp.zeros_like(values)
    first = jnp.where(lane < BLOCK // 2, values, zero)
    second = jnp.where(lane < BLOCK // 2, zero, values)
    return jnp.concatenate([first, second], axis=0)


def pair_pick(values):
    lane = lax.broadcasted_iota(jnp.int32, (BLOCK, BLOCK), 1)
    return jnp.where(lane < BLOCK // 2, values[:BLOCK], values[BLOCK:])


def pad_rows(pad_ref, values):
    tokens = values.shape[0]
    zeros = jnp.zeros((RADIUS, values.shape[1]), pad_ref.dtype)
    pad_ref[pl.ds(0, RADIUS), :] = zeros
    pad_ref[pl.ds(RADIUS + tokens, RADIUS), :] = zeros
    pad_ref[pl.ds(RADIUS, tokens), :] = values


def attention_kernel(
    length_ref, dist_rate_ref, order_rate_ref, point_ref, q_ref, k_ref, v_ref,
    out_ref, probs_ref, far_out, order_out,
    keys, values,
):
    row, pair = pl.program_id(0), pl.program_id(1)

    @pl.when(pair == 0)
    def _():
        fill_bias(length_ref[row], point_ref, far_out.at[0], order_out.at[0])

    pad_rows(keys, k_ref[0])
    pad_rows(values, v_ref[0])
    for b in range(q_ref.shape[1] // BLOCK):
        lanes = slice(b * BLOCK, (b + 1) * BLOCK)
        window = slice(b * BLOCK, b * BLOCK + SPAN)
        queries = pair_rows(q_ref[0, lanes, :] * 0.125)
        raw = nt(keys[window, :], queries)
        far, order = far_out[0, b], order_out[0, b]
        sides = []
        for h in range(2):
            bias = order_rate_ref[2 * pair + h] * order - dist_rate_ref[2 * pair + h] * far
            scores = raw[:, h * BLOCK : (h + 1) * BLOCK] + bias
            grown = jnp.exp(scores - jnp.max(scores, axis=0, keepdims=True))
            scale = 1.0 / jnp.sum(grown, axis=0, keepdims=True)
            sides.append((grown * scale).astype(LOW))
        probs = jnp.concatenate(sides, axis=1)
        probs_ref[0, 0, b] = probs
        out_ref[0, lanes, :] = pair_pick(tn(probs, values[window, :])).astype(LOW)


def attention_forward(length, dist_rate, order_rate, point, qkv):
    rows, tokens, wide = qkv.shape
    width = wide // 3
    pairs = width // BLOCK
    blocks = tokens // BLOCK
    part = lambda k: pl.BlockSpec((1, tokens, BLOCK), lambda r, p: (r, 0, k * pairs + p))
    smem = pl.BlockSpec(memory_space=pltpu.SMEM)
    bias = pl.BlockSpec((1, blocks, SPAN, BLOCK), lambda r, p: (r, 0, 0, 0))
    return pl.pallas_call(
        attention_kernel,
        grid=(rows, pairs),
        in_specs=[smem, smem, smem, pl.BlockSpec((1, 2, tokens), lambda r, p: (r, 0, 0)), part(0), part(1), part(2)],
        out_specs=[
            part(0),
            pl.BlockSpec((1, 1, blocks, SPAN, 2 * BLOCK), lambda r, p: (r, p, 0, 0, 0)),
            bias,
            bias,
        ],
        out_shape=[
            jax.ShapeDtypeStruct((rows, tokens, width), LOW),
            jax.ShapeDtypeStruct((rows, pairs, blocks, SPAN, 2 * BLOCK), LOW),
            jax.ShapeDtypeStruct((rows, blocks, SPAN, BLOCK), F32),
            jax.ShapeDtypeStruct((rows, blocks, SPAN, BLOCK), F32),
        ],
        scratch_shapes=[pltpu.VMEM((tokens + 2 * RADIUS, BLOCK), LOW)] * 2,
        compiler_params=params(2),
        name="attention_forward",
    )(length, dist_rate, order_rate, point, qkv, qkv, qkv)


def attention_back_kernel(
    q_ref, k_ref, v_ref, grad_ref, probs_ref, far_ref, order_ref,
    dq_ref, dk_ref, dv_ref, rate_ref,
    keys, values, grad_keys, grad_values,
):
    pad_rows(keys, k_ref[0])
    pad_rows(values, v_ref[0])
    grad_keys[...] = jnp.zeros_like(grad_keys)
    grad_values[...] = jnp.zeros_like(grad_values)
    tokens = q_ref.shape[1]
    sums = [jnp.zeros((8, BLOCK), F32)] * 4
    for b in range(tokens // BLOCK):
        lanes = slice(b * BLOCK, (b + 1) * BLOCK)
        window = slice(b * BLOCK, b * BLOCK + SPAN)
        queries = pair_rows(q_ref[0, lanes, :] * 0.125)
        grads = pair_rows(grad_ref[0, lanes, :])
        probs_low = probs_ref[0, 0, b]
        back = nt(values[window, :], grads)
        dist = jnp.where(far_ref[0, b] < FAR, far_ref[0, b], 0.0)
        order = order_ref[0, b]
        sides = []
        for h in range(2):
            probs = probs_low[:, h * BLOCK : (h + 1) * BLOCK].astype(F32)
            part = back[:, h * BLOCK : (h + 1) * BLOCK]
            delta = jnp.sum(probs * part, axis=0, keepdims=True)
            scores = probs * (part - delta)
            sums[2 * h] = sums[2 * h] - fold(scores * dist)
            sums[2 * h + 1] = sums[2 * h + 1] + fold(scores * order)
            sides.append(scores.astype(LOW))
        scores_low = jnp.concatenate(sides, axis=1)
        grad_values[window, :] += nn(probs_low, grads)
        grad_keys[window, :] += nn(scores_low, queries)
        dq_ref[0, lanes, :] = (pair_pick(tn(scores_low, keys[window, :])) * 0.125).astype(LOW)
    dk_ref[0] = grad_keys[pl.ds(RADIUS, tokens), :].astype(LOW)
    dv_ref[0] = grad_values[pl.ds(RADIUS, tokens), :].astype(LOW)
    for k in range(4):
        rate_ref[0, 0, k] = sums[k]


def attention_backward(qkv, grad, probs, far, order):
    rows, tokens, wide = qkv.shape
    width = wide // 3
    pairs = width // BLOCK
    blocks = tokens // BLOCK
    part = lambda k: pl.BlockSpec((1, tokens, BLOCK), lambda r, p: (r, 0, k * pairs + p))
    bias = pl.BlockSpec((1, blocks, SPAN, BLOCK), lambda r, p: (r, 0, 0, 0))
    grads = jax.ShapeDtypeStruct((rows, tokens, width), LOW)
    return pl.pallas_call(
        attention_back_kernel,
        grid=(rows, pairs),
        in_specs=[
            part(0),
            part(1),
            part(2),
            part(0),
            pl.BlockSpec((1, 1, blocks, SPAN, 2 * BLOCK), lambda r, p: (r, p, 0, 0, 0)),
            bias,
            bias,
        ],
        out_specs=[part(0)] * 3 + [pl.BlockSpec((1, 1, 4, 8, BLOCK), lambda r, p: (r, p, 0, 0, 0))],
        out_shape=[grads] * 3 + [jax.ShapeDtypeStruct((rows, pairs, 4, 8, BLOCK), F32)],
        scratch_shapes=[pltpu.VMEM((tokens + 2 * RADIUS, BLOCK), LOW)] * 2
        + [pltpu.VMEM((tokens + 2 * RADIUS, BLOCK), F32)] * 2,
        compiler_params=params(2),
        name="attention_backward",
    )(qkv, qkv, qkv, grad, probs, far, order)


TILE = 256
PARTS = 6


def block_kernel(
    att_ref, normed_ref, cot_ref, out_w_ref, up_ref, down_ref, gain_ref, shift_ref,
    result_ref, grad_two_ref, grad_att_ref, grad_out_ref, grad_up_ref, grad_down_ref, norms_ref,
    act_all, up_all, second_all, down_all, attn_all, att_all, slope_tile,
):
    step = pl.program_id(0)
    width = att_ref.shape[1]
    steps = act_all.shape[1] // TILE
    piece = act_all.shape[2]

    @pl.when(step == 0)
    def _():
        norms_ref[...] = jnp.zeros_like(norms_ref)

    @pl.when(step < steps)
    def _():
        at = pl.ds(pl.multiple_of(step * TILE, TILE), TILE)
        att = att_ref[...]
        att_all[at, :] = att
        resid = normed_ref[...] + nn(att, out_w_ref[...])
        unit_two, rstd_two = norm_parts(resid)
        gain_two, gain_three = gain_ref[1:2, :], gain_ref[2:3, :]
        normed = unit_two * gain_two + shift_ref[1:2, :]
        second = normed.astype(LOW)
        second_all[at, :] = second
        resid = normed
        for c in range(PARTS):
            cols = slice(c * piece, (c + 1) * piece)
            act, deriv = gelu_pair(nn(second, up_ref[:, cols]))
            slope_tile[:, cols] = deriv.astype(LOW)
            act = act.astype(LOW)
            act_all[c, at, :] = act
            resid = resid + nn(act, down_ref[cols, :])
        unit, rstd = norm_parts(resid)
        result_ref[...] = (unit * gain_three + shift_ref[2:3, :]).astype(LOW)
        cot = cot_ref[...].astype(F32)
        norms_ref[2] += fold(cot * unit)
        norms_ref[3] += fold(cot)
        grad = norm_back(cot, unit, rstd, gain_three)
        low = grad.astype(LOW)
        down_all[at, :] = low
        for c in range(PARTS):
            cols = slice(c * piece, (c + 1) * piece)
            up_low = (nt(low, down_ref[cols, :]) * slope_tile[:, cols].astype(F32)).astype(LOW)
            up_all[c, at, :] = up_low
            grad = grad + nt(up_low, up_ref[:, cols])
        norms_ref[0] += fold(grad * unit_two)
        norms_ref[1] += fold(grad)
        grad = norm_back(grad, unit_two, rstd_two, gain_two)
        grad_two_ref[...] = grad
        low = grad.astype(LOW)
        attn_all[at, :] = low
        grad_att_ref[...] = nt(low, out_w_ref[...]).astype(LOW)

    @pl.when(step >= steps)
    def _():
        c = step - steps
        grad_down_ref[...] = tn(act_all[c], down_all[...]).astype(LOW)
        grad_up_ref[...] = tn(second_all[...], up_all[c]).astype(LOW)
        cols = pl.ds(pl.multiple_of(c * BLOCK, BLOCK), BLOCK)
        grad_out_ref[...] = tn(att_all[:, cols], attn_all[...]).astype(LOW)


def block_both(att, normed, cot, out_w, up, down, gains, shifts):
    tokens, width = att.shape
    wide = up.shape[1]
    steps = tokens // TILE
    piece = wide // PARTS
    tile = lambda cols: pl.BlockSpec((TILE, cols), lambda s: (jnp.minimum(s, steps - 1), 0))
    late = lambda s: jnp.maximum(s - steps, 0)
    return pl.pallas_call(
        block_kernel,
        grid=(steps + PARTS,),
        in_specs=[
            tile(width), tile(width), tile(width),
            whole((width, width)), whole(up.shape), whole(down.shape), whole(gains.shape), whole(shifts.shape),
        ],
        out_specs=[
            tile(width), tile(width), tile(width),
            pl.BlockSpec((width // PARTS, width), lambda s: (late(s), 0)),
            pl.BlockSpec((width, piece), lambda s: (0, late(s))),
            pl.BlockSpec((piece, width), lambda s: (late(s), 0)),
            pl.BlockSpec((4, 8, width), lambda s: (0, 0, 0)),
        ],
        out_shape=[
            jax.ShapeDtypeStruct((tokens, width), LOW),
            jax.ShapeDtypeStruct((tokens, width), F32),
            jax.ShapeDtypeStruct((tokens, width), LOW),
            jax.ShapeDtypeStruct((width, width), LOW),
            jax.ShapeDtypeStruct(up.shape, LOW),
            jax.ShapeDtypeStruct(down.shape, LOW),
            jax.ShapeDtypeStruct((4, 8, width), F32),
        ],
        scratch_shapes=[
            pltpu.VMEM((PARTS, tokens, piece), LOW),
            pltpu.VMEM((PARTS, tokens, piece), LOW),
            pltpu.VMEM((tokens, width), LOW),
            pltpu.VMEM((tokens, width), LOW),
            pltpu.VMEM((tokens, width), LOW),
            pltpu.VMEM((tokens, width), LOW),
            pltpu.VMEM((TILE, wide), LOW),
        ],
        compiler_params=params(1),
        name="block_both",
    )(att, normed, cot, out_w, up, down, gains, shifts)


def graph_back_kernel(
    dq_ref, dk_ref, dv_ref, low_ref, two_ref, unit_ref, rstd_ref, slope_ref, hidden_ref, agg1_ref,
    agg2_ref, x_ref, adj_ref, cols_ref, graph_ref, qkv_w_ref, gain_ref,
    input_grad_ref, grad_qkv_ref, grad_graph_ref, norms_ref, edge_ref,
    branch_all, pre_all, one_row, mean_row, back_row,
):
    step = pl.program_id(0)
    rows, tokens, width = dq_ref.shape
    blocks = tokens // BLOCK
    chunk = 2 * BLOCK
    chunks = tokens // chunk

    @pl.when(step == 0)
    def _():
        norms_ref[...] = jnp.zeros_like(norms_ref)
        edge_ref[...] = jnp.zeros_like(edge_ref)

    def spread():
        back_row[...] = jnp.zeros_like(back_row)
        for b in range(blocks):
            back_row[b * BLOCK : b * BLOCK + WIDE, :] += nn(adj_ref[0, b], mean_row[b * BLOCK : (b + 1) * BLOCK, :])

    @pl.when(step < rows)
    def _():
        base = step * tokens
        for c in range(chunks):
            part = slice(c * chunk, (c + 1) * chunk)
            grad = two_ref[0, part, :]
            for k, ref in enumerate((dq_ref, dk_ref, dv_ref)):
                grad = grad + nt(ref[step, part, :], qkv_w_ref[:, k * width : (k + 1) * width])
            unit = unit_ref[0, part, :].astype(F32)
            norms_ref[0] += fold(grad * unit)
            norms_ref[1] += fold(grad)
            grad = norm_back(grad, unit, rstd_ref[0, part, :], gain_ref[0:1, :])
            one_row[part, :] = grad
            low = grad.astype(LOW)
            branch_all[pl.ds(pl.multiple_of(base + c * chunk, chunk), chunk), :] = low
            mean_row[part, :] = (nt(low, graph_ref[:, 3 * width : 4 * width]) * cols_ref[0, part, 2:3]).astype(LOW)
        spread()
        for c in range(chunks):
            part = slice(c * chunk, (c + 1) * chunk)
            at = pl.ds(pl.multiple_of(base + c * chunk, chunk), chunk)
            grad = back_row[REACH + c * chunk : REACH + (c + 1) * chunk, :]
            grad = grad + nt(branch_all[at, :], graph_ref[:, 2 * width : 3 * width])
            grad = grad * slope_ref[0, part, :].astype(F32)
            edge_ref[0] += fold(grad * cols_ref[0, part, 0:1])
            edge_ref[1] += fold(grad * cols_ref[0, part, 1:2])
            low = grad.astype(LOW)
            pre_all[at, :] = low
            mean_row[part, :] = (nt(low, graph_ref[:, width : 2 * width]) * cols_ref[0, part, 2:3]).astype(LOW)
        spread()
        for c in range(chunks):
            part = slice(c * chunk, (c + 1) * chunk)
            at = pl.ds(pl.multiple_of(base + c * chunk, chunk), chunk)
            grad = one_row[part, :] + back_row[REACH + c * chunk : REACH + (c + 1) * chunk, :]
            input_grad_ref[0, part, :] = grad + nt(pre_all[at, :], graph_ref[:, 0:width])

    flat = lambda ref: ref[...].reshape(rows * tokens, width)
    for k, (left, right) in enumerate(
        ((low_ref, dq_ref), (low_ref, dk_ref), (low_ref, dv_ref))
    ):
        @pl.when(step == rows + k)
        def _(left=left, right=right):
            grad_qkv_ref[...] = tn(flat(left), flat(right)).astype(LOW)

    for k, (left, right) in enumerate(
        ((x_ref, pre_all), (agg1_ref, pre_all), (hidden_ref, branch_all), (agg2_ref, branch_all))
    ):
        @pl.when(step == rows + 3 + k)
        def _(left=left, right=right):
            grad_graph_ref[...] = tn(flat(left), right[...]).astype(LOW)


def graph_backward(dq, dk, dv, low, two, unit, rstd, slope, hidden, agg1, agg2, x, adj, cols, graph_w, qkv_w, gains):
    rows, tokens, width = x.shape
    blocks = tokens // BLOCK
    per_row = lambda *shape: pl.BlockSpec(
        (1,) + shape, lambda s: (jnp.minimum(s, rows - 1),) + (0,) * len(shape)
    )
    full = whole((rows, tokens, width))
    return pl.pallas_call(
        graph_back_kernel,
        grid=(rows + 7,),
        in_specs=[
            full, full, full, full,
            per_row(tokens, width), per_row(tokens, width), per_row(tokens, 1), per_row(tokens, width),
            full, full, full, full,
            per_row(blocks, WIDE, BLOCK), per_row(tokens, 8),
            whole(graph_w.shape), whole(qkv_w.shape), whole(gains.shape),
        ],
        out_specs=[
            per_row(tokens, width),
            pl.BlockSpec((width, width), lambda s: (0, jnp.clip(s - rows, 0, 2))),
            pl.BlockSpec((width, width), lambda s: (0, jnp.clip(s - rows - 3, 0, 3))),
            pl.BlockSpec((2, 8, width), lambda s: (0, 0, 0)),
            pl.BlockSpec((2, 8, width), lambda s: (0, 0, 0)),
        ],
        out_shape=[
            jax.ShapeDtypeStruct((rows, tokens, width), F32),
            jax.ShapeDtypeStruct((width, 3 * width), LOW),
            jax.ShapeDtypeStruct((width, 4 * width), LOW),
            jax.ShapeDtypeStruct((2, 8, width), F32),
            jax.ShapeDtypeStruct((2, 8, width), F32),
        ],
        scratch_shapes=[
            pltpu.VMEM((rows * tokens, width), LOW),
            pltpu.VMEM((rows * tokens, width), LOW),
            pltpu.VMEM((tokens, width), F32),
            pltpu.VMEM((tokens, width), LOW),
            pltpu.VMEM((tokens + 2 * REACH, width), F32),
        ],
        compiler_params=params(1),
        name="graph_backward",
    )(dq, dk, dv, low, two, unit, rstd, slope, hidden, agg1, agg2, x, adj, cols, graph_w, qkv_w, gains)


def device_work(inputs, coords, neighbours, counts, doc_length, graph_w, qkv_w, out_w, up, down,
                edge_proj, norm_gains, norm_shifts, distance_rate, order_rate, cotangent):
    rows, tokens, width = inputs.shape
    length = doc_length[:, 0]
    (adj, cols, agg1, slope, hidden, agg2, unit, rstd, normed, low, qkv) = graph_forward(
        length, neighbours, counts[:, None, :], coords, inputs, graph_w, edge_proj, norm_gains, norm_shifts, qkv_w
    )
    att, probs, far, order = attention_forward(length, distance_rate, order_rate, coords, qkv)
    flat = lambda v: v.reshape(rows * tokens, width)
    tall = lambda v: v.reshape(rows, tokens, width)
    result, two, grad_att, grad_out, grad_up, grad_down, norms_late = block_both(
        flat(att), flat(normed), flat(cotangent), out_w, up, down, norm_gains, norm_shifts
    )
    dq, dk, dv, rates = attention_backward(qkv, tall(grad_att), probs, far, order)
    input_grad, grad_qkv, grad_graph, norms_first, edge = graph_backward(
        dq, dk, dv, low, tall(two), unit, rstd, slope, hidden, agg1, agg2, inputs, adj, cols, graph_w, qkv_w, norm_gains
    )
    norms = jnp.concatenate([norms_first, norms_late], axis=0).sum(axis=1)
    rates = rates.sum(axis=(0, 3, 4)).reshape(-1, 2, 2)
    small = (edge.sum(axis=1), norms[0::2], norms[1::2], rates[:, :, 0].reshape(-1), rates[:, :, 1].reshape(-1))
    return tall(result), input_grad, grad_graph, grad_qkv, grad_out, grad_up, grad_down, small


def add_small(small, axes):
    edge, gains, shifts, rates, orders = small
    width = edge.shape[1]
    heads = rates.shape[0]
    line = jnp.concatenate([rates, orders, jnp.zeros((width - 2 * heads,), F32)])[None]
    total = lax.psum(jnp.concatenate([edge, gains, shifts, line], axis=0), axes)
    return total[0:2], total[2:5], total[5:8], total[8, :heads], total[8, heads : 2 * heads]


def local(
    inputs, coords, neighbours, counts, doc_length, self_one, near_one, self_two, near_two, edge_proj,
    qkv_proj, out_proj, up_proj, down_proj, norm_gains, norm_shifts, distance_rate, order_rate, cotangent,
):
    axes = ("wide", "narrow")
    width = inputs.shape[2]
    gather = lambda v: lax.all_gather(v, axes, axis=0, tiled=True)
    scatter = lambda v: lax.psum_scatter(v, axes, scatter_dimension=0, tiled=True)
    graph_w = gather(jnp.concatenate([self_one, near_one, self_two, near_two], axis=1))
    qkv_out = gather(jnp.concatenate([qkv_proj, out_proj], axis=1))
    up, down = gather(up_proj), gather(down_proj)
    result, input_grad, grad_graph, grad_qkv, grad_out, grad_up, grad_down, small = device_work(
        inputs, coords, neighbours, counts, doc_length, graph_w, qkv_out[:, : 3 * width], qkv_out[:, 3 * width :],
        up, down, edge_proj, norm_gains, norm_shifts, distance_rate, order_rate, cotangent,
    )
    down_own = scatter(grad_down).astype(F32)
    up_own = scatter(jnp.concatenate([grad_up, grad_out], axis=1)).astype(F32)
    rest = scatter(jnp.concatenate([grad_graph, grad_qkv], axis=1)).astype(F32)
    edge, gains, shifts, rates, orders = add_small(small, axes)
    wide = up_proj.shape[1]
    return (
        result, input_grad,
        rest[:, :width], rest[:, width : 2 * width], rest[:, 2 * width : 3 * width], rest[:, 3 * width : 4 * width],
        edge,
        rest[:, 4 * width :], up_own[:, wide:], up_own[:, :wide], down_own,
        gains, shifts, rates, orders,
    )


def solution(mesh):
    axes = ("wide", "narrow")
    middle, last = P(None, axes, None), P(None, None, axes)
    count, weight, same = P(None, axes), P(axes, None), P()
    return jax.shard_map(
        local,
        mesh=mesh,
        in_specs=(middle, last, last, count, count)
        + (weight,) * 4
        + (same,)
        + (weight,) * 4
        + (same,) * 4
        + (middle,),
        out_specs=(middle, middle) + (weight,) * 4 + (same,) + (weight,) * 4 + (same,) * 4,
        check_vma=False,
    )
```

```python
import functools
import jax
import jax.numpy as jnp
from jax import lax
from jax.experimental import pallas as pl
from jax.experimental.pallas import tpu as pltpu
from jax.sharding import PartitionSpec as P

RADIUS = 128
REACH = 64
BLOCK = 128
WIDE = BLOCK + 2 * REACH
SPAN = BLOCK + 2 * RADIUS
FAR = 1e10
F32 = jnp.float32
LOW = jnp.bfloat16
VMEM = 60 * 2**20


def dot(left, right, dims):
    return lax.dot_general(left, right, ((dims[:1], dims[1:]), ((), ())), preferred_element_type=F32)


def nn(left, right):
    return dot(left, right, (1, 0))


def nt(left, right):
    return dot(left, right, (1, 1))


def tn(left, right):
    return dot(left, right, (0, 0))


def gelu_pair(pre):
    slope = 0.7978845608028654
    square = pre * pre
    half = 0.5 + 0.5 * jnp.tanh(pre * (slope + (slope * 0.044715) * square))
    act = pre * half
    deriv = half + act * (1.0 - half) * (2.0 * slope + (6.0 * slope * 0.044715) * square)
    return act, deriv


def norm_parts(values):
    centre = values - jnp.mean(values, axis=-1, keepdims=True)
    rstd = lax.rsqrt(jnp.mean(centre * centre, axis=-1, keepdims=True) + 1e-05)
    return centre * rstd, rstd


def norm_back(grad, unit, rstd, gain):
    scaled = grad * gain
    mean = jnp.mean(scaled, axis=-1, keepdims=True)
    along = jnp.mean(scaled * unit, axis=-1, keepdims=True)
    return rstd * (scaled - mean - unit * along)


def fold(values):
    rows, cols = values.shape
    return jnp.sum(values.reshape(rows // 8, 8, cols), axis=0)


def whole(shape, space=None):
    return pl.BlockSpec(shape, lambda *_: (0,) * len(shape), pipeline_mode=pl.Buffered(1))


def params(grid_rank, **more):
    return pltpu.CompilerParams(
        vmem_limit_bytes=VMEM, dimension_semantics=("arbitrary",) * grid_rank, **more
    )


def fill_bias(length, point_ref, far_ref, order_ref, row):
    tokens = point_ref.shape[2]
    side = jnp.zeros((2, RADIUS), F32)
    padded = jnp.concatenate([side, point_ref[row], side], axis=1)
    tall = jnp.concatenate([padded, jnp.zeros((6, tokens + 2 * RADIUS), F32)], axis=0)
    for b in range(tokens // BLOCK):
        window = tall[:, b * BLOCK : b * BLOCK + SPAN].T
        key_x, key_y = window[:, 0:1], window[:, 1:2]
        lanes = slice(b * BLOCK, (b + 1) * BLOCK)
        delta_x = key_x - point_ref[row, 0:1, lanes]
        delta_y = key_y - point_ref[row, 1:2, lanes]
        dist = jnp.log(1.0 + 16.0 * (delta_x * delta_x + delta_y * delta_y))
        query = lax.broadcasted_iota(jnp.int32, (SPAN, BLOCK), 1) + b * BLOCK
        key = lax.broadcasted_iota(jnp.int32, (SPAN, BLOCK), 0) + (b * BLOCK - RADIUS)
        allowed = (jnp.abs(query - key) <= RADIUS) & ((query >= length) == (key >= length))
        allowed = allowed & (key >= 0) & (key < tokens)
        far_ref[row, b] = jnp.where(allowed, dist, FAR)
        order_ref[row, b] = jnp.tanh(4.0 * delta_x)


def pair_rows(values):
    lane = lax.broadcasted_iota(jnp.int32, values.shape, 1)
    zero = jnp.zeros_like(values)
    first = jnp.where(lane < BLOCK // 2, values, zero)
    second = jnp.where(lane < BLOCK // 2, zero, values)
    return jnp.concatenate([first, second], axis=0)


def pair_pick(values):
    lane = lax.broadcasted_iota(jnp.int32, (BLOCK, BLOCK), 1)
    return jnp.where(lane < BLOCK // 2, values[:BLOCK], values[BLOCK:])


def pad_rows(pad_ref, values):
    tokens = values.shape[0]
    zeros = jnp.zeros((RADIUS, values.shape[1]), pad_ref.dtype)
    pad_ref[pl.ds(0, RADIUS), :] = zeros
    pad_ref[pl.ds(RADIUS + tokens, RADIUS), :] = zeros
    pad_ref[pl.ds(RADIUS, tokens), :] = values


FIRST, OWN, PASSED, SIBLING = 0, 1, 2, 3


class Place:
    def __init__(self, depth):
        self.depth = depth
        wide, self.x = lax.axis_index("wide"), lax.axis_index("narrow")
        self.core = lax.rem(wide, 2)
        self.y = lax.rem(lax.div(wide, 2), 2)
        self.z = lax.div(wide, 4)
        core, y, x = self.core, self.y, self.x
        self.first_y = (1 - core) * (1 - y) + core * y
        self.first_x = core * (1 - x) + (1 - core) * x
        self.second_y = core * (1 - y) + (1 - core) * y
        self.second_x = (1 - core) * (1 - x) + core * x

    def at(self, z, y, core, x):
        return ((z * 2 + y) * 2 + core, x)

    def along(self, k):
        return lax.rem(self.z + k, self.depth)

    def partners(self):
        along = [self.at(self.along(k), self.y, self.core, self.x) for k in range(1, self.depth)]
        return along + [
            self.at(self.z, self.first_y, self.core, self.first_x),
            self.at(self.z, self.second_y, self.core, self.second_x),
            self.at(self.z, self.y, 1 - self.core, self.x),
        ]


def meet(place):
    barrier = pltpu.get_barrier_semaphore()
    partners = place.partners()
    for partner in partners:
        pl.semaphore_signal(barrier, inc=1, device_id=partner, device_id_type=pl.DeviceIdType.MESH)
    pl.semaphore_wait(barrier, len(partners))


class Gather:
    def __init__(self, place, land, send, recv, group):
        self.place, self.land, self.send, self.recv, self.group = place, land, send, recv, group

    def copy(self, view, slot, device):
        return pltpu.make_async_remote_copy(
            src_ref=view, dst_ref=view, send_sem=self.send.at[self.group, slot], recv_sem=self.recv.at[self.group, slot],
            device_id=device, device_id_type=pl.DeviceIdType.MESH,
        )

    def pieces(self, stage):
        p, land = self.place, self.land
        base = p.depth - 1
        mine = land.at[:, p.y, p.core, p.x]
        if stage == "along":
            here = land.at[p.z, p.y, p.core, p.x]
            found = []
            for k in range(1, p.depth):
                there = land.at[p.along(p.depth - k), p.y, p.core, p.x]
                found.append((here, there, k - 1, p.at(p.along(k), p.y, p.core, p.x)))
            return found
        first = p.at(p.z, p.first_y, p.core, p.first_x)
        second = p.at(p.z, p.second_y, p.core, p.second_x)
        if stage == FIRST:
            return [(mine, land.at[:, p.first_y, p.core, p.first_x], base, first)]
        if stage == OWN:
            return [(mine, land.at[:, p.second_y, p.core, p.second_x], base + 1, second)]
        if stage == PASSED:
            return [(land.at[:, p.first_y, p.core, p.first_x], land.at[:, 1 - p.y, p.core, 1 - p.x], base + 2, second)]
        return [(land.at[:, :, p.core], land.at[:, :, 1 - p.core], base + 3, p.at(p.z, p.y, 1 - p.core, p.x))]

    def start(self, *stages):
        for stage in stages:
            for leaves, _, slot, device in self.pieces(stage):
                self.copy(leaves, slot, device).start()

    def arrive(self, *stages):
        for stage in stages:
            for _, arrives, slot, device in self.pieces(stage):
                self.copy(arrives, slot, device).wait_recv()

    def sent(self):
        for stage in ("along", FIRST, OWN, PASSED, SIBLING):
            for leaves, _, slot, device in self.pieces(stage):
                self.copy(leaves, slot, device).wait_send()


def merge_rows(full, land):
    depth, rows = land.shape[0], land.shape[4]

    @pl.loop(0, depth * 4)
    def _(k):
        z, y, core = lax.div(k, 4), lax.rem(lax.div(k, 2), 2), lax.rem(k, 2)
        pair = jnp.concatenate([land[z, y, core, 0].astype(F32), land[z, y, core, 1].astype(F32)], axis=0)
        full[pl.ds(pl.multiple_of(k * 2 * rows, 16), 2 * rows), :] = pair.astype(LOW)


def front_kernel(remote, *refs):
    (length_ref, dist_rate_ref, order_rate_ref, near_ref, count_ref, point_ref, x_ref, edge_w_ref, gain_ref, shift_ref,
     self1_ref, near1_ref, self2_ref, near2_ref, qkv_w_ref) = refs[:15]
    refs = refs[15:]
    shards, refs = (refs[:3], refs[3:]) if remote else ((), refs)
    outs, refs = refs[:18], refs[18:]
    fulls, refs = (refs[:3], refs[3:]) if remote else ((), refs)
    (adj, cols, agg1, slope, hidden, agg2, unit, rstd, normed, low, qkv, att, probs, far, order,
     first_w, second_w, third_w, pad, point_pad, rel, keys, values, out_sem, probs_sem, in_sem) = refs[:26]
    rows, slots, tokens = near_ref.shape
    width = x_ref.shape[2]
    pairs = width // BLOCK
    blocks = tokens // BLOCK
    chunk = 2 * BLOCK

    writes = {}

    def write(k, source, dest=None):
        writes[k] = pltpu.make_async_copy(source, outs[k] if dest is None else dest, out_sem.at[k])
        writes[k].start()

    if remote:
        land_a, land_b, land_q, send, recv = refs[26:]
        place = Place(land_a.shape[0])
        lands = (land_a, land_b, land_q) + tuple(fulls)
        groups = [Gather(place, land, send, recv, g) for g, land in enumerate(lands)]
        ga, gb, gq, go, gu, gd = groups
        column = lambda land, k: land.at[place.z, place.y, place.core, place.x, :, pl.ds(k * width, width)]
        own = lambda land: land.at[place.z, place.y, place.core, place.x]
        loads = [
            [pltpu.make_async_copy(ref, column(land_a, k), in_sem.at[k]) for k, ref in enumerate((self1_ref, near1_ref))],
            [pltpu.make_async_copy(ref, column(land_b, k), in_sem.at[2 + k]) for k, ref in enumerate((self2_ref, near2_ref))],
            [pltpu.make_async_copy(qkv_w_ref, own(land_q), in_sem.at[4])],
        ] + [[pltpu.make_async_copy(ref, own(full), in_sem.at[5 + k])] for k, (ref, full) in enumerate(zip(shards, fulls))]
        for load in loads:
            for copy in load:
                copy.start()
        meet(place)

        def begin(g):
            for copy in loads[g]:
                copy.wait()
            groups[g].start("along")

        begin(0)
        begin(1)
    else:
        loads = [
            pltpu.make_async_copy(ref, dest, in_sem.at[k])
            for k, (ref, dest) in enumerate((
                (self1_ref, first_w.at[:, pl.ds(0, width)]), (near1_ref, first_w.at[:, pl.ds(width, width)]),
                (self2_ref, second_w.at[:, pl.ds(0, width)]), (near2_ref, second_w.at[:, pl.ds(width, width)]),
                (qkv_w_ref, third_w),
            ))
        ]
        for copy in loads:
            copy.start()

    side = jnp.zeros((REACH, width), LOW)
    pad[pl.ds(0, REACH), :] = side
    pad[pl.ds(tokens + REACH, REACH), :] = side

    @pl.loop(0, rows)
    def _(row):
        length = length_ref[row]
        pad[pl.ds(REACH, tokens), :] = x_ref[row]
        points = point_ref[row]
        high = points.astype(LOW).astype(F32)
        mid = (points - high).astype(LOW).astype(F32)
        tail = points - high - mid
        split = jnp.concatenate([high, mid, tail, jnp.ones((1, tokens), F32), jnp.zeros((9, tokens), F32)], axis=0)
        edge_side = jnp.zeros((16, REACH), F32)
        point_pad[...] = jnp.concatenate([edge_side, split, edge_side], axis=1).astype(LOW)

        @pl.loop(0, blocks)
        def _(b):
            start = pl.multiple_of(b * BLOCK, BLOCK)
            lanes = pl.ds(start, BLOCK)
            near = near_ref[row, :, lanes]
            count = count_ref[row, :, lanes]
            spot = lax.broadcasted_iota(jnp.int32, (1, BLOCK), 1) + start
            slot = lax.broadcasted_iota(jnp.int32, (slots, BLOCK), 0)
            same = (near >= length) == (spot >= length)
            rel[...] = jnp.where((slot < count) & same, near - (start - REACH), -1)
            target = lax.broadcasted_iota(jnp.int32, (WIDE, BLOCK), 0)
            total = jnp.zeros((WIDE, BLOCK), F32)
            for s in range(slots):
                total = total + jnp.where(rel[s : s + 1, :] == target, 1.0, 0.0)
            band = total.astype(LOW)
            adj[row, b] = band
            sums = nn(point_pad[:, pl.ds(start, WIDE)], band)
            inverse = 1.0 / count.astype(F32)
            here = point_ref[row, :, lanes]
            edge = (sums[0:2] + sums[2:4] + sums[4:6] - sums[6:7] * here) * inverse
            lines = jnp.concatenate([edge, inverse, jnp.zeros((5, BLOCK), F32)], axis=0).T
            cols[row, lanes, :] = lines
            agg = tn(band, pad[pl.ds(start, WIDE), :])
            agg1[row, lanes, :] = (agg * lines[:, 2:3]).astype(LOW)

        if remote:
            @pl.when(row == 0)
            def _():
                ga.arrive("along")
                ga.start(FIRST, OWN)
                begin(2)

    write(0, adj)
    write(1, cols)
    write(2, agg1)
    if remote:
        ga.arrive(FIRST)
        ga.start(PASSED)
        gb.arrive("along")
        gb.start(FIRST, OWN)

    @pl.loop(0, rows)
    def _(row):
        fill_bias(length_ref[row], point_ref, far, order, row)

    write(13, far)
    write(14, order)
    if remote:
        ga.arrive(OWN, PASSED)
        ga.start(SIBLING)
        gb.arrive(FIRST)
        gb.start(PASSED)
        gq.arrive("along")
        gq.start(FIRST, OWN)
        begin(3)
        begin(4)
        ga.arrive(SIBLING)
        merge_rows(first_w, land_a)
    else:
        for copy in loads:
            copy.wait()
        write(16, second_w)
        write(17, third_w)
    write(15, first_w)

    @pl.loop(0, rows)
    def _(row):
        for c in range(tokens // chunk):
            part = slice(c * chunk, (c + 1) * chunk)
            pre = nn(x_ref[row, part, :], first_w[:, 0:width])
            pre = pre + nn(agg1[row, part, :], first_w[:, width : 2 * width])
            pre = pre + cols[row, part, 0:1] * edge_w_ref[0:1, :] + cols[row, part, 1:2] * edge_w_ref[1:2, :]
            act, deriv = gelu_pair(pre)
            slope[row, part, :] = deriv.astype(LOW)
            hidden[row, part, :] = act.astype(LOW)
            pad[REACH + c * chunk : REACH + (c + 1) * chunk, :] = act.astype(LOW)
        for b in range(blocks):
            lanes = slice(b * BLOCK, (b + 1) * BLOCK)
            agg = tn(adj[row, b], pad[b * BLOCK : b * BLOCK + WIDE, :])
            agg2[row, lanes, :] = (agg * cols[row, lanes, 2:3]).astype(LOW)
        if remote:
            @pl.when(row == 0)
            def _():
                gb.arrive(OWN, PASSED)
                gb.start(SIBLING)

    write(3, slope)
    write(4, hidden)
    write(5, agg2)
    if remote:
        gq.arrive(FIRST)
        gq.start(PASSED)
        gb.arrive(SIBLING)
        merge_rows(second_w, land_b)
        write(16, second_w)

    @pl.loop(0, rows)
    def _(row):
        for c in range(tokens // chunk):
            part = slice(c * chunk, (c + 1) * chunk)
            resid = x_ref[row, part, :].astype(F32) + nn(hidden[row, part, :], second_w[:, 0:width])
            resid = resid + nn(agg2[row, part, :], second_w[:, width : 2 * width])
            plain, scale = norm_parts(resid)
            unit[row, part, :] = plain.astype(LOW)
            rstd[row, part, :] = scale
            out = plain * gain_ref[0:1, :] + shift_ref[0:1, :]
            normed[row, part, :] = out
            low[row, part, :] = out.astype(LOW)
        if remote:
            @pl.when(row == 0)
            def _():
                for g in (go, gu):
                    g.arrive("along")
                    g.start(FIRST, OWN)
                begin(5)

    write(6, unit)
    write(7, rstd)
    write(8, normed)
    write(9, low)
    if remote:
        gq.arrive(OWN, PASSED)
        gq.start(SIBLING)
        for g in (go, gu):
            g.arrive(FIRST)
            g.start(PASSED)
        gq.arrive(SIBLING)
        merge_rows(third_w, land_q)
        write(17, third_w)

    @pl.loop(0, rows)
    def _(row):
        for c in range(tokens // chunk):
            part = slice(c * chunk, (c + 1) * chunk)
            out = nn(low[row, part, :], third_w[...]).astype(LOW)
            for k in range(3 * pairs):
                qkv[k, row, part, :] = out[:, k * BLOCK : (k + 1) * BLOCK]

    write(10, qkv)
    zeros = jnp.zeros((RADIUS, BLOCK), LOW)
    for ref in (keys, values):
        ref[pl.ds(0, RADIUS), :] = zeros
        ref[pl.ds(RADIUS + tokens, RADIUS), :] = zeros

    @pl.loop(0, rows * pairs)
    def _(turn):
        row, pair, slot = lax.div(turn, pairs), lax.rem(turn, pairs), lax.rem(turn, 2)
        if remote:
            @pl.when(turn == 1)
            def _():
                gd.arrive("along")
                gd.start(FIRST, OWN)

            @pl.when(turn == 4)
            def _():
                for g in (go, gu):
                    g.arrive(OWN, PASSED)
                    g.start(SIBLING)
                gd.arrive(FIRST)
                gd.start(PASSED)

            @pl.when(turn == 9)
            def _():
                gd.arrive(OWN, PASSED)
                gd.start(SIBLING)

        def probs_copy(t, s):
            return pltpu.make_async_copy(
                probs.at[s], outs[12].at[lax.div(t, pairs), lax.rem(t, pairs)], probs_sem.at[s]
            )

        @pl.when(turn >= 2)
        def _():
            probs_copy(turn - 2, slot).wait()

        keys[pl.ds(RADIUS, tokens), :] = qkv[pairs + pair, row]
        values[pl.ds(RADIUS, tokens), :] = qkv[2 * pairs + pair, row]
        for b in range(blocks):
            lanes = slice(b * BLOCK, (b + 1) * BLOCK)
            window = slice(b * BLOCK, b * BLOCK + SPAN)
            queries = pair_rows(qkv[pair, row, lanes, :] * 0.125)
            raw = nt(keys[window, :], queries)
            sides = []
            for h in range(2):
                bias = order_rate_ref[2 * pair + h] * order[row, b] - dist_rate_ref[2 * pair + h] * far[row, b]
                scores = raw[:, h * BLOCK : (h + 1) * BLOCK] + bias
                grown = jnp.exp(scores - jnp.max(scores, axis=0, keepdims=True))
                scale = 1.0 / jnp.sum(grown, axis=0, keepdims=True)
                sides.append((grown * scale).astype(LOW))
            both = jnp.concatenate(sides, axis=1)
            probs[slot, b] = both
            att[pair, row, lanes, :] = pair_pick(tn(both, values[window, :])).astype(LOW)
        probs_copy(turn, slot).start()

    last = rows * pairs
    for turn in (last - 2, last - 1):
        pltpu.make_async_copy(probs.at[turn % 2], outs[12].at[turn // pairs, turn % pairs], probs_sem.at[turn % 2]).wait()
    write(11, att)
    if remote:
        for g in (go, gu, gd):
            g.arrive(SIBLING)
        for g in groups:
            g.sent()
    for copy in writes.values():
        copy.wait()


def front(remote, depth, length, dist_rate, order_rate, near, count, point, x, edge_w, gains, shifts, weights, shards):
    rows, tokens, width = x.shape
    slots = near.shape[1]
    blocks, pairs = tokens // BLOCK, width // BLOCK
    smem, vmem, hbm = (pl.BlockSpec(memory_space=s) for s in (pltpu.SMEM, pltpu.VMEM, pl.ANY))
    each = lambda dtype, *shape: ((rows,) + shape, dtype)
    kept = [
        each(LOW, blocks, WIDE, BLOCK),
        each(F32, tokens, 8),
        each(LOW, tokens, width),
        each(LOW, tokens, width),
        each(LOW, tokens, width),
        each(LOW, tokens, width),
        each(LOW, tokens, width),
        each(F32, tokens, 1),
        each(F32, tokens, width),
        each(LOW, tokens, width),
        ((3 * pairs, rows, tokens, BLOCK), LOW),
        ((pairs, rows, tokens, BLOCK), LOW),
        each(LOW, pairs, blocks, SPAN, 2 * BLOCK),
        each(F32, blocks, SPAN, BLOCK),
        each(F32, blocks, SPAN, BLOCK),
        ((width, 2 * width), LOW),
        ((width, 2 * width), LOW),
        ((width, 3 * width), LOW),
    ]
    out_shape = [jax.ShapeDtypeStruct(*k) for k in kept]
    kept[12] = ((2, blocks, SPAN, 2 * BLOCK), LOW)
    scratch = [pltpu.VMEM(*k) for k in kept]
    scratch += [
        pltpu.VMEM((tokens + 2 * REACH, width), LOW),
        pltpu.VMEM((16, tokens + 2 * REACH), LOW),
        pltpu.VMEM((slots, BLOCK), jnp.int32),
        pltpu.VMEM((tokens + 2 * RADIUS, BLOCK), LOW),
        pltpu.VMEM((tokens + 2 * RADIUS, BLOCK), LOW),
        pltpu.SemaphoreType.DMA((18,)),
        pltpu.SemaphoreType.DMA((2,)),
        pltpu.SemaphoreType.DMA((8,)),
    ]
    more = {}
    if remote:
        blocked = lambda shape: (depth, 2, 2, 2) + shape
        out_shape += [jax.ShapeDtypeStruct(blocked(s.shape), LOW) for s in shards]
        share = weights[0].shape[0]
        scratch += [pltpu.VMEM(blocked((share, k * width)), LOW) for k in (2, 2, 3)]
        scratch += [pltpu.SemaphoreType.DMA((6, depth + 3))] * 2
        more = {"collective_id": 0, "has_side_effects": True}
    return pl.pallas_call(
        functools.partial(front_kernel, remote),
        in_specs=[smem] * 3 + [vmem] * 7 + [hbm] * (len(weights) + len(shards)),
        out_specs=[hbm] * len(out_shape),
        out_shape=out_shape,
        scratch_shapes=scratch,
        compiler_params=pltpu.CompilerParams(vmem_limit_bytes=VMEM, **more),
        name="front",
    )(length, dist_rate, order_rate, near, count, point, x, edge_w, gains, shifts, *weights, *shards)


def attention_back_kernel(
    q_ref, k_ref, v_ref, grad_ref, probs_ref, far_ref, order_ref,
    dq_ref, dk_ref, dv_ref, rate_ref,
    keys, values, grad_keys, grad_values,
):
    pad_rows(keys, k_ref[0, 0])
    pad_rows(values, v_ref[0, 0])
    grad_keys[...] = jnp.zeros_like(grad_keys)
    grad_values[...] = jnp.zeros_like(grad_values)
    tokens = q_ref.shape[2]
    sums = [jnp.zeros((8, BLOCK), F32)] * 4
    for b in range(tokens // BLOCK):
        lanes = slice(b * BLOCK, (b + 1) * BLOCK)
        window = slice(b * BLOCK, b * BLOCK + SPAN)
        queries = pair_rows(q_ref[0, 0, lanes, :] * 0.125)
        grads = pair_rows(grad_ref[0, lanes, :])
        probs_low = probs_ref[0, 0, b]
        back = nt(values[window, :], grads)
        dist = jnp.where(far_ref[0, b] < FAR, far_ref[0, b], 0.0)
        order = order_ref[0, b]
        sides = []
        for h in range(2):
            probs = probs_low[:, h * BLOCK : (h + 1) * BLOCK].astype(F32)
            part = back[:, h * BLOCK : (h + 1) * BLOCK]
            delta = jnp.sum(probs * part, axis=0, keepdims=True)
            scores = probs * (part - delta)
            sums[2 * h] = sums[2 * h] - fold(scores * dist)
            sums[2 * h + 1] = sums[2 * h + 1] + fold(scores * order)
            sides.append(scores.astype(LOW))
        scores_low = jnp.concatenate(sides, axis=1)
        grad_values[window, :] += nn(probs_low, grads)
        grad_keys[window, :] += nn(scores_low, queries)
        dq_ref[0, lanes, :] = (pair_pick(tn(scores_low, keys[window, :])) * 0.125).astype(LOW)
    dk_ref[0] = grad_keys[pl.ds(RADIUS, tokens), :].astype(LOW)
    dv_ref[0] = grad_values[pl.ds(RADIUS, tokens), :].astype(LOW)
    for k in range(4):
        rate_ref[0, 0, k] = sums[k]


def attention_backward(qkv, grad, probs, far, order):
    pairs, rows, tokens = qkv.shape[0] // 3, qkv.shape[1], qkv.shape[2]
    width = pairs * BLOCK
    blocks = tokens // BLOCK
    part = lambda k: pl.BlockSpec((1, 1, tokens, BLOCK), lambda r, p: (k * pairs + p, r, 0, 0))
    flat = pl.BlockSpec((1, tokens, BLOCK), lambda r, p: (r, 0, p))
    bias = pl.BlockSpec((1, blocks, SPAN, BLOCK), lambda r, p: (r, 0, 0, 0))
    grads = jax.ShapeDtypeStruct((rows, tokens, width), LOW)
    return pl.pallas_call(
        attention_back_kernel,
        grid=(rows, pairs),
        in_specs=[
            part(0),
            part(1),
            part(2),
            flat,
            pl.BlockSpec((1, 1, blocks, SPAN, 2 * BLOCK), lambda r, p: (r, p, 0, 0, 0)),
            bias,
            bias,
        ],
        out_specs=[flat] * 3 + [pl.BlockSpec((1, 1, 4, 8, BLOCK), lambda r, p: (r, p, 0, 0, 0))],
        out_shape=[grads] * 3 + [jax.ShapeDtypeStruct((rows, pairs, 4, 8, BLOCK), F32)],
        scratch_shapes=[pltpu.VMEM((tokens + 2 * RADIUS, BLOCK), LOW)] * 2
        + [pltpu.VMEM((tokens + 2 * RADIUS, BLOCK), F32)] * 2,
        compiler_params=params(2),
        name="attention_backward",
    )(qkv, qkv, qkv, grad, probs, far, order)


TILE = 256
PARTS = 6


def block_kernel(
    att_ref, normed_ref, cot_ref, out_w_ref, up_ref, down_ref, gain_ref, shift_ref,
    result_ref, grad_two_ref, grad_att_ref, grad_out_ref, grad_up_ref, grad_down_ref, norms_ref,
    act_all, up_all, second_all, down_all, attn_all, att_all, slope_tile,
):
    step = pl.program_id(0)
    width = normed_ref.shape[1]
    steps = act_all.shape[1] // TILE
    piece = act_all.shape[2]

    @pl.when(step == 0)
    def _():
        norms_ref[...] = jnp.zeros_like(norms_ref)

    @pl.when(step < steps)
    def _():
        at = pl.ds(pl.multiple_of(step * TILE, TILE), TILE)
        att = jnp.concatenate([att_ref[k] for k in range(att_ref.shape[0])], axis=1)
        att_all[at, :] = att
        resid = normed_ref[...] + nn(att, out_w_ref[...])
        unit_two, rstd_two = norm_parts(resid)
        gain_two, gain_three = gain_ref[1:2, :], gain_ref[2:3, :]
        normed = unit_two * gain_two + shift_ref[1:2, :]
        second = normed.astype(LOW)
        second_all[at, :] = second
        resid = normed
        for c in range(PARTS):
            cols = slice(c * piece, (c + 1) * piece)
            act, deriv = gelu_pair(nn(second, up_ref[:, cols]))
            slope_tile[:, cols] = deriv.astype(LOW)
            act = act.astype(LOW)
            act_all[c, at, :] = act
            resid = resid + nn(act, down_ref[cols, :])
        unit, rstd = norm_parts(resid)
        result_ref[...] = (unit * gain_three + shift_ref[2:3, :]).astype(LOW)
        cot = cot_ref[...].astype(F32)
        norms_ref[2] += fold(cot * unit)
        norms_ref[3] += fold(cot)
        grad = norm_back(cot, unit, rstd, gain_three)
        low = grad.astype(LOW)
        down_all[at, :] = low
        for c in range(PARTS):
            cols = slice(c * piece, (c + 1) * piece)
            up_low = (nt(low, down_ref[cols, :]) * slope_tile[:, cols].astype(F32)).astype(LOW)
            up_all[c, at, :] = up_low
            grad = grad + nt(up_low, up_ref[:, cols])
        norms_ref[0] += fold(grad * unit_two)
        norms_ref[1] += fold(grad)
        grad = norm_back(grad, unit_two, rstd_two, gain_two)
        grad_two_ref[...] = grad
        low = grad.astype(LOW)
        attn_all[at, :] = low
        grad_att_ref[...] = nt(low, out_w_ref[...]).astype(LOW)

    @pl.when(step >= steps)
    def _():
        c = step - steps
        grad_down_ref[...] = tn(act_all[c], down_all[...]).astype(LOW)
        grad_up_ref[...] = tn(second_all[...], up_all[c]).astype(LOW)
        cols = pl.ds(pl.multiple_of(c * BLOCK, BLOCK), BLOCK)
        grad_out_ref[...] = tn(att_all[:, cols], attn_all[...]).astype(LOW)


def block_both(att, normed, cot, out_w, up, down, gains, shifts):
    tokens, width = normed.shape
    wide = up.shape[1]
    steps = tokens // TILE
    piece = wide // PARTS
    tile = lambda cols: pl.BlockSpec((TILE, cols), lambda s: (jnp.minimum(s, steps - 1), 0))
    late = lambda s: jnp.maximum(s - steps, 0)
    return pl.pallas_call(
        block_kernel,
        grid=(steps + PARTS,),
        in_specs=[
            pl.BlockSpec((width // BLOCK, TILE, BLOCK), lambda s: (0, jnp.minimum(s, steps - 1), 0)), tile(width), tile(width),
            whole((width, width)), whole(up.shape), whole(down.shape), whole(gains.shape), whole(shifts.shape),
        ],
        out_specs=[
            tile(width), tile(width), tile(width),
            pl.BlockSpec((width // PARTS, width), lambda s: (late(s), 0)),
            pl.BlockSpec((width, piece), lambda s: (0, late(s))),
            pl.BlockSpec((piece, width), lambda s: (late(s), 0)),
            pl.BlockSpec((4, 8, width), lambda s: (0, 0, 0)),
        ],
        out_shape=[
            jax.ShapeDtypeStruct((tokens, width), LOW),
            jax.ShapeDtypeStruct((tokens, width), F32),
            jax.ShapeDtypeStruct((tokens, width), LOW),
            jax.ShapeDtypeStruct((width, width), LOW),
            jax.ShapeDtypeStruct(up.shape, LOW),
            jax.ShapeDtypeStruct(down.shape, LOW),
            jax.ShapeDtypeStruct((4, 8, width), F32),
        ],
        scratch_shapes=[
            pltpu.VMEM((PARTS, tokens, piece), LOW),
            pltpu.VMEM((PARTS, tokens, piece), LOW),
            pltpu.VMEM((tokens, width), LOW),
            pltpu.VMEM((tokens, width), LOW),
            pltpu.VMEM((tokens, width), LOW),
            pltpu.VMEM((tokens, width), LOW),
            pltpu.VMEM((TILE, wide), LOW),
        ],
        compiler_params=params(1),
        name="block_both",
    )(att, normed, cot, out_w, up, down, gains, shifts)


def graph_back_kernel(
    dq_ref, dk_ref, dv_ref, low_ref, two_ref, unit_ref, rstd_ref, slope_ref, hidden_ref, agg1_ref,
    agg2_ref, x_ref, adj_ref, cols_ref, first_ref, second_ref, qkv_w_ref, gain_ref,
    input_grad_ref, grad_qkv_ref, grad_graph_ref, norms_ref, edge_ref,
    branch_all, pre_all, one_row, mean_row, back_row,
):
    step = pl.program_id(0)
    rows, tokens, width = dq_ref.shape
    blocks = tokens // BLOCK
    chunk = 2 * BLOCK
    chunks = tokens // chunk

    @pl.when(step == 0)
    def _():
        norms_ref[...] = jnp.zeros_like(norms_ref)
        edge_ref[...] = jnp.zeros_like(edge_ref)

    def spread():
        back_row[...] = jnp.zeros_like(back_row)
        for b in range(blocks):
            back_row[b * BLOCK : b * BLOCK + WIDE, :] += nn(adj_ref[0, b], mean_row[b * BLOCK : (b + 1) * BLOCK, :])

    @pl.when(step < rows)
    def _():
        base = step * tokens
        for c in range(chunks):
            part = slice(c * chunk, (c + 1) * chunk)
            grad = two_ref[0, part, :]
            for k, ref in enumerate((dq_ref, dk_ref, dv_ref)):
                grad = grad + nt(ref[step, part, :], qkv_w_ref[:, k * width : (k + 1) * width])
            unit = unit_ref[0, part, :].astype(F32)
            norms_ref[0] += fold(grad * unit)
            norms_ref[1] += fold(grad)
            grad = norm_back(grad, unit, rstd_ref[0, part, :], gain_ref[0:1, :])
            one_row[part, :] = grad
            low = grad.astype(LOW)
            branch_all[pl.ds(pl.multiple_of(base + c * chunk, chunk), chunk), :] = low
            mean_row[part, :] = (nt(low, second_ref[:, width : 2 * width]) * cols_ref[0, part, 2:3]).astype(LOW)
        spread()
        for c in range(chunks):
            part = slice(c * chunk, (c + 1) * chunk)
            at = pl.ds(pl.multiple_of(base + c * chunk, chunk), chunk)
            grad = back_row[REACH + c * chunk : REACH + (c + 1) * chunk, :]
            grad = grad + nt(branch_all[at, :], second_ref[:, 0:width])
            grad = grad * slope_ref[0, part, :].astype(F32)
            edge_ref[0] += fold(grad * cols_ref[0, part, 0:1])
            edge_ref[1] += fold(grad * cols_ref[0, part, 1:2])
            low = grad.astype(LOW)
            pre_all[at, :] = low
            mean_row[part, :] = (nt(low, first_ref[:, width : 2 * width]) * cols_ref[0, part, 2:3]).astype(LOW)
        spread()
        for c in range(chunks):
            part = slice(c * chunk, (c + 1) * chunk)
            at = pl.ds(pl.multiple_of(base + c * chunk, chunk), chunk)
            grad = one_row[part, :] + back_row[REACH + c * chunk : REACH + (c + 1) * chunk, :]
            input_grad_ref[0, part, :] = grad + nt(pre_all[at, :], first_ref[:, 0:width])

    flat = lambda ref: ref[...].reshape(rows * tokens, width)
    for k, (left, right) in enumerate(
        ((low_ref, dq_ref), (low_ref, dk_ref), (low_ref, dv_ref))
    ):
        @pl.when(step == rows + k)
        def _(left=left, right=right):
            grad_qkv_ref[...] = tn(flat(left), flat(right)).astype(LOW)

    for k, (left, right) in enumerate(
        ((x_ref, pre_all), (agg1_ref, pre_all), (hidden_ref, branch_all), (agg2_ref, branch_all))
    ):
        @pl.when(step == rows + 3 + k)
        def _(left=left, right=right):
            grad_graph_ref[...] = tn(flat(left), right[...]).astype(LOW)


def graph_backward(dq, dk, dv, low, two, unit, rstd, slope, hidden, agg1, agg2, x, adj, cols, first_w, second_w, qkv_w, gains):
    rows, tokens, width = x.shape
    blocks = tokens // BLOCK
    per_row = lambda *shape: pl.BlockSpec(
        (1,) + shape, lambda s: (jnp.minimum(s, rows - 1),) + (0,) * len(shape)
    )
    full = whole((rows, tokens, width))
    return pl.pallas_call(
        graph_back_kernel,
        grid=(rows + 7,),
        in_specs=[
            full, full, full, full,
            per_row(tokens, width), per_row(tokens, width), per_row(tokens, 1), per_row(tokens, width),
            full, full, full, full,
            per_row(blocks, WIDE, BLOCK), per_row(tokens, 8),
            whole(first_w.shape), whole(second_w.shape), whole(qkv_w.shape), whole(gains.shape),
        ],
        out_specs=[
            per_row(tokens, width),
            pl.BlockSpec((width, width), lambda s: (0, jnp.clip(s - rows, 0, 2))),
            pl.BlockSpec((width, width), lambda s: (0, jnp.clip(s - rows - 3, 0, 3))),
            pl.BlockSpec((2, 8, width), lambda s: (0, 0, 0)),
            pl.BlockSpec((2, 8, width), lambda s: (0, 0, 0)),
        ],
        out_shape=[
            jax.ShapeDtypeStruct((rows, tokens, width), F32),
            jax.ShapeDtypeStruct((width, 3 * width), LOW),
            jax.ShapeDtypeStruct((width, 4 * width), LOW),
            jax.ShapeDtypeStruct((2, 8, width), F32),
            jax.ShapeDtypeStruct((2, 8, width), F32),
        ],
        scratch_shapes=[
            pltpu.VMEM((rows * tokens, width), LOW),
            pltpu.VMEM((rows * tokens, width), LOW),
            pltpu.VMEM((tokens, width), F32),
            pltpu.VMEM((tokens, width), LOW),
            pltpu.VMEM((tokens + 2 * REACH, width), F32),
        ],
        compiler_params=params(1),
        name="graph_backward",
    )(dq, dk, dv, low, two, unit, rstd, slope, hidden, agg1, agg2, x, adj, cols, first_w, second_w, qkv_w, gains)


def device_work(remote, depth, inputs, coords, neighbours, counts, doc_length, weights, shards,
                edge_proj, norm_gains, norm_shifts, distance_rate, order_rate, cotangent):
    rows, tokens, width = inputs.shape
    results = front(
        remote, depth, doc_length[:, 0], distance_rate, order_rate, neighbours, counts[:, None, :], coords, inputs,
        edge_proj, norm_gains, norm_shifts, weights, shards if remote else (),
    )
    (adj, cols, agg1, slope, hidden, agg2, unit, rstd, normed, low, qkv, att, probs, far, order, first_w, second_w, qkv_w) = results[:18]
    fulls = tuple(v.reshape(-1, v.shape[-1]) for v in results[18:]) if remote else shards
    out_w, up, down = fulls
    flat = lambda v: v.reshape(rows * tokens, width)
    tall = lambda v: v.reshape(rows, tokens, width)
    result, two, grad_att, grad_out, grad_up, grad_down, norms_late = block_both(
        att.reshape(-1, rows * tokens, BLOCK), flat(normed), flat(cotangent), out_w, up, down, norm_gains, norm_shifts
    )
    dq, dk, dv, rates = attention_backward(qkv, tall(grad_att), probs, far, order)
    input_grad, grad_qkv, grad_graph, norms_first, edge = graph_backward(
        dq, dk, dv, low, tall(two), unit, rstd, slope, hidden, agg1, agg2, inputs, adj, cols,
        first_w, second_w, qkv_w, norm_gains,
    )
    norms = jnp.concatenate([norms_first, norms_late], axis=0).sum(axis=1)
    rates = rates.sum(axis=(0, 3, 4)).reshape(-1, 2, 2)
    small = (edge.sum(axis=1), norms[0::2], norms[1::2], rates[:, :, 0].reshape(-1), rates[:, :, 1].reshape(-1))
    return tall(result), input_grad, grad_graph, grad_qkv, grad_out, grad_up, grad_down, small


def add_small(small, axes):
    edge, gains, shifts, rates, orders = small
    width = edge.shape[1]
    heads = rates.shape[0]
    line = jnp.concatenate([rates, orders, jnp.zeros((width - 2 * heads,), F32)])[None]
    total = lax.psum(jnp.concatenate([edge, gains, shifts, line], axis=0), axes)
    return total[0:2], total[2:5], total[5:8], total[8, :heads], total[8, heads : 2 * heads]


def local(
    sizes, inputs, coords, neighbours, counts, doc_length, self_one, near_one, self_two, near_two, edge_proj,
    qkv_proj, out_proj, up_proj, down_proj, norm_gains, norm_shifts, distance_rate, order_rate, cotangent,
):
    axes = ("wide", "narrow")
    width = inputs.shape[2]
    wide_size, narrow_size = sizes
    remote = wide_size % 4 == 0 and narrow_size == 2 and self_one.shape[0] % 8 == 0
    weights, shards = (self_one, near_one, self_two, near_two, qkv_proj), (out_proj, up_proj, down_proj)
    if not remote:
        gather = lambda v: lax.all_gather(v, axes, axis=0, tiled=True)
        weights, shards = tuple(map(gather, weights)), tuple(map(gather, shards))
    scatter = lambda v: lax.psum_scatter(v, axes, scatter_dimension=0, tiled=True)
    result, input_grad, grad_graph, grad_qkv, grad_out, grad_up, grad_down, small = device_work(
        remote, wide_size // 4, inputs, coords, neighbours, counts, doc_length, weights, shards,
        edge_proj, norm_gains, norm_shifts, distance_rate, order_rate, cotangent,
    )
    down_own = scatter(grad_down).astype(F32)
    up_own = scatter(jnp.concatenate([grad_up, grad_out], axis=1)).astype(F32)
    rest = scatter(jnp.concatenate([grad_graph, grad_qkv], axis=1)).astype(F32)
    edge, gains, shifts, rates, orders = add_small(small, axes)
    wide = up_proj.shape[1]
    return (
        result, input_grad,
        rest[:, :width], rest[:, width : 2 * width], rest[:, 2 * width : 3 * width], rest[:, 3 * width : 4 * width],
        edge,
        rest[:, 4 * width :], up_own[:, wide:], up_own[:, :wide], down_own,
        gains, shifts, rates, orders,
    )


def solution(mesh):
    axes = ("wide", "narrow")
    middle, last = P(None, axes, None), P(None, None, axes)
    count, weight, same = P(None, axes), P(axes, None), P()
    sizes = (mesh.shape["wide"], mesh.shape["narrow"])
    return jax.shard_map(
        functools.partial(local, sizes),
        mesh=mesh,
        in_specs=(middle, last, last, count, count)
        + (weight,) * 4
        + (same,)
        + (weight,) * 4
        + (same,) * 4
        + (middle,),
        out_specs=(middle, middle) + (weight,) * 4 + (same,) + (weight,) * 4 + (same,) * 4,
        check_vma=False,
    )
```

```python
import functools
import jax
import jax.numpy as jnp
from jax import lax
from jax.experimental import pallas as pl
from jax.experimental.pallas import tpu as pltpu
from jax.sharding import PartitionSpec as P

RADIUS = 128
REACH = 64
BLOCK = 128
WIDE = BLOCK + 2 * REACH
SPAN = BLOCK + 2 * RADIUS
FAR = 1e10
F32 = jnp.float32
LOW = jnp.bfloat16
VMEM = 62 * 2**20


def dot(left, right, dims):
    return lax.dot_general(left, right, ((dims[:1], dims[1:]), ((), ())), preferred_element_type=F32)


def nn(left, right):
    return dot(left, right, (1, 0))


def nt(left, right):
    return dot(left, right, (1, 1))


def tn(left, right):
    return dot(left, right, (0, 0))


def gelu_pair(pre):
    slope = 0.7978845608028654
    square = pre * pre
    half = 0.5 + 0.5 * jnp.tanh(pre * (slope + (slope * 0.044715) * square))
    act = pre * half
    deriv = half + act * (1.0 - half) * (2.0 * slope + (6.0 * slope * 0.044715) * square)
    return act, deriv


def norm_parts(values):
    centre = values - jnp.mean(values, axis=-1, keepdims=True)
    rstd = lax.rsqrt(jnp.mean(centre * centre, axis=-1, keepdims=True) + 1e-05)
    return centre * rstd, rstd


def norm_back(grad, unit, rstd, gain):
    scaled = grad * gain
    mean = jnp.mean(scaled, axis=-1, keepdims=True)
    along = jnp.mean(scaled * unit, axis=-1, keepdims=True)
    return rstd * (scaled - mean - unit * along)


def fold(values):
    rows, cols = values.shape
    return jnp.sum(values.reshape(rows // 8, 8, cols), axis=0)


def whole(shape, space=None):
    return pl.BlockSpec(shape, lambda *_: (0,) * len(shape), pipeline_mode=pl.Buffered(1))


def params(grid_rank, **more):
    return pltpu.CompilerParams(
        vmem_limit_bytes=VMEM, dimension_semantics=("arbitrary",) * grid_rank, **more
    )


def fill_bias(length, point_ref, far_ref, order_ref, row):
    tokens = point_ref.shape[2]
    side = jnp.zeros((2, RADIUS), F32)
    padded = jnp.concatenate([side, point_ref[row], side], axis=1)
    tall = jnp.concatenate([padded, jnp.zeros((6, tokens + 2 * RADIUS), F32)], axis=0)
    for b in range(tokens // BLOCK):
        window = tall[:, b * BLOCK : b * BLOCK + SPAN].T
        key_x, key_y = window[:, 0:1], window[:, 1:2]
        lanes = slice(b * BLOCK, (b + 1) * BLOCK)
        delta_x = key_x - point_ref[row, 0:1, lanes]
        delta_y = key_y - point_ref[row, 1:2, lanes]
        dist = jnp.log(1.0 + 16.0 * (delta_x * delta_x + delta_y * delta_y))
        query = lax.broadcasted_iota(jnp.int32, (SPAN, BLOCK), 1) + b * BLOCK
        key = lax.broadcasted_iota(jnp.int32, (SPAN, BLOCK), 0) + (b * BLOCK - RADIUS)
        allowed = (jnp.abs(query - key) <= RADIUS) & ((query >= length) == (key >= length))
        allowed = allowed & (key >= 0) & (key < tokens)
        far_ref[row, b] = jnp.where(allowed, dist, FAR)
        order_ref[row, b] = jnp.tanh(4.0 * delta_x)


def pair_rows(values):
    lane = lax.broadcasted_iota(jnp.int32, values.shape, 1)
    zero = jnp.zeros_like(values)
    first = jnp.where(lane < BLOCK // 2, values, zero)
    second = jnp.where(lane < BLOCK // 2, zero, values)
    return jnp.concatenate([first, second], axis=0)


def pair_pick(values):
    lane = lax.broadcasted_iota(jnp.int32, (BLOCK, BLOCK), 1)
    return jnp.where(lane < BLOCK // 2, values[:BLOCK], values[BLOCK:])


def pad_rows(pad_ref, values):
    tokens = values.shape[0]
    zeros = jnp.zeros((RADIUS, values.shape[1]), pad_ref.dtype)
    pad_ref[pl.ds(0, RADIUS), :] = zeros
    pad_ref[pl.ds(RADIUS + tokens, RADIUS), :] = zeros
    pad_ref[pl.ds(RADIUS, tokens), :] = values


FIRST, OWN, PASSED, SIBLING = 0, 1, 2, 3


class Place:
    def __init__(self, depth):
        self.depth = depth
        wide, self.x = lax.axis_index("wide"), lax.axis_index("narrow")
        self.core = lax.rem(wide, 2)
        self.y = lax.rem(lax.div(wide, 2), 2)
        self.z = lax.div(wide, 4)
        core, y, x = self.core, self.y, self.x
        self.first_y = (1 - core) * (1 - y) + core * y
        self.first_x = core * (1 - x) + (1 - core) * x
        self.second_y = core * (1 - y) + (1 - core) * y
        self.second_x = (1 - core) * (1 - x) + core * x

    def at(self, z, y, core, x):
        return ((z * 2 + y) * 2 + core, x)

    def along(self, k):
        return lax.rem(self.z + k, self.depth)

    def partners(self):
        along = [self.at(self.along(k), self.y, self.core, self.x) for k in range(1, self.depth)]
        return along + [
            self.at(self.z, self.first_y, self.core, self.first_x),
            self.at(self.z, self.second_y, self.core, self.second_x),
            self.at(self.z, self.y, 1 - self.core, self.x),
        ]


def meet(place):
    barrier = pltpu.get_barrier_semaphore()
    partners = place.partners()
    for partner in partners:
        pl.semaphore_signal(barrier, inc=1, device_id=partner, device_id_type=pl.DeviceIdType.MESH)
    pl.semaphore_wait(barrier, len(partners))


class Gather:
    def __init__(self, place, land, send, recv, group):
        self.place, self.land, self.send, self.recv, self.group = place, land, send, recv, group

    def copy(self, view, slot, device):
        return pltpu.make_async_remote_copy(
            src_ref=view, dst_ref=view, send_sem=self.send.at[self.group, slot], recv_sem=self.recv.at[self.group, slot],
            device_id=device, device_id_type=pl.DeviceIdType.MESH,
        )

    def pieces(self, stage):
        p, land = self.place, self.land
        base = p.depth - 1
        mine = land.at[:, p.y, p.core, p.x]
        if stage == "along":
            here = land.at[p.z, p.y, p.core, p.x]
            found = []
            for k in range(1, p.depth):
                there = land.at[p.along(p.depth - k), p.y, p.core, p.x]
                found.append((here, there, k - 1, p.at(p.along(k), p.y, p.core, p.x)))
            return found
        first = p.at(p.z, p.first_y, p.core, p.first_x)
        second = p.at(p.z, p.second_y, p.core, p.second_x)
        if stage == FIRST:
            return [(mine, land.at[:, p.first_y, p.core, p.first_x], base, first)]
        if stage == OWN:
            return [(mine, land.at[:, p.second_y, p.core, p.second_x], base + 1, second)]
        if stage == PASSED:
            return [(land.at[:, p.first_y, p.core, p.first_x], land.at[:, 1 - p.y, p.core, 1 - p.x], base + 2, second)]
        return [(land.at[:, :, p.core], land.at[:, :, 1 - p.core], base + 3, p.at(p.z, p.y, 1 - p.core, p.x))]

    def start(self, *stages):
        for stage in stages:
            for leaves, _, slot, device in self.pieces(stage):
                self.copy(leaves, slot, device).start()

    def arrive(self, *stages):
        for stage in stages:
            for _, arrives, slot, device in self.pieces(stage):
                self.copy(arrives, slot, device).wait_recv()

    def sent(self):
        for stage in ("along", FIRST, OWN, PASSED, SIBLING):
            for leaves, _, slot, device in self.pieces(stage):
                self.copy(leaves, slot, device).wait_send()


def merge_rows(full, land):
    depth, rows = land.shape[0], land.shape[4]

    @pl.loop(0, depth * 4)
    def _(k):
        z, y, core = lax.div(k, 4), lax.rem(lax.div(k, 2), 2), lax.rem(k, 2)
        pair = jnp.concatenate([land[z, y, core, 0].astype(F32), land[z, y, core, 1].astype(F32)], axis=0)
        full[pl.ds(pl.multiple_of(k * 2 * rows, 16), 2 * rows), :] = pair.astype(LOW)


def front_kernel(remote, *refs):
    (length_ref, dist_rate_ref, order_rate_ref, near_ref, count_ref, point_ref, x_ref, edge_w_ref, gain_ref, shift_ref,
     self1_ref, near1_ref, self2_ref, near2_ref, qkv_w_ref) = refs[:15]
    refs = refs[15:]
    shards, refs = (refs[:3], refs[3:]) if remote else ((), refs)
    outs, refs = refs[:18], refs[18:]
    fulls, refs = (refs[:3], refs[3:]) if remote else ((), refs)
    (adj, cols, agg1, slope, hidden, agg2, unit, rstd, normed, low, qkv, att, probs, far, order,
     first_w, second_w, third_w, pad, point_pad, rel, keys, values, out_sem, probs_sem, in_sem) = refs[:26]
    rows, slots, tokens = near_ref.shape
    width = x_ref.shape[2]
    pairs = width // BLOCK
    blocks = tokens // BLOCK
    chunk = 2 * BLOCK

    writes = {}

    def write(k, source, dest=None):
        writes[k] = pltpu.make_async_copy(source, outs[k] if dest is None else dest, out_sem.at[k])
        writes[k].start()

    if remote:
        land_a, land_b, land_q, send, recv = refs[26:]
        place = Place(land_a.shape[0])
        lands = (land_a, land_b, land_q) + tuple(fulls)
        groups = [Gather(place, land, send, recv, g) for g, land in enumerate(lands)]
        ga, gb, gq, go, gu, gd = groups
        column = lambda land, k: land.at[place.z, place.y, place.core, place.x, :, pl.ds(k * width, width)]
        own = lambda land: land.at[place.z, place.y, place.core, place.x]
        loads = [
            [pltpu.make_async_copy(ref, column(land_a, k), in_sem.at[k]) for k, ref in enumerate((self1_ref, near1_ref))],
            [pltpu.make_async_copy(ref, column(land_b, k), in_sem.at[2 + k]) for k, ref in enumerate((self2_ref, near2_ref))],
            [pltpu.make_async_copy(qkv_w_ref, own(land_q), in_sem.at[4])],
        ] + [[pltpu.make_async_copy(ref, own(full), in_sem.at[5 + k])] for k, (ref, full) in enumerate(zip(shards, fulls))]
        for load in loads:
            for copy in load:
                copy.start()
        meet(place)

        def begin(g):
            for copy in loads[g]:
                copy.wait()
            groups[g].start("along")

        begin(0)
        begin(1)
    else:
        loads = [
            pltpu.make_async_copy(ref, dest, in_sem.at[k])
            for k, (ref, dest) in enumerate((
                (self1_ref, first_w.at[:, pl.ds(0, width)]), (near1_ref, first_w.at[:, pl.ds(width, width)]),
                (self2_ref, second_w.at[:, pl.ds(0, width)]), (near2_ref, second_w.at[:, pl.ds(width, width)]),
                (qkv_w_ref, third_w),
            ))
        ]
        for copy in loads:
            copy.start()

    side = jnp.zeros((REACH, width), LOW)
    pad[pl.ds(0, REACH), :] = side
    pad[pl.ds(tokens + REACH, REACH), :] = side

    @pl.loop(0, rows)
    def _(row):
        length = length_ref[row]
        pad[pl.ds(REACH, tokens), :] = x_ref[row]
        points = point_ref[row]
        high = points.astype(LOW).astype(F32)
        mid = (points - high).astype(LOW).astype(F32)
        tail = points - high - mid
        split = jnp.concatenate([high, mid, tail, jnp.ones((1, tokens), F32), jnp.zeros((9, tokens), F32)], axis=0)
        edge_side = jnp.zeros((16, REACH), F32)
        point_pad[...] = jnp.concatenate([edge_side, split, edge_side], axis=1).astype(LOW)

        @pl.loop(0, blocks)
        def _(b):
            start = pl.multiple_of(b * BLOCK, BLOCK)
            lanes = pl.ds(start, BLOCK)
            near = near_ref[row, :, lanes]
            count = count_ref[row, :, lanes]
            spot = lax.broadcasted_iota(jnp.int32, (1, BLOCK), 1) + start
            slot = lax.broadcasted_iota(jnp.int32, (slots, BLOCK), 0)
            same = (near >= length) == (spot >= length)
            rel[...] = jnp.where((slot < count) & same, near - (start - REACH), -1)
            target = lax.broadcasted_iota(jnp.int32, (WIDE, BLOCK), 0)
            total = jnp.zeros((WIDE, BLOCK), F32)
            for s in range(slots):
                total = total + jnp.where(rel[s : s + 1, :] == target, 1.0, 0.0)
            band = total.astype(LOW)
            adj[row, b] = band
            sums = nn(point_pad[:, pl.ds(start, WIDE)], band)
            inverse = 1.0 / count.astype(F32)
            here = point_ref[row, :, lanes]
            edge = (sums[0:2] + sums[2:4] + sums[4:6] - sums[6:7] * here) * inverse
            lines = jnp.concatenate([edge, inverse, jnp.zeros((5, BLOCK), F32)], axis=0).T
            cols[row, lanes, :] = lines
            agg = tn(band, pad[pl.ds(start, WIDE), :])
            agg1[row, lanes, :] = (agg * lines[:, 2:3]).astype(LOW)

        if remote:
            @pl.when(row == 0)
            def _():
                ga.arrive("along")
                ga.start(FIRST, OWN)
                begin(2)

    write(0, adj)
    write(1, cols)
    write(2, agg1)
    if remote:
        ga.arrive(FIRST)
        ga.start(PASSED)
        gb.arrive("along")
        gb.start(FIRST, OWN)

    @pl.loop(0, rows)
    def _(row):
        fill_bias(length_ref[row], point_ref, far, order, row)

    write(13, far)
    write(14, order)
    if remote:
        ga.arrive(OWN, PASSED)
        ga.start(SIBLING)
        gb.arrive(FIRST)
        gb.start(PASSED)
        gq.arrive("along")
        gq.start(FIRST, OWN)
        begin(3)
        begin(4)
        ga.arrive(SIBLING)
        merge_rows(first_w, land_a)
    else:
        for copy in loads:
            copy.wait()
        write(16, second_w)
        write(17, third_w)
    write(15, first_w)

    @pl.loop(0, rows)
    def _(row):
        for c in range(tokens // chunk):
            part = slice(c * chunk, (c + 1) * chunk)
            pre = nn(x_ref[row, part, :], first_w[:, 0:width])
            pre = pre + nn(agg1[row, part, :], first_w[:, width : 2 * width])
            pre = pre + cols[row, part, 0:1] * edge_w_ref[0:1, :] + cols[row, part, 1:2] * edge_w_ref[1:2, :]
            act, deriv = gelu_pair(pre)
            slope[row, part, :] = deriv.astype(LOW)
            hidden[row, part, :] = act.astype(LOW)
            pad[REACH + c * chunk : REACH + (c + 1) * chunk, :] = act.astype(LOW)
        for b in range(blocks):
            lanes = slice(b * BLOCK, (b + 1) * BLOCK)
            agg = tn(adj[row, b], pad[b * BLOCK : b * BLOCK + WIDE, :])
            agg2[row, lanes, :] = (agg * cols[row, lanes, 2:3]).astype(LOW)
        if remote:
            @pl.when(row == 0)
            def _():
                gb.arrive(OWN, PASSED)
                gb.start(SIBLING)

    write(3, slope)
    write(4, hidden)
    write(5, agg2)
    if remote:
        gq.arrive(FIRST)
        gq.start(PASSED)
        gb.arrive(SIBLING)
        merge_rows(second_w, land_b)
        write(16, second_w)

    @pl.loop(0, rows)
    def _(row):
        for c in range(tokens // chunk):
            part = slice(c * chunk, (c + 1) * chunk)
            resid = x_ref[row, part, :].astype(F32) + nn(hidden[row, part, :], second_w[:, 0:width])
            resid = resid + nn(agg2[row, part, :], second_w[:, width : 2 * width])
            plain, scale = norm_parts(resid)
            unit[row, part, :] = plain.astype(LOW)
            rstd[row, part, :] = scale
            out = plain * gain_ref[0:1, :] + shift_ref[0:1, :]
            normed[row, part, :] = out
            low[row, part, :] = out.astype(LOW)
        if remote:
            @pl.when(row == 0)
            def _():
                for g in (go, gu):
                    g.arrive("along")
                    g.start(FIRST, OWN)
                begin(5)

    write(6, unit)
    write(7, rstd)
    write(8, normed)
    write(9, low)
    if remote:
        gq.arrive(OWN, PASSED)
        gq.start(SIBLING)
        for g in (go, gu):
            g.arrive(FIRST)
            g.start(PASSED)
        gq.arrive(SIBLING)
        merge_rows(third_w, land_q)
        write(17, third_w)

    @pl.loop(0, rows)
    def _(row):
        for c in range(tokens // chunk):
            part = slice(c * chunk, (c + 1) * chunk)
            out = nn(low[row, part, :], third_w[...]).astype(LOW)
            for k in range(3 * pairs):
                qkv[k, row, part, :] = out[:, k * BLOCK : (k + 1) * BLOCK]

    write(10, qkv)
    zeros = jnp.zeros((RADIUS, BLOCK), LOW)
    for ref in (keys, values):
        ref[pl.ds(0, RADIUS), :] = zeros
        ref[pl.ds(RADIUS + tokens, RADIUS), :] = zeros

    @pl.loop(0, rows * pairs)
    def _(turn):
        row, pair, slot = lax.div(turn, pairs), lax.rem(turn, pairs), lax.rem(turn, 2)
        if remote:
            @pl.when(turn == 1)
            def _():
                gd.arrive("along")
                gd.start(FIRST, OWN)

            @pl.when(turn == 4)
            def _():
                for g in (go, gu):
                    g.arrive(OWN, PASSED)
                    g.start(SIBLING)
                gd.arrive(FIRST)
                gd.start(PASSED)

            @pl.when(turn == 9)
            def _():
                gd.arrive(OWN, PASSED)
                gd.start(SIBLING)

        def probs_copy(t, s):
            return pltpu.make_async_copy(
                probs.at[s], outs[12].at[lax.div(t, pairs), lax.rem(t, pairs)], probs_sem.at[s]
            )

        @pl.when(turn >= 2)
        def _():
            probs_copy(turn - 2, slot).wait()

        keys[pl.ds(RADIUS, tokens), :] = qkv[pairs + pair, row]
        values[pl.ds(RADIUS, tokens), :] = qkv[2 * pairs + pair, row]
        for b in range(blocks):
            lanes = slice(b * BLOCK, (b + 1) * BLOCK)
            window = slice(b * BLOCK, b * BLOCK + SPAN)
            queries = pair_rows(qkv[pair, row, lanes, :] * 0.125)
            raw = nt(keys[window, :], queries)
            sides = []
            for h in range(2):
                bias = order_rate_ref[2 * pair + h] * order[row, b] - dist_rate_ref[2 * pair + h] * far[row, b]
                scores = raw[:, h * BLOCK : (h + 1) * BLOCK] + bias
                grown = jnp.exp(scores - jnp.max(scores, axis=0, keepdims=True))
                scale = 1.0 / jnp.sum(grown, axis=0, keepdims=True)
                sides.append((grown * scale).astype(LOW))
            both = jnp.concatenate(sides, axis=1)
            probs[slot, b] = both
            att[pair, row, lanes, :] = pair_pick(tn(both, values[window, :])).astype(LOW)
        probs_copy(turn, slot).start()

    last = rows * pairs
    for turn in (last - 2, last - 1):
        pltpu.make_async_copy(probs.at[turn % 2], outs[12].at[turn // pairs, turn % pairs], probs_sem.at[turn % 2]).wait()
    write(11, att)
    if remote:
        for g in (go, gu, gd):
            g.arrive(SIBLING)
        for g in groups:
            g.sent()
    for copy in writes.values():
        copy.wait()


def front(remote, depth, length, dist_rate, order_rate, near, count, point, x, edge_w, gains, shifts, weights, shards):
    rows, tokens, width = x.shape
    slots = near.shape[1]
    blocks, pairs = tokens // BLOCK, width // BLOCK
    smem, vmem, hbm = (pl.BlockSpec(memory_space=s) for s in (pltpu.SMEM, pltpu.VMEM, pl.ANY))
    each = lambda dtype, *shape: ((rows,) + shape, dtype)
    kept = [
        each(LOW, blocks, WIDE, BLOCK),
        each(F32, tokens, 8),
        each(LOW, tokens, width),
        each(LOW, tokens, width),
        each(LOW, tokens, width),
        each(LOW, tokens, width),
        each(LOW, tokens, width),
        each(F32, tokens, 1),
        each(F32, tokens, width),
        each(LOW, tokens, width),
        ((3 * pairs, rows, tokens, BLOCK), LOW),
        ((pairs, rows, tokens, BLOCK), LOW),
        each(LOW, pairs, blocks, SPAN, 2 * BLOCK),
        each(F32, blocks, SPAN, BLOCK),
        each(F32, blocks, SPAN, BLOCK),
        ((width, 2 * width), LOW),
        ((width, 2 * width), LOW),
        ((width, 3 * width), LOW),
    ]
    out_shape = [jax.ShapeDtypeStruct(*k) for k in kept]
    kept[12] = ((2, blocks, SPAN, 2 * BLOCK), LOW)
    scratch = [pltpu.VMEM(*k) for k in kept]
    scratch += [
        pltpu.VMEM((tokens + 2 * REACH, width), LOW),
        pltpu.VMEM((16, tokens + 2 * REACH), LOW),
        pltpu.VMEM((slots, BLOCK), jnp.int32),
        pltpu.VMEM((tokens + 2 * RADIUS, BLOCK), LOW),
        pltpu.VMEM((tokens + 2 * RADIUS, BLOCK), LOW),
        pltpu.SemaphoreType.DMA((18,)),
        pltpu.SemaphoreType.DMA((2,)),
        pltpu.SemaphoreType.DMA((8,)),
    ]
    more = {}
    if remote:
        blocked = lambda shape: (depth, 2, 2, 2) + shape
        out_shape += [jax.ShapeDtypeStruct(blocked(s.shape), LOW) for s in shards]
        share = weights[0].shape[0]
        scratch += [pltpu.VMEM(blocked((share, k * width)), LOW) for k in (2, 2, 3)]
        scratch += [pltpu.SemaphoreType.DMA((6, depth + 3))] * 2
        more = {"collective_id": CALLS["front"], "has_side_effects": True}
    return pl.pallas_call(
        functools.partial(front_kernel, remote),
        in_specs=[smem] * 3 + [vmem] * 7 + [hbm] * (len(weights) + len(shards)),
        out_specs=[hbm] * len(out_shape),
        out_shape=out_shape,
        scratch_shapes=scratch,
        compiler_params=pltpu.CompilerParams(vmem_limit_bytes=VMEM, **more),
        name="front",
    )(length, dist_rate, order_rate, near, count, point, x, edge_w, gains, shifts, *weights, *shards)


TILE = 256
PARTS = 6


def block_kernel(
    att_ref, normed_ref, cot_ref, out_w_ref, up_ref, down_ref, gain_ref, shift_ref,
    result_ref, grad_two_ref, grad_att_ref, grad_out_ref, grad_up_ref, grad_down_ref, norms_ref,
    act_all, up_all, second_all, down_all, attn_all, att_all, slope_tile,
):
    step = pl.program_id(0)
    width = normed_ref.shape[1]
    steps = act_all.shape[1] // TILE
    piece = act_all.shape[2]

    @pl.when(step == 0)
    def _():
        norms_ref[...] = jnp.zeros_like(norms_ref)

    @pl.when(step < steps)
    def _():
        at = pl.ds(pl.multiple_of(step * TILE, TILE), TILE)
        att = jnp.concatenate([att_ref[k] for k in range(att_ref.shape[0])], axis=1)
        att_all[at, :] = att
        resid = normed_ref[...] + nn(att, out_w_ref[...])
        unit_two, rstd_two = norm_parts(resid)
        gain_two, gain_three = gain_ref[1:2, :], gain_ref[2:3, :]
        normed = unit_two * gain_two + shift_ref[1:2, :]
        second = normed.astype(LOW)
        second_all[at, :] = second
        resid = normed
        for c in range(PARTS):
            cols = slice(c * piece, (c + 1) * piece)
            act, deriv = gelu_pair(nn(second, up_ref[:, cols]))
            slope_tile[:, cols] = deriv.astype(LOW)
            act = act.astype(LOW)
            act_all[c, at, :] = act
            resid = resid + nn(act, down_ref[cols, :])
        unit, rstd = norm_parts(resid)
        result_ref[...] = (unit * gain_three + shift_ref[2:3, :]).astype(LOW)
        cot = cot_ref[...].astype(F32)
        norms_ref[2] += fold(cot * unit)
        norms_ref[3] += fold(cot)
        grad = norm_back(cot, unit, rstd, gain_three)
        low = grad.astype(LOW)
        down_all[at, :] = low
        for c in range(PARTS):
            cols = slice(c * piece, (c + 1) * piece)
            up_low = (nt(low, down_ref[cols, :]) * slope_tile[:, cols].astype(F32)).astype(LOW)
            up_all[c, at, :] = up_low
            grad = grad + nt(up_low, up_ref[:, cols])
        norms_ref[0] += fold(grad * unit_two)
        norms_ref[1] += fold(grad)
        grad = norm_back(grad, unit_two, rstd_two, gain_two)
        grad_two_ref[...] = grad
        low = grad.astype(LOW)
        attn_all[at, :] = low
        grad_att_ref[...] = nt(low, out_w_ref[...]).astype(LOW)

    @pl.when(step >= steps)
    def _():
        c = step - steps
        grad_down_ref[...] = tn(act_all[c], down_all[...]).astype(LOW)
        grad_up_ref[...] = tn(second_all[...], up_all[c]).astype(LOW)
        cols = pl.ds(pl.multiple_of(c * BLOCK, BLOCK), BLOCK)
        grad_out_ref[...] = tn(att_all[:, cols], attn_all[...]).astype(LOW)


def block_both(att, normed, cot, out_w, up, down, gains, shifts):
    tokens, width = normed.shape
    wide = up.shape[1]
    steps = tokens // TILE
    piece = wide // PARTS
    tile = lambda cols: pl.BlockSpec((TILE, cols), lambda s: (jnp.minimum(s, steps - 1), 0))
    late = lambda s: jnp.maximum(s - steps, 0)
    return pl.pallas_call(
        block_kernel,
        grid=(steps + PARTS,),
        in_specs=[
            pl.BlockSpec((width // BLOCK, TILE, BLOCK), lambda s: (0, jnp.minimum(s, steps - 1), 0)), tile(width), tile(width),
            whole((width, width)), whole(up.shape), whole(down.shape), whole(gains.shape), whole(shifts.shape),
        ],
        out_specs=[
            tile(width), tile(width), tile(width),
            pl.BlockSpec((width // PARTS, width), lambda s: (late(s), 0)),
            pl.BlockSpec((width, piece), lambda s: (0, late(s))),
            pl.BlockSpec((piece, width), lambda s: (late(s), 0)),
            pl.BlockSpec((4, 8, width), lambda s: (0, 0, 0)),
        ],
        out_shape=[
            jax.ShapeDtypeStruct((tokens, width), LOW),
            jax.ShapeDtypeStruct((tokens, width), F32),
            jax.ShapeDtypeStruct((tokens, width), LOW),
            jax.ShapeDtypeStruct((width, width), LOW),
            jax.ShapeDtypeStruct(up.shape, LOW),
            jax.ShapeDtypeStruct(down.shape, LOW),
            jax.ShapeDtypeStruct((4, 8, width), F32),
        ],
        scratch_shapes=[
            pltpu.VMEM((PARTS, tokens, piece), LOW),
            pltpu.VMEM((PARTS, tokens, piece), LOW),
            pltpu.VMEM((tokens, width), LOW),
            pltpu.VMEM((tokens, width), LOW),
            pltpu.VMEM((tokens, width), LOW),
            pltpu.VMEM((tokens, width), LOW),
            pltpu.VMEM((TILE, wide), LOW),
        ],
        compiler_params=params(1),
        name="block_both",
    )(att, normed, cot, out_w, up, down, gains, shifts)


CALLS = {"front": 0, "attention": 1, "graph": 2}


class Scatter:
    def __init__(self, place, leaving, room, send, recv, group):
        self.place, self.leaving, self.send, self.recv, self.group = place, leaving, send, recv, group
        self.total, self.lands = room[0], room[1:]

    def copies(self, stage):
        p, total = self.place, self.total
        if stage == 0:
            found = [(self.leaving, self.lands[0], 0, p.at(p.z, p.y, 1 - p.core, p.x))]
        elif stage == 1:
            second = p.at(p.z, p.second_y, p.core, p.second_x)
            found = [
                (total.at[:, p.second_y, p.second_x], self.lands[1].at[0], 1, second),
                (total.at[:, 1 - p.y, 1 - p.x], self.lands[1].at[1], 2, second),
            ]
        elif stage == 2:
            first = p.at(p.z, p.first_y, p.core, p.first_x)
            found = [(total.at[:, p.first_y, p.first_x], self.lands[2], 3, first)]
        else:
            found = [
                (total.at[p.along(k), p.y, p.x], self.lands[3].at[k - 1], 3 + k, p.at(p.along(k), p.y, p.core, p.x))
                for k in range(1, p.depth)
            ]
        return [
            pltpu.make_async_remote_copy(
                src_ref=source, dst_ref=land, send_sem=self.send.at[self.group, slot],
                recv_sem=self.recv.at[self.group, slot], device_id=device, device_id_type=pl.DeviceIdType.MESH,
            )
            for source, land, slot, device in found
        ]

    def start(self, stage):
        for copy in self.copies(stage):
            copy.start()

    def arrive(self, stage):
        for copy in self.copies(stage):
            copy.wait_recv()

    def add(self, y, x, land):
        @pl.loop(0, self.place.depth)
        def _(z):
            self.total[z, y, x] = (self.total[z, y, x].astype(F32) + land(z).astype(F32)).astype(LOW)

    def fold(self, stage):
        p = self.place
        self.arrive(stage)
        if stage == 0:
            add = lambda y, x: self.add(y, x, lambda z: self.lands[0][z, y, x])
            add(p.second_y, p.second_x)
            add(1 - p.y, 1 - p.x)
            self.start(1)
            add(p.first_y, p.first_x)
            add(p.y, p.x)
        elif stage == 1:
            self.add(p.first_y, p.first_x, lambda z: self.lands[1][1, z])
            self.start(2)
            self.add(p.y, p.x, lambda z: self.lands[1][0, z])
        else:
            self.add(p.y, p.x, lambda z: self.lands[2][z])
            self.start(3)

    def finish(self):
        p = self.place
        self.arrive(3)
        result = self.total[p.z, p.y, p.x].astype(F32)
        for k in range(p.depth - 1):
            result = result + self.lands[3][k].astype(F32)
        return result

    def sent(self):
        for stage in range(4):
            for copy in self.copies(stage):
                copy.wait_send()


def scatter_room(depth, share, cols, kept=()):
    return [
        pltpu.VMEM(shape + (share, cols), LOW)
        for shape in (kept + (depth, 2, 2), (depth, 2, 2), (2, depth), (depth,), (depth - 1,))
    ]


def attention_back_kernel(remote, pairs, *refs):
    (q_ref, k_ref, v_ref, grad_ref, probs_ref, far_ref, order_ref, low_ref) = refs[:8]
    refs = refs[8:]
    sources, refs = (refs[:2], refs[2:]) if remote else ((), refs)
    (dq_ref, dk_ref, dv_ref, rate_ref, grad_qkv_ref), refs = refs[:5], refs[5:]
    owned, refs = (refs[:2], refs[2:]) if remote else ((), refs)
    (keys, values, grad_keys, grad_values, all_q, all_k, all_v), refs = refs[:7], refs[7:]
    step = pl.program_id(0)
    tokens = q_ref.shape[2]
    turns = all_q.shape[0] * pairs

    def when(k, action):
        @pl.when(step == k)
        def _():
            action()

    if remote:
        rooms, (send, recv, own_sem) = (refs[:5], refs[5:10]), refs[10:]
        place = Place(rooms[0][0].shape[0])
        own = [
            pltpu.make_async_copy(source.at[:, :, place.core], room[0], own_sem.at[g])
            for g, (source, room) in enumerate(zip(sources, rooms))
        ]
        down, out = [
            Scatter(place, source.at[:, :, 1 - place.core], room, send, recv, g)
            for g, (source, room) in enumerate(zip(sources, rooms))
        ]

        def begin():
            for copy in own:
                copy.start()
            meet(place)
            down.start(0)
            out.start(0)

        def first():
            own[0].wait()
            down.fold(0)
            own[1].wait()
            out.fold(0)

        when(0, begin)
        when(2, first)
        when(7, lambda: (down.fold(1), out.fold(1)))
        when(10, lambda: (down.fold(2), out.fold(2)))

    @pl.when(step < turns)
    def _():
        row, pair = lax.div(step, pairs), lax.rem(step, pairs)
        pad_rows(keys, k_ref[0, 0])
        pad_rows(values, v_ref[0, 0])
        grad_keys[...] = jnp.zeros_like(grad_keys)
        grad_values[...] = jnp.zeros_like(grad_values)
        sums = [jnp.zeros((8, BLOCK), F32)] * 4
        cols = pl.ds(pl.multiple_of(pair * BLOCK, BLOCK), BLOCK)
        for b in range(tokens // BLOCK):
            lanes = slice(b * BLOCK, (b + 1) * BLOCK)
            window = slice(b * BLOCK, b * BLOCK + SPAN)
            queries = pair_rows(q_ref[0, 0, lanes, :] * 0.125)
            grads = pair_rows(grad_ref[0, lanes, :])
            probs_low = probs_ref[0, 0, b]
            back = nt(values[window, :], grads)
            dist = jnp.where(far_ref[0, b] < FAR, far_ref[0, b], 0.0)
            order = order_ref[0, b]
            sides = []
            for h in range(2):
                probs = probs_low[:, h * BLOCK : (h + 1) * BLOCK].astype(F32)
                part = back[:, h * BLOCK : (h + 1) * BLOCK]
                delta = jnp.sum(probs * part, axis=0, keepdims=True)
                scores = probs * (part - delta)
                sums[2 * h] = sums[2 * h] - fold(scores * dist)
                sums[2 * h + 1] = sums[2 * h + 1] + fold(scores * order)
                sides.append(scores.astype(LOW))
            scores_low = jnp.concatenate(sides, axis=1)
            grad_values[window, :] += nn(probs_low, grads)
            grad_keys[window, :] += nn(scores_low, queries)
            grad_queries = (pair_pick(tn(scores_low, keys[window, :])) * 0.125).astype(LOW)
            dq_ref[0, lanes, :] = grad_queries
            all_q[row, lanes, cols] = grad_queries
        dk = grad_keys[pl.ds(RADIUS, tokens), :].astype(LOW)
        dv = grad_values[pl.ds(RADIUS, tokens), :].astype(LOW)
        dk_ref[0], all_k[row, :, cols] = dk, dk
        dv_ref[0], all_v[row, :, cols] = dv, dv
        for k in range(4):
            rate_ref[0, 0, k] = sums[k]

    for k, ref in enumerate((all_q, all_k, all_v)):
        @pl.when(step == turns + k)
        def _(ref=ref):
            flat = lambda v: v.reshape(-1, v.shape[-1])
            grad_qkv_ref[...] = tn(flat(low_ref[...]), flat(ref[...])).astype(LOW)

    if remote:
        def last():
            owned[0][...] = down.finish()
            owned[1][...] = out.finish()
            down.sent()
            out.sent()

        when(turns + 2, last)


def attention_backward(remote, depth, qkv, grad, probs, far, order, low, sources):
    pairs, rows, tokens = qkv.shape[0] // 3, qkv.shape[1], qkv.shape[2]
    width = pairs * BLOCK
    blocks = tokens // BLOCK
    turns = rows * pairs
    where = lambda s: (jnp.minimum(s, turns - 1) // pairs, jnp.minimum(s, turns - 1) % pairs)
    row_of, pair_of = lambda s: where(s)[0], lambda s: where(s)[1]
    part = lambda k: pl.BlockSpec((1, 1, tokens, BLOCK), lambda s: (k * pairs + pair_of(s), row_of(s), 0, 0))
    flat = pl.BlockSpec((1, tokens, BLOCK), lambda s: (row_of(s), 0, pair_of(s)))
    bias = pl.BlockSpec((1, blocks, SPAN, BLOCK), lambda s: (row_of(s), 0, 0, 0))
    grads = jax.ShapeDtypeStruct((rows, tokens, width), LOW)
    in_specs = [part(0), part(1), part(2), flat]
    in_specs += [pl.BlockSpec((1, 1, blocks, SPAN, 2 * BLOCK), lambda s: where(s) + (0, 0, 0)), bias, bias, whole(low.shape)]
    out_specs = [flat] * 3 + [
        pl.BlockSpec((1, 1, 4, 8, BLOCK), lambda s: where(s) + (0, 0, 0)),
        pl.BlockSpec((width, width), lambda s: (0, jnp.clip(s - turns, 0, 2))),
    ]
    out_shape = [grads] * 3 + [
        jax.ShapeDtypeStruct((rows, pairs, 4, 8, BLOCK), F32),
        jax.ShapeDtypeStruct((width, 3 * width), LOW),
    ]
    scratch = [pltpu.VMEM((tokens + 2 * RADIUS, BLOCK), LOW)] * 2
    scratch += [pltpu.VMEM((tokens + 2 * RADIUS, BLOCK), F32)] * 2
    scratch += [pltpu.VMEM((rows, tokens, width), LOW)] * 3
    more = {}
    if remote:
        in_specs += [pl.BlockSpec(memory_space=pl.ANY)] * 2
        for source in sources:
            shape = source.shape[4:]
            out_specs.append(pl.BlockSpec(shape, lambda s: (0, 0)))
            out_shape.append(jax.ShapeDtypeStruct(shape, F32))
            scratch += scatter_room(depth, *shape)
        scratch += [pltpu.SemaphoreType.DMA((2, depth + 3))] * 2 + [pltpu.SemaphoreType.DMA((2,))]
        more = {"collective_id": CALLS["attention"], "has_side_effects": True}
    return pl.pallas_call(
        functools.partial(attention_back_kernel, remote, pairs),
        grid=(turns + 3,),
        in_specs=in_specs,
        out_specs=out_specs,
        out_shape=out_shape,
        scratch_shapes=scratch,
        compiler_params=params(1, **more),
        name="attention_backward",
    )(qkv, qkv, qkv, grad, probs, far, order, low, *(sources if remote else ()))


def graph_back_kernel(remote, *refs):
    (dq_in, dk_in, dv_in, two_in, unit_in, rstd_in, slope_in, hidden_in, agg2_in, agg1_in, x_in, adj_in, cols_in,
     first_in, second_in, qkv_w_in, gain_ref, late_ref, rate_ref) = refs[:19]
    refs = refs[19:]
    sources, refs = (refs[:2], refs[2:]) if remote else ((), refs)
    (input_grad_out, edge_out, gains_out, shifts_out, rates_out), refs = refs[:5], refs[5:]
    owned, refs = (refs[:6], refs[6:]) if remote else (refs[:2], refs[2:])
    (dq, dk, dv, two, unit, rstd, slope, hidden, agg2, adj, cols, first_w, second_w, qkv_w,
     back, norms, edge_sums, row_sem, in_sem, out_sem), refs = refs[:20], refs[20:]
    rows, tokens, width = dq.shape
    blocks, chunk = tokens // BLOCK, 2 * BLOCK
    chunks = tokens // chunk
    agg1, x, branch, mean, pre, one = agg2, hidden, dq, dk, dv, two

    by_row = [(dq_in, dq), (dk_in, dk), (dv_in, dv), (two_in, two), (unit_in, unit), (rstd_in, rstd)]
    row_load = lambda k, row: pltpu.make_async_copy(by_row[k][0].at[row], by_row[k][1].at[row], row_sem.at[k, row])
    once = [(qkv_w_in, qkv_w), (second_in, second_w), (cols_in, cols), (hidden_in, hidden), (agg2_in, agg2),
            (adj_in, adj), (slope_in, slope), (first_in, first_w), (x_in, x), (agg1_in, agg1)]
    load = lambda k: pltpu.make_async_copy(*once[k], in_sem.at[k])
    load(0).start()
    for k in range(len(by_row)):
        row_load(k, 0).start()
    load(1).start()
    load(2).start()
    for row in range(1, rows):
        for k in range(len(by_row)):
            row_load(k, row).start()
    for k in range(3, 8):
        load(k).start()

    if remote:
        rooms = [refs[5 * g : 5 * g + 5] for g in range(4)]
        sums, s_land, s_far, send, recv, own_sem, s_send, s_recv = refs[20:]
        depth = rooms[0][0].shape[0]
        place = Place(depth)
        own = [
            pltpu.make_async_copy(source.at[:, :, place.core], room[0], own_sem.at[g])
            for g, (source, room) in enumerate(zip(sources, rooms))
        ]
        up, qkv = [
            Scatter(place, source.at[:, :, 1 - place.core], room, send, recv, g)
            for g, (source, room) in enumerate(zip(sources, rooms))
        ]
        late, early = [
            Scatter(place, room[0].at[1], (room[0].at[0],) + tuple(room[1:]), send, recv, 2 + g)
            for g, room in enumerate(rooms[2:])
        ]
        for copy in own:
            copy.start()
        meet(place)
        up.start(0)
        qkv.start(0)

    norms[...] = jnp.zeros_like(norms)
    edge_sums[...] = jnp.zeros_like(edge_sums)
    flat = lambda ref: ref[...].reshape(rows * tokens, width)

    def weight_grad(dest, col, left, right):
        half = width // 2
        for part in range(2):
            grad = tn(left[:, :, part * half : (part + 1) * half].reshape(rows * tokens, half), flat(right))
            if not remote:
                dest[part * half : (part + 1) * half, col * width : (col + 1) * width] = grad.astype(LOW)
                continue
            share = dest.shape[4]
            for k in range(half // share):
                index = part * (half // share) + k
                z, y, core, x_at = index // 8, index // 4 % 2, index // 2 % 2, index % 2
                side = place.core if core == 0 else 1 - place.core
                dest[side, z, y, x_at, :, col * width : (col + 1) * width] = grad[k * share : (k + 1) * share].astype(LOW)

    def spread(row, source):
        back[...] = jnp.zeros_like(back)
        for b in range(blocks):
            back[b * BLOCK : b * BLOCK + WIDE, :] += nn(adj[row, b], source[row, b * BLOCK : (b + 1) * BLOCK, :])

    load(0).wait()
    load(1).wait()
    load(2).wait()

    @pl.loop(0, rows)
    def _(row):
        for k in range(len(by_row)):
            row_load(k, row).wait()
        for c in range(chunks):
            part = slice(c * chunk, (c + 1) * chunk)
            grad = two[row, part, :]
            for k, ref in enumerate((dq, dk, dv)):
                grad = grad + nt(ref[row, part, :], qkv_w[:, k * width : (k + 1) * width])
            plain = unit[row, part, :].astype(F32)
            norms[0] += fold(grad * plain)
            norms[1] += fold(grad)
            grad = norm_back(grad, plain, rstd[row, part, :], gain_ref[0:1, :])
            one[row, part, :] = grad
            low = grad.astype(LOW)
            branch[row, part, :] = low
            mean[row, part, :] = (nt(low, second_w[:, width : 2 * width]) * cols[row, part, 2:3]).astype(LOW)
        if remote:
            @pl.when(row == 0)
            def _():
                own[0].wait()
                up.fold(0)

    if remote:
        own[1].wait()
        qkv.fold(0)
    load(3).wait()
    load(4).wait()
    second_dest, first_dest = (rooms[2][0], rooms[3][0]) if remote else (owned[1], owned[0])
    weight_grad(second_dest, 0, hidden, branch)
    weight_grad(second_dest, 1, agg2, branch)
    load(8).start()
    load(9).start()
    if remote:
        late.start(0)
        up.fold(1)
    for k in range(5, 8):
        load(k).wait()

    @pl.loop(0, rows)
    def _(row):
        spread(row, mean)
        for c in range(chunks):
            part = slice(c * chunk, (c + 1) * chunk)
            grad = back[REACH + c * chunk : REACH + (c + 1) * chunk, :]
            grad = grad + nt(branch[row, part, :], second_w[:, 0:width])
            grad = grad * slope[row, part, :].astype(F32)
            edge_sums[0] += fold(grad * cols[row, part, 0:1])
            edge_sums[1] += fold(grad * cols[row, part, 1:2])
            low = grad.astype(LOW)
            pre[row, part, :] = low
            mean[row, part, :] = (nt(low, first_w[:, width : 2 * width]) * cols[row, part, 2:3]).astype(LOW)
        if remote:
            @pl.when(row == 0)
            def _():
                late.fold(0)
                qkv.fold(1)

    if remote:
        up.fold(2)
    load(8).wait()
    load(9).wait()
    weight_grad(first_dest, 0, x, pre)
    weight_grad(first_dest, 1, agg1, pre)

    line = lambda v: jnp.sum(v, axis=0, keepdims=True)
    lines = jnp.concatenate(
        [line(edge_sums[0]), line(edge_sums[1]), line(norms[0]), line(late_ref[0]), line(late_ref[2]),
         line(norms[1]), line(late_ref[1]), line(late_ref[3])], axis=0,
    )
    rates = jnp.sum(jnp.sum(rate_ref[...], axis=0), axis=2).reshape(-1, BLOCK)

    if remote:
        early.start(0)
        pieces = width // BLOCK
        for k in range(pieces):
            sums[0, k] = lines[:, k * BLOCK : (k + 1) * BLOCK]
        for k in range(3):
            sums[0, pieces + k] = rates[8 * k : 8 * (k + 1)]
        turns = [
            (sums.at[k], s_land.at[k], k, device)
            for k, device in enumerate((
                place.at(place.z, place.y, 1 - place.core, place.x),
                place.at(place.z, place.y, place.core, 1 - place.x),
                place.at(place.z, 1 - place.y, place.core, place.x),
            ))
        ] + [
            (s_far.at[place.z], s_far.at[place.z], 2 + k, place.at(place.along(k), place.y, place.core, place.x))
            for k in range(1, depth)
        ]
        turns = [
            pltpu.make_async_remote_copy(
                src_ref=source, dst_ref=land, send_sem=s_send.at[slot], recv_sem=s_recv.at[slot],
                device_id=device, device_id_type=pl.DeviceIdType.MESH,
            )
            for source, land, slot, device in turns
        ]
        turns[0].start()
        qkv.fold(2)
        late.fold(1)

    writes = lambda row: pltpu.make_async_copy(one.at[row], input_grad_out.at[row], out_sem.at[row])

    @pl.loop(0, rows)
    def _(row):
        spread(row, mean)
        for c in range(chunks):
            part = slice(c * chunk, (c + 1) * chunk)
            grad = one[row, part, :] + back[REACH + c * chunk : REACH + (c + 1) * chunk, :]
            one[row, part, :] = grad + nt(pre[row, part, :], first_w[:, 0:width])
        writes(row).start()
        if remote:
            @pl.when(row == 0)
            def _():
                early.fold(0)
                turns[0].wait_recv()
                sums[1] = sums[0] + s_land[0]
                turns[1].start()

    if remote:
        turns[1].wait_recv()
        sums[2] = sums[1] + s_land[1]
        turns[2].start()
        late.fold(2)
        early.fold(1)
        turns[2].wait_recv()
        s_far[place.z] = sums[2] + s_land[2]
        for turn in turns[3:]:
            turn.start()
        owned[4][...] = up.finish()
        owned[5][...] = qkv.finish()
        early.fold(2)
        result = late.finish()
        owned[2][...] = result[:, :width]
        owned[3][...] = result[:, width:]
        for turn in turns[3:]:
            turn.wait_recv()
        total = s_far[0]
        for k in range(1, depth):
            total = total + s_far[k]
        for k in range(pieces):
            part = slice(k * BLOCK, (k + 1) * BLOCK)
            edge_out[:, part] = total[k, 0:2]
            gains_out[:, part] = total[k, 2:5]
            shifts_out[:, part] = total[k, 5:8]
        for k in range(3):
            rates_out[8 * k : 8 * (k + 1)] = jnp.sum(total[pieces + k], axis=1, keepdims=True)
        result = early.finish()
        owned[0][...] = result[:, :width]
        owned[1][...] = result[:, width:]
        for group in (up, qkv, late, early):
            group.sent()
        for turn in turns:
            turn.wait_send()
    else:
        edge_out[...], gains_out[...], shifts_out[...] = lines[0:2], lines[2:5], lines[5:8]
        rates_out[...] = jnp.sum(rates, axis=1, keepdims=True)
    for row in range(rows):
        writes(row).wait()


def graph_backward(remote, depth, arrays, gains, late, rates, sources):
    dq, two, unit, rstd, slope, hidden, adj, cols = (arrays[k] for k in (0, 3, 4, 5, 6, 7, 11, 12))
    rows, tokens, width = dq.shape
    vmem, hbm = pl.BlockSpec(memory_space=pltpu.VMEM), pl.BlockSpec(memory_space=pl.ANY)
    shape = lambda dtype, *dims: jax.ShapeDtypeStruct(dims, dtype)
    out_shape = [
        shape(F32, rows, tokens, width), shape(F32, 2, width), shape(F32, 3, width), shape(F32, 3, width),
        shape(F32, rates.shape[1] * 4, 1),
    ]
    like = lambda v: pltpu.VMEM(v.shape, v.dtype)
    scratch = [like(v) for v in (dq, dq, dq, two, unit, rstd, slope, hidden, hidden, adj, cols) + tuple(arrays[13:16])]
    scratch += [
        pltpu.VMEM((tokens + 2 * REACH, width), F32),
        pltpu.VMEM((2, 8, width), F32),
        pltpu.VMEM((2, 8, width), F32),
        pltpu.SemaphoreType.DMA((6, rows)),
        pltpu.SemaphoreType.DMA((10,)),
        pltpu.SemaphoreType.DMA((rows,)),
    ]
    more = {}
    if remote:
        share = sources[0].shape[4]
        out_shape += [shape(F32, share, width)] * 4 + [shape(F32, share, s.shape[5]) for s in sources]
        for source in sources:
            scratch += scatter_room(depth, share, source.shape[5])
        for _ in range(2):
            scratch += scatter_room(depth, share, 2 * width, (2,))
        lines = (width // BLOCK + 3, 8, BLOCK)
        scratch += [pltpu.VMEM((3,) + lines, F32), pltpu.VMEM((3,) + lines, F32), pltpu.VMEM((depth,) + lines, F32)]
        scratch += [pltpu.SemaphoreType.DMA((4, depth + 3))] * 2 + [pltpu.SemaphoreType.DMA((2,))]
        scratch += [pltpu.SemaphoreType.DMA((depth + 2,))] * 2
        more = {"collective_id": CALLS["graph"], "has_side_effects": True}
    else:
        out_shape += [shape(LOW, width, 2 * width)] * 2
    return pl.pallas_call(
        functools.partial(graph_back_kernel, remote),
        in_specs=[hbm] * 16 + [vmem] * 3 + [hbm] * (2 if remote else 0),
        out_specs=[hbm] + [vmem] * (len(out_shape) - 1),
        out_shape=out_shape,
        scratch_shapes=scratch,
        compiler_params=pltpu.CompilerParams(vmem_limit_bytes=VMEM, **more),
        name="graph_backward",
    )(*arrays, gains, late, rates, *(sources if remote else ()))


def local(
    sizes, inputs, coords, neighbours, counts, doc_length, self_one, near_one, self_two, near_two, edge_proj,
    qkv_proj, out_proj, up_proj, down_proj, norm_gains, norm_shifts, distance_rate, order_rate, cotangent,
):
    axes = ("wide", "narrow")
    rows, tokens, width = inputs.shape
    wide_size, narrow_size = sizes
    depth = wide_size // 4
    remote = wide_size % 4 == 0 and narrow_size == 2 and self_one.shape[0] % 8 == 0
    weights, shards = (self_one, near_one, self_two, near_two, qkv_proj), (out_proj, up_proj, down_proj)
    gather = lambda v: lax.all_gather(v, axes, axis=0, tiled=True)
    scatter = lambda v: lax.psum_scatter(v, axes, scatter_dimension=0, tiled=True).astype(F32)
    blocked = lambda v: v.reshape(depth, 2, 2, 2, -1, v.shape[1])
    flat = lambda v: v.reshape(rows * tokens, width)
    tall = lambda v: v.reshape(rows, tokens, width)
    if not remote:
        weights, shards = tuple(map(gather, weights)), tuple(map(gather, shards))
    results = front(
        remote, depth, doc_length[:, 0], distance_rate, order_rate, neighbours, counts[:, None, :], coords, inputs,
        edge_proj, norm_gains, norm_shifts, weights, shards if remote else (),
    )
    (adj, cols, agg1, slope, hidden, agg2, unit, rstd, normed, low, qkv, att, probs, far, order, first_w, second_w, qkv_w) = results[:18]
    out_w, up, down = (v.reshape(-1, v.shape[-1]) for v in results[18:]) if remote else shards
    result, two, grad_att, grad_out, grad_up, grad_down, late = block_both(
        att.reshape(-1, rows * tokens, BLOCK), flat(normed), flat(cotangent), out_w, up, down, norm_gains, norm_shifts
    )
    first_sources = (blocked(grad_down), blocked(grad_out)) if remote else ()
    dq, dk, dv, rates, grad_qkv, *first_owned = attention_backward(
        remote, depth, qkv, tall(grad_att), probs, far, order, low, first_sources
    )
    arrays = (dq, dk, dv, tall(two), unit, rstd, slope, hidden, agg2, agg1, inputs, adj, cols, first_w, second_w, qkv_w)
    sources = (blocked(grad_up), blocked(grad_qkv)) if remote else ()
    input_grad, edge, gains, shifts, rates, *owned = graph_backward(remote, depth, arrays, norm_gains, late, rates, sources)
    if remote:
        down_own, out_own = first_owned
        self1, near1, self2, near2, up_own, qkv_own = owned
    else:
        down_own, out_own, up_own, qkv_own = map(scatter, (grad_down, grad_out, grad_up, grad_qkv))
        self1, near1 = jnp.split(scatter(owned[0]), 2, axis=1)
        self2, near2 = jnp.split(scatter(owned[1]), 2, axis=1)
        edge, gains, shifts, rates = lax.psum((edge, gains, shifts, rates), axes)
    rates = rates.reshape(-1, 2, 2)
    return (
        tall(result), input_grad, self1, near1, self2, near2, edge, qkv_own, out_own, up_own, down_own, gains, shifts,
        rates[:, :, 0].reshape(-1), rates[:, :, 1].reshape(-1),
    )


def solution(mesh):
    axes = ("wide", "narrow")
    middle, last = P(None, axes, None), P(None, None, axes)
    count, weight, same = P(None, axes), P(axes, None), P()
    sizes = (mesh.shape["wide"], mesh.shape["narrow"])
    return jax.shard_map(
        functools.partial(local, sizes),
        mesh=mesh,
        in_specs=(middle, last, last, count, count)
        + (weight,) * 4
        + (same,)
        + (weight,) * 4
        + (same,) * 4
        + (middle,),
        out_specs=(middle, middle) + (weight,) * 4 + (same,) + (weight,) * 4 + (same,) * 4,
        check_vma=False,
    )
```

```python
import functools
import jax
import jax.numpy as jnp
from jax import lax
from jax.experimental import pallas as pl
from jax.experimental.pallas import tpu as pltpu
from jax.sharding import PartitionSpec as P

RADIUS = 128
REACH = 64
BLOCK = 128
WIDE = BLOCK + 2 * REACH
SPAN = BLOCK + 2 * RADIUS
FAR = 1e10
F32 = jnp.float32
LOW = jnp.bfloat16
VMEM = 62 * 2**20
CALLS = {"front": 0, "block": 1, "attention": 2, "graph": 3}


def dot(left, right, dims):
    return lax.dot_general(left, right, ((dims[:1], dims[1:]), ((), ())), preferred_element_type=F32)


def nn(left, right):
    return dot(left, right, (1, 0))


def nt(left, right):
    return dot(left, right, (1, 1))


def tn(left, right):
    return dot(left, right, (0, 0))


def gelu_pair(pre):
    slope = 0.7978845608028654
    square = pre * pre
    half = 0.5 + 0.5 * jnp.tanh(pre * (slope + (slope * 0.044715) * square))
    act = pre * half
    deriv = half + act * (1.0 - half) * (2.0 * slope + (6.0 * slope * 0.044715) * square)
    return act, deriv


def norm_parts(values):
    centre = values - jnp.mean(values, axis=-1, keepdims=True)
    rstd = lax.rsqrt(jnp.mean(centre * centre, axis=-1, keepdims=True) + 1e-05)
    return centre * rstd, rstd


def norm_back(grad, unit, rstd, gain):
    scaled = grad * gain
    mean = jnp.mean(scaled, axis=-1, keepdims=True)
    along = jnp.mean(scaled * unit, axis=-1, keepdims=True)
    return rstd * (scaled - mean - unit * along)


def fold(values):
    rows, cols = values.shape
    return jnp.sum(values.reshape(rows // 8, 8, cols), axis=0)


def whole(shape, space=None):
    return pl.BlockSpec(shape, lambda *_: (0,) * len(shape), pipeline_mode=pl.Buffered(1))


def params(grid_rank, **more):
    return pltpu.CompilerParams(
        vmem_limit_bytes=VMEM, dimension_semantics=("arbitrary",) * grid_rank, **more
    )


def fill_bias(length, point_ref, far_ref, order_ref, row):
    tokens = point_ref.shape[2]
    side = jnp.zeros((2, RADIUS), F32)
    padded = jnp.concatenate([side, point_ref[row], side], axis=1)
    tall = jnp.concatenate([padded, jnp.zeros((6, tokens + 2 * RADIUS), F32)], axis=0)
    for b in range(tokens // BLOCK):
        window = tall[:, b * BLOCK : b * BLOCK + SPAN].T
        key_x, key_y = window[:, 0:1], window[:, 1:2]
        lanes = slice(b * BLOCK, (b + 1) * BLOCK)
        delta_x = key_x - point_ref[row, 0:1, lanes]
        delta_y = key_y - point_ref[row, 1:2, lanes]
        dist = jnp.log(1.0 + 16.0 * (delta_x * delta_x + delta_y * delta_y))
        query = lax.broadcasted_iota(jnp.int32, (SPAN, BLOCK), 1) + b * BLOCK
        key = lax.broadcasted_iota(jnp.int32, (SPAN, BLOCK), 0) + (b * BLOCK - RADIUS)
        allowed = (jnp.abs(query - key) <= RADIUS) & ((query >= length) == (key >= length))
        allowed = allowed & (key >= 0) & (key < tokens)
        far_ref[row, b] = jnp.where(allowed, dist, FAR)
        order_ref[row, b] = jnp.tanh(4.0 * delta_x)


def pair_rows(values):
    lane = lax.broadcasted_iota(jnp.int32, values.shape, 1)
    zero = jnp.zeros_like(values)
    first = jnp.where(lane < BLOCK // 2, values, zero)
    second = jnp.where(lane < BLOCK // 2, zero, values)
    return jnp.concatenate([first, second], axis=0)


def pair_pick(values):
    lane = lax.broadcasted_iota(jnp.int32, (BLOCK, BLOCK), 1)
    return jnp.where(lane < BLOCK // 2, values[:BLOCK], values[BLOCK:])


def pad_rows(pad_ref, values):
    tokens = values.shape[0]
    zeros = jnp.zeros((RADIUS, values.shape[1]), pad_ref.dtype)
    pad_ref[pl.ds(0, RADIUS), :] = zeros
    pad_ref[pl.ds(RADIUS + tokens, RADIUS), :] = zeros
    pad_ref[pl.ds(RADIUS, tokens), :] = values


FIRST, OWN, PASSED, SIBLING = 0, 1, 2, 3


class Place:
    def __init__(self, depth):
        self.depth = depth
        wide, self.x = lax.axis_index("wide"), lax.axis_index("narrow")
        self.core = lax.rem(wide, 2)
        self.y = lax.rem(lax.div(wide, 2), 2)
        self.z = lax.div(wide, 4)
        core, y, x = self.core, self.y, self.x
        self.first_y = (1 - core) * (1 - y) + core * y
        self.first_x = core * (1 - x) + (1 - core) * x
        self.second_y = core * (1 - y) + (1 - core) * y
        self.second_x = (1 - core) * (1 - x) + core * x

    def at(self, z, y, core, x):
        return ((z * 2 + y) * 2 + core, x)

    def along(self, k):
        return lax.rem(self.z + k, self.depth)

    def partners(self):
        along = [self.at(self.along(k), self.y, self.core, self.x) for k in range(1, self.depth)]
        return along + [
            self.at(self.z, self.first_y, self.core, self.first_x),
            self.at(self.z, self.second_y, self.core, self.second_x),
            self.at(self.z, self.y, 1 - self.core, self.x),
        ]


def meet(place):
    barrier = pltpu.get_barrier_semaphore()
    partners = place.partners()
    for partner in partners:
        pl.semaphore_signal(barrier, inc=1, device_id=partner, device_id_type=pl.DeviceIdType.MESH)
    pl.semaphore_wait(barrier, len(partners))


class Gather:
    def __init__(self, place, land, send, recv, group):
        self.place, self.land, self.send, self.recv, self.group = place, land, send, recv, group

    def copy(self, view, slot, device):
        return pltpu.make_async_remote_copy(
            src_ref=view, dst_ref=view, send_sem=self.send.at[self.group, slot], recv_sem=self.recv.at[self.group, slot],
            device_id=device, device_id_type=pl.DeviceIdType.MESH,
        )

    def pieces(self, stage):
        p, land = self.place, self.land
        base = p.depth - 1
        mine = land.at[:, p.y, p.core, p.x]
        if stage == "along":
            here = land.at[p.z, p.y, p.core, p.x]
            found = []
            for k in range(1, p.depth):
                there = land.at[p.along(p.depth - k), p.y, p.core, p.x]
                found.append((here, there, k - 1, p.at(p.along(k), p.y, p.core, p.x)))
            return found
        first = p.at(p.z, p.first_y, p.core, p.first_x)
        second = p.at(p.z, p.second_y, p.core, p.second_x)
        if stage == FIRST:
            return [(mine, land.at[:, p.first_y, p.core, p.first_x], base, first)]
        if stage == OWN:
            return [(mine, land.at[:, p.second_y, p.core, p.second_x], base + 1, second)]
        if stage == PASSED:
            return [(land.at[:, p.first_y, p.core, p.first_x], land.at[:, 1 - p.y, p.core, 1 - p.x], base + 2, second)]
        return [(land.at[:, :, p.core], land.at[:, :, 1 - p.core], base + 3, p.at(p.z, p.y, 1 - p.core, p.x))]

    def start(self, *stages):
        for stage in stages:
            for leaves, _, slot, device in self.pieces(stage):
                self.copy(leaves, slot, device).start()

    def arrive(self, *stages):
        for stage in stages:
            for _, arrives, slot, device in self.pieces(stage):
                self.copy(arrives, slot, device).wait_recv()

    def sent(self, *stages):
        for stage in stages or ("along", FIRST, OWN, PASSED, SIBLING):
            for leaves, _, slot, device in self.pieces(stage):
                self.copy(leaves, slot, device).wait_send()


def merge_rows(full, land):
    depth, rows = land.shape[0], land.shape[4]

    @pl.loop(0, depth * 4)
    def _(k):
        z, y, core = lax.div(k, 4), lax.rem(lax.div(k, 2), 2), lax.rem(k, 2)
        pair = jnp.concatenate([land[z, y, core, 0].astype(F32), land[z, y, core, 1].astype(F32)], axis=0)
        full[pl.ds(pl.multiple_of(k * 2 * rows, 16), 2 * rows), :] = pair.astype(LOW)


def front_kernel(remote, *refs):
    (length_ref, dist_rate_ref, order_rate_ref, near_ref, count_ref, point_ref, x_ref, edge_w_ref, gain_ref, shift_ref,
     self1_ref, near1_ref, self2_ref, near2_ref, qkv_w_ref) = refs[:15]
    refs = refs[15:]
    shards, refs = (refs[:3], refs[3:]) if remote else ((), refs)
    outs, refs = refs[:18], refs[18:]
    fulls, refs = (refs[:3], refs[3:]) if remote else ((), refs)
    (adj, cols, agg1, slope, hidden, agg2, unit, rstd, normed, low, qkv, att, probs, far, order,
     first_w, second_w, third_w, pad, point_pad, rel, keys, values, out_sem, probs_sem, in_sem) = refs[:26]
    rows, slots, tokens = near_ref.shape
    width = x_ref.shape[2]
    pairs = width // BLOCK
    blocks = tokens // BLOCK
    chunk = 2 * BLOCK

    writes = {}

    def write(k, source, dest=None):
        writes[k] = pltpu.make_async_copy(source, outs[k] if dest is None else dest, out_sem.at[k])
        writes[k].start()

    if remote:
        land_a, land_b, land_q, send, recv = refs[26:]
        place = Place(land_a.shape[0])
        lands = (land_a, land_b, land_q) + tuple(fulls)
        groups = [Gather(place, land, send, recv, g) for g, land in enumerate(lands)]
        ga, gb, gq, go, gu, gd = groups
        column = lambda land, k: land.at[place.z, place.y, place.core, place.x, :, pl.ds(k * width, width)]
        own = lambda land: land.at[place.z, place.y, place.core, place.x]
        loads = [
            [pltpu.make_async_copy(ref, column(land_a, k), in_sem.at[k]) for k, ref in enumerate((self1_ref, near1_ref))],
            [pltpu.make_async_copy(ref, column(land_b, k), in_sem.at[2 + k]) for k, ref in enumerate((self2_ref, near2_ref))],
            [pltpu.make_async_copy(qkv_w_ref, own(land_q), in_sem.at[4])],
        ] + [[pltpu.make_async_copy(ref, own(full), in_sem.at[5 + k])] for k, (ref, full) in enumerate(zip(shards, fulls))]
        for load in loads:
            for copy in load:
                copy.start()
        meet(place)

        def begin(g):
            for copy in loads[g]:
                copy.wait()
            groups[g].start("along")

        begin(0)
    else:
        loads = [
            pltpu.make_async_copy(ref, dest, in_sem.at[k])
            for k, (ref, dest) in enumerate((
                (self1_ref, first_w.at[:, pl.ds(0, width)]), (near1_ref, first_w.at[:, pl.ds(width, width)]),
                (self2_ref, second_w.at[:, pl.ds(0, width)]), (near2_ref, second_w.at[:, pl.ds(width, width)]),
                (qkv_w_ref, third_w),
            ))
        ]
        for copy in loads:
            copy.start()

    side = jnp.zeros((REACH, width), LOW)
    pad[pl.ds(0, REACH), :] = side
    pad[pl.ds(tokens + REACH, REACH), :] = side

    @pl.loop(0, rows)
    def _(row):
        length = length_ref[row]
        pad[pl.ds(REACH, tokens), :] = x_ref[row]
        points = point_ref[row]
        high = points.astype(LOW).astype(F32)
        mid = (points - high).astype(LOW).astype(F32)
        tail = points - high - mid
        split = jnp.concatenate([high, mid, tail, jnp.ones((1, tokens), F32), jnp.zeros((9, tokens), F32)], axis=0)
        edge_side = jnp.zeros((16, REACH), F32)
        point_pad[...] = jnp.concatenate([edge_side, split, edge_side], axis=1).astype(LOW)

        @pl.loop(0, blocks)
        def _(b):
            start = pl.multiple_of(b * BLOCK, BLOCK)
            lanes = pl.ds(start, BLOCK)
            near = near_ref[row, :, lanes]
            count = count_ref[row, :, lanes]
            spot = lax.broadcasted_iota(jnp.int32, (1, BLOCK), 1) + start
            slot = lax.broadcasted_iota(jnp.int32, (slots, BLOCK), 0)
            same = (near >= length) == (spot >= length)
            rel[...] = jnp.where((slot < count) & same, near - (start - REACH), -1)
            target = lax.broadcasted_iota(jnp.int32, (WIDE, BLOCK), 0)
            total = jnp.zeros((WIDE, BLOCK), F32)
            for s in range(slots):
                total = total + jnp.where(rel[s : s + 1, :] == target, 1.0, 0.0)
            band = total.astype(LOW)
            adj[row, b] = band
            sums = nn(point_pad[:, pl.ds(start, WIDE)], band)
            inverse = 1.0 / count.astype(F32)
            here = point_ref[row, :, lanes]
            edge = (sums[0:2] + sums[2:4] + sums[4:6] - sums[6:7] * here) * inverse
            lines = jnp.concatenate([edge, inverse, jnp.zeros((5, BLOCK), F32)], axis=0).T
            cols[row, lanes, :] = lines
            agg = tn(band, pad[pl.ds(start, WIDE), :])
            agg1[row, lanes, :] = (agg * lines[:, 2:3]).astype(LOW)

        if remote:
            @pl.when(row == 0)
            def _():
                ga.arrive("along")
                ga.start(FIRST, OWN)
                begin(1)

    write(0, adj)
    write(1, cols)
    write(2, agg1)
    if remote:
        ga.arrive(FIRST)
        ga.start(PASSED)
        gb.arrive("along")
        gb.start(FIRST, OWN)
        begin(2)

    @pl.loop(0, rows)
    def _(row):
        fill_bias(length_ref[row], point_ref, far, order, row)

    write(13, far)
    write(14, order)
    if remote:
        ga.arrive(OWN, PASSED)
        ga.start(SIBLING)
        gb.arrive(FIRST)
        gb.start(PASSED)
        ga.arrive(SIBLING)
        merge_rows(first_w, land_a)
    else:
        for copy in loads:
            copy.wait()
        write(16, second_w)
        write(17, third_w)
    write(15, first_w)

    @pl.loop(0, rows)
    def _(row):
        for c in range(tokens // chunk):
            part = slice(c * chunk, (c + 1) * chunk)
            pre = nn(x_ref[row, part, :], first_w[:, 0:width])
            pre = pre + nn(agg1[row, part, :], first_w[:, width : 2 * width])
            pre = pre + cols[row, part, 0:1] * edge_w_ref[0:1, :] + cols[row, part, 1:2] * edge_w_ref[1:2, :]
            act, deriv = gelu_pair(pre)
            slope[row, part, :] = deriv.astype(LOW)
            hidden[row, part, :] = act.astype(LOW)
            pad[REACH + c * chunk : REACH + (c + 1) * chunk, :] = act.astype(LOW)
        for b in range(blocks):
            lanes = slice(b * BLOCK, (b + 1) * BLOCK)
            agg = tn(adj[row, b], pad[b * BLOCK : b * BLOCK + WIDE, :])
            agg2[row, lanes, :] = (agg * cols[row, lanes, 2:3]).astype(LOW)
        if remote:
            @pl.when(row == 0)
            def _():
                gb.arrive(OWN, PASSED)
                gb.start(SIBLING)
                gq.arrive("along")
                gq.start(FIRST, OWN)
                begin(3)
                begin(4)

    write(3, slope)
    write(4, hidden)
    write(5, agg2)
    if remote:
        gb.arrive(SIBLING)
        merge_rows(second_w, land_b)
        write(16, second_w)

    @pl.loop(0, rows)
    def _(row):
        for c in range(tokens // chunk):
            part = slice(c * chunk, (c + 1) * chunk)
            resid = x_ref[row, part, :].astype(F32) + nn(hidden[row, part, :], second_w[:, 0:width])
            resid = resid + nn(agg2[row, part, :], second_w[:, width : 2 * width])
            plain, scale = norm_parts(resid)
            unit[row, part, :] = plain.astype(LOW)
            rstd[row, part, :] = scale
            out = plain * gain_ref[0:1, :] + shift_ref[0:1, :]
            normed[row, part, :] = out
            low[row, part, :] = out.astype(LOW)
        if remote:
            @pl.when(row == 0)
            def _():
                gq.arrive(FIRST)
                gq.start(PASSED)
                for g in (go, gu):
                    g.arrive("along")
                    g.start(FIRST, OWN)
                begin(5)

    write(6, unit)
    write(7, rstd)
    write(8, normed)
    write(9, low)
    if remote:
        gq.arrive(OWN, PASSED)
        gq.start(SIBLING)
        gq.arrive(SIBLING)
        merge_rows(third_w, land_q)
        write(17, third_w)

    @pl.loop(0, rows)
    def _(row):
        for c in range(tokens // chunk):
            part = slice(c * chunk, (c + 1) * chunk)
            out = nn(low[row, part, :], third_w[...]).astype(LOW)
            for k in range(3 * pairs):
                qkv[k, row, part, :] = out[:, k * BLOCK : (k + 1) * BLOCK]

    write(10, qkv)
    zeros = jnp.zeros((RADIUS, BLOCK), LOW)
    for ref in (keys, values):
        ref[pl.ds(0, RADIUS), :] = zeros
        ref[pl.ds(RADIUS + tokens, RADIUS), :] = zeros

    @pl.loop(0, rows * pairs)
    def _(turn):
        row, pair, slot = lax.div(turn, pairs), lax.rem(turn, pairs), lax.rem(turn, 2)
        if remote:
            @pl.when(turn == 1)
            def _():
                for g in (go, gu):
                    g.arrive(FIRST)
                    g.start(PASSED)
                gd.arrive("along")
                gd.start(FIRST, OWN)

            @pl.when(turn == 6)
            def _():
                for g in (go, gu):
                    g.arrive(OWN, PASSED)
                    g.start(SIBLING)

        def probs_copy(t, s):
            return pltpu.make_async_copy(
                probs.at[s], outs[12].at[lax.div(t, pairs), lax.rem(t, pairs)], probs_sem.at[s]
            )

        @pl.when(turn >= 2)
        def _():
            probs_copy(turn - 2, slot).wait()

        keys[pl.ds(RADIUS, tokens), :] = qkv[pairs + pair, row]
        values[pl.ds(RADIUS, tokens), :] = qkv[2 * pairs + pair, row]
        for b in range(blocks):
            lanes = slice(b * BLOCK, (b + 1) * BLOCK)
            window = slice(b * BLOCK, b * BLOCK + SPAN)
            queries = pair_rows(qkv[pair, row, lanes, :] * 0.125)
            raw = nt(keys[window, :], queries)
            sides = []
            for h in range(2):
                bias = order_rate_ref[2 * pair + h] * order[row, b] - dist_rate_ref[2 * pair + h] * far[row, b]
                scores = raw[:, h * BLOCK : (h + 1) * BLOCK] + bias
                grown = jnp.exp(scores - jnp.max(scores, axis=0, keepdims=True))
                scale = 1.0 / jnp.sum(grown, axis=0, keepdims=True)
                sides.append((grown * scale).astype(LOW))
            both = jnp.concatenate(sides, axis=1)
            probs[slot, b] = both
            att[pair, row, lanes, :] = pair_pick(tn(both, values[window, :])).astype(LOW)
        probs_copy(turn, slot).start()

    last = rows * pairs
    for turn in (last - 2, last - 1):
        pltpu.make_async_copy(probs.at[turn % 2], outs[12].at[turn // pairs, turn % pairs], probs_sem.at[turn % 2]).wait()
    write(11, att)
    if remote:
        for g in (go, gu):
            g.arrive(SIBLING)
        gd.arrive(FIRST, OWN)
        for g in groups[:5]:
            g.sent()
        gd.sent("along", FIRST, OWN)
    for copy in writes.values():
        copy.wait()


def front(remote, depth, length, dist_rate, order_rate, near, count, point, x, edge_w, gains, shifts, weights, shards):
    rows, tokens, width = x.shape
    slots = near.shape[1]
    blocks, pairs = tokens // BLOCK, width // BLOCK
    smem, vmem, hbm = (pl.BlockSpec(memory_space=s) for s in (pltpu.SMEM, pltpu.VMEM, pl.ANY))
    each = lambda dtype, *shape: ((rows,) + shape, dtype)
    kept = [
        each(LOW, blocks, WIDE, BLOCK),
        each(F32, tokens, 8),
        each(LOW, tokens, width),
        each(LOW, tokens, width),
        each(LOW, tokens, width),
        each(LOW, tokens, width),
        each(LOW, tokens, width),
        each(F32, tokens, 1),
        each(F32, tokens, width),
        each(LOW, tokens, width),
        ((3 * pairs, rows, tokens, BLOCK), LOW),
        ((pairs, rows, tokens, BLOCK), LOW),
        each(LOW, pairs, blocks, SPAN, 2 * BLOCK),
        each(F32, blocks, SPAN, BLOCK),
        each(F32, blocks, SPAN, BLOCK),
        ((width, 2 * width), LOW),
        ((width, 2 * width), LOW),
        ((width, 3 * width), LOW),
    ]
    out_shape = [jax.ShapeDtypeStruct(*k) for k in kept]
    kept[12] = ((2, blocks, SPAN, 2 * BLOCK), LOW)
    scratch = [pltpu.VMEM(*k) for k in kept]
    scratch += [
        pltpu.VMEM((tokens + 2 * REACH, width), LOW),
        pltpu.VMEM((16, tokens + 2 * REACH), LOW),
        pltpu.VMEM((slots, BLOCK), jnp.int32),
        pltpu.VMEM((tokens + 2 * RADIUS, BLOCK), LOW),
        pltpu.VMEM((tokens + 2 * RADIUS, BLOCK), LOW),
        pltpu.SemaphoreType.DMA((18,)),
        pltpu.SemaphoreType.DMA((2,)),
        pltpu.SemaphoreType.DMA((8,)),
    ]
    more = {}
    if remote:
        blocked = lambda shape: (depth, 2, 2, 2) + shape
        out_shape += [jax.ShapeDtypeStruct(blocked(s.shape), LOW) for s in shards]
        share = weights[0].shape[0]
        scratch += [pltpu.VMEM(blocked((share, k * width)), LOW) for k in (2, 2, 3)]
        scratch += [pltpu.SemaphoreType.DMA((6, depth + 3))] * 2
        more = {"collective_id": CALLS["front"], "has_side_effects": True}
    return pl.pallas_call(
        functools.partial(front_kernel, remote),
        in_specs=[smem] * 3 + [vmem] * 7 + [hbm] * (len(weights) + len(shards)),
        out_specs=[hbm] * len(out_shape),
        out_shape=out_shape,
        scratch_shapes=scratch,
        compiler_params=pltpu.CompilerParams(vmem_limit_bytes=VMEM, **more),
        name="front",
    )(length, dist_rate, order_rate, near, count, point, x, edge_w, gains, shifts, *weights, *shards)


TILE = 512


def block_kernel(remote, steps, *refs):
    (att_ref, normed_in, cot_ref, out_w_ref, up_ref, down_in, gain_ref, shift_ref,
     result_ref, two_out, grad_att_ref, grad_out_out, grad_up_ref, grad_down_ref, norms_ref,
     act_all, up_all, second_all, down_all, attn_all, normed_all, unit_all, rstd_all, down_w, in_sem, out_sem) = refs[:26]
    step = pl.program_id(0)
    turns, tokens, half = act_all.shape
    parts, piece = turns // 2, 2 * half
    width = normed_all.shape[1]
    load = pltpu.make_async_copy(normed_in, normed_all, in_sem.at[0])
    write_two = pltpu.make_async_copy(normed_all, two_out, out_sem.at[0])
    write_out = pltpu.make_async_copy(unit_all.at[pl.ds(0, width)], grad_out_out, out_sem.at[1])

    if remote:
        send, recv = refs[26:]
        place = Place(parts)
        mine, first, second, last = [
            down_w.at[:, y, place.core, x]
            for y, x in (
                (place.y, place.x), (place.first_y, place.first_x), (place.second_y, place.second_x), (1 - place.y, 1 - place.x)
            )
        ]
        loads = [
            pltpu.make_async_copy(down_in.at[:, y, place.core, x], view, in_sem.at[1 + k])
            for k, (y, x, view) in enumerate((
                (place.y, place.x, mine), (place.first_y, place.first_x, first), (place.second_y, place.second_x, second)
            ))
        ]

        def copy(view, slot, device):
            return pltpu.make_async_remote_copy(
                src_ref=view, dst_ref=view, send_sem=send.at[slot], recv_sem=recv.at[slot],
                device_id=device, device_id_type=pl.DeviceIdType.MESH,
            )

        partner = place.at(place.z, place.second_y, place.core, place.second_x)
        sibling = place.at(place.z, place.y, 1 - place.core, place.x)
        pass_on, arriving = copy(first, 4, partner), copy(last, 4, partner)
        across = [copy(view, k, sibling) for k, view in enumerate((mine, first, second, last))]
        theirs = [
            copy(down_w.at[:, y, 1 - place.core, x], k, sibling)
            for k, (y, x) in enumerate((
                (place.y, place.x), (place.second_y, place.second_x), (place.first_y, place.first_x), (1 - place.y, 1 - place.x)
            ))
        ]

        def begin():
            for item in loads:
                item.start()
            meet(place)
            loads[1].wait()
            pass_on.start()
            across[1].start()
            loads[0].wait()
            across[0].start()
            loads[2].wait()
            across[2].start()

        def finish():
            arriving.wait_recv()
            across[3].start()
            for item in theirs:
                item.wait_recv()
            for item in across:
                item.wait_send()
            pass_on.wait_send()
    else:
        full = pltpu.make_async_copy(down_in, down_w, in_sem.at[1])
        begin, finish = full.start, full.wait

    def put(ref, c, at, value):
        ref[2 * c, at, :], ref[2 * c + 1, at, :] = value[:, :half], value[:, half:]

    def get(ref, c, at):
        return jnp.concatenate([ref[2 * c, at, :], ref[2 * c + 1, at, :]], axis=1)

    def down_rows(c):
        return down_w[c].reshape(piece, width)

    @pl.when(step == 0)
    def _():
        load.start()
        norms_ref[...] = jnp.zeros_like(norms_ref)
        begin()
        load.wait()

    @pl.when(step < steps)
    def _():
        at = pl.ds(pl.multiple_of(step * TILE, TILE), TILE)
        att = jnp.concatenate([att_ref[k, at, :] for k in range(att_ref.shape[0])], axis=1)
        unit, rstd = norm_parts(normed_all[at, :] + nn(att, out_w_ref[...]))
        unit_all[at, :] = unit.astype(LOW)
        rstd_all[at, :] = rstd
        normed = unit * gain_ref[1:2, :] + shift_ref[1:2, :]
        normed_all[at, :] = normed
        second_all[at, :] = normed.astype(LOW)
        for c in range(parts):
            act, deriv = gelu_pair(nn(second_all[at, :], up_ref[:, c * piece : (c + 1) * piece]))
            put(act_all, c, at, act.astype(LOW))
            put(up_all, c, at, deriv.astype(LOW))

    @pl.when(step == steps)
    def _():
        finish()

    @pl.when((step >= steps) & (step < 2 * steps))
    def _():
        at = pl.ds(pl.multiple_of((step - steps) * TILE, TILE), TILE)
        resid = normed_all[at, :]
        for c in range(parts):
            resid = resid + nn(get(act_all, c, at), down_rows(c))
        unit, rstd = norm_parts(resid)
        result_ref[...] = (unit * gain_ref[2:3, :] + shift_ref[2:3, :]).astype(LOW)
        cot = cot_ref[...].astype(F32)
        norms_ref[2] += fold(cot * unit)
        norms_ref[3] += fold(cot)
        grad = norm_back(cot, unit, rstd, gain_ref[2:3, :])
        down_all[at, :] = grad.astype(LOW)
        for c in range(parts):
            up_low = (nt(down_all[at, :], down_rows(c)) * get(up_all, c, at).astype(F32)).astype(LOW)
            put(up_all, c, at, up_low)
            grad = grad + nt(up_low, up_ref[:, c * piece : (c + 1) * piece])
        unit = unit_all[at, :].astype(F32)
        norms_ref[0] += fold(grad * unit)
        norms_ref[1] += fold(grad)
        grad = norm_back(grad, unit, rstd_all[at, :], gain_ref[1:2, :])
        normed_all[at, :] = grad
        low = grad.astype(LOW)
        attn_all[at, :] = low
        grad_att_ref[...] = nt(low, out_w_ref[...]).astype(LOW)

    @pl.when(step == 2 * steps)
    def _():
        write_two.start()
        att = jnp.concatenate([att_ref[k] for k in range(att_ref.shape[0])], axis=1)
        unit_all[pl.ds(0, width), :] = tn(att, attn_all[...]).astype(LOW)
        write_out.start()

    @pl.when(step >= 2 * steps)
    def _():
        turn = step - 2 * steps
        grad_down_ref[...] = tn(act_all[turn], down_all[...]).astype(LOW)
        grad_up_ref[...] = tn(second_all[...], up_all[turn]).astype(LOW)

    @pl.when(step == 2 * steps + turns - 1)
    def _():
        write_two.wait()
        write_out.wait()


def block_both(remote, depth, att, normed, cot, out_w, up, down, gains, shifts):
    tokens, width = normed.shape
    wide = up.shape[1]
    steps = tokens // TILE
    parts = depth if remote else 4
    piece = wide // parts
    tile = pl.BlockSpec((TILE, width), lambda s: (jnp.clip(s - steps, 0, steps - 1), 0))
    late = lambda s: jnp.maximum(s - 2 * steps, 0)
    hbm = pl.BlockSpec(memory_space=pl.ANY)
    down = down if remote else down.reshape(parts, piece, width)
    more = {"collective_id": CALLS["block"], "has_side_effects": True} if remote else {}
    wide_low = pltpu.VMEM((2 * parts, tokens, piece // 2), LOW)
    tall_low = pltpu.VMEM((tokens, width), LOW)
    return pl.pallas_call(
        functools.partial(block_kernel, remote, steps),
        grid=(2 * steps + 2 * parts,),
        in_specs=[
            whole(att.shape), hbm, tile, whole((width, width)), whole(up.shape), hbm, whole(gains.shape), whole(shifts.shape),
        ],
        out_specs=[
            tile, hbm, tile, hbm,
            pl.BlockSpec((width, piece // 2), lambda s: (0, late(s))),
            pl.BlockSpec((piece // 2, width), lambda s: (late(s), 0)),
            pl.BlockSpec((4, 8, width), lambda s: (0, 0, 0)),
        ],
        out_shape=[
            jax.ShapeDtypeStruct((tokens, width), LOW),
            jax.ShapeDtypeStruct((tokens, width), F32),
            jax.ShapeDtypeStruct((tokens, width), LOW),
            jax.ShapeDtypeStruct((width, width), LOW),
            jax.ShapeDtypeStruct(up.shape, LOW),
            jax.ShapeDtypeStruct((wide, width), LOW),
            jax.ShapeDtypeStruct((4, 8, width), F32),
        ],
        scratch_shapes=[
            wide_low, wide_low, tall_low, tall_low, tall_low,
            pltpu.VMEM((tokens, width), F32),
            tall_low,
            pltpu.VMEM((tokens, 1), F32),
            pltpu.VMEM(down.shape, LOW),
            pltpu.SemaphoreType.DMA((4,)),
            pltpu.SemaphoreType.DMA((2,)),
        ]
        + ([pltpu.SemaphoreType.DMA((5,))] * 2 if remote else []),
        compiler_params=params(1, **more),
        name="block_both",
    )(att, normed, cot, out_w, up, down, gains, shifts)


class Scatter:
    def __init__(self, place, leaving, room, send, recv, group):
        self.place, self.leaving, self.send, self.recv, self.group = place, leaving, send, recv, group
        self.total, self.lands = room[0], room[1:]

    def copies(self, stage):
        p, total = self.place, self.total
        if stage == 0:
            found = [(self.leaving, self.lands[0], 0, p.at(p.z, p.y, 1 - p.core, p.x))]
        elif stage == 1:
            second = p.at(p.z, p.second_y, p.core, p.second_x)
            found = [
                (total.at[:, p.second_y, p.second_x], self.lands[1].at[0], 1, second),
                (total.at[:, 1 - p.y, 1 - p.x], self.lands[1].at[1], 2, second),
            ]
        elif stage == 2:
            first = p.at(p.z, p.first_y, p.core, p.first_x)
            found = [(total.at[:, p.first_y, p.first_x], self.lands[2], 3, first)]
        else:
            found = [
                (total.at[p.along(k), p.y, p.x], self.lands[3].at[k - 1], 3 + k, p.at(p.along(k), p.y, p.core, p.x))
                for k in range(1, p.depth)
            ]
        return [
            pltpu.make_async_remote_copy(
                src_ref=source, dst_ref=land, send_sem=self.send.at[self.group, slot],
                recv_sem=self.recv.at[self.group, slot], device_id=device, device_id_type=pl.DeviceIdType.MESH,
            )
            for source, land, slot, device in found
        ]

    def start(self, stage):
        for copy in self.copies(stage):
            copy.start()

    def arrive(self, stage):
        for copy in self.copies(stage):
            copy.wait_recv()

    def add(self, y, x, land):
        @pl.loop(0, self.place.depth)
        def _(z):
            self.total[z, y, x] = (self.total[z, y, x].astype(F32) + land(z).astype(F32)).astype(LOW)

    def fold(self, stage, go=True):
        p = self.place
        self.arrive(stage)
        if stage == 0:
            add = lambda y, x: self.add(y, x, lambda z: self.lands[0][z, y, x])
            add(p.second_y, p.second_x)
            add(1 - p.y, 1 - p.x)
            if go:
                self.start(1)
            add(p.first_y, p.first_x)
            add(p.y, p.x)
        elif stage == 1:
            self.add(p.first_y, p.first_x, lambda z: self.lands[1][1, z])
            if go:
                self.start(2)
            self.add(p.y, p.x, lambda z: self.lands[1][0, z])
        else:
            self.add(p.y, p.x, lambda z: self.lands[2][z])
            if go:
                self.start(3)

    def finish(self):
        p = self.place
        self.arrive(3)
        result = self.total[p.z, p.y, p.x].astype(F32)
        for k in range(p.depth - 1):
            result = result + self.lands[3][k].astype(F32)
        return result

    def sent(self, stages=4):
        for stage in range(stages):
            for copy in self.copies(stage):
                copy.wait_send()


class Tail:
    def __init__(self, place, parts, room, send, recv, own_sem, group):
        self.place = place
        self.total, self.land, self.far = room
        self.load = pltpu.make_async_copy(parts.at[1], self.total, own_sem.at[group])
        make = lambda source, land, slot, device: pltpu.make_async_remote_copy(
            src_ref=source, dst_ref=land, send_sem=send.at[group, slot], recv_sem=recv.at[group, slot],
            device_id=device, device_id_type=pl.DeviceIdType.MESH,
        )
        p = place
        self.across = make(parts.at[0], self.land, 0, p.at(p.z, p.first_y, p.core, p.first_x))
        self.along = [
            make(self.total.at[p.along(k)], self.far.at[k - 1], k, p.at(p.along(k), p.y, p.core, p.x))
            for k in range(1, p.depth)
        ]

    def fold(self):
        self.load.wait()
        self.across.wait_recv()

        @pl.loop(0, self.place.depth)
        def _(z):
            self.total[z] = (self.total[z].astype(F32) + self.land[z].astype(F32)).astype(LOW)

        for copy in self.along:
            copy.start()

    def finish(self):
        for copy in self.along:
            copy.wait_recv()
        result = self.total[self.place.z].astype(F32)
        for k in range(self.place.depth - 1):
            result = result + self.far[k].astype(F32)
        for copy in [self.across] + self.along:
            copy.wait_send()
        return result


def scatter_room(depth, share, cols, kept=()):
    return [
        pltpu.VMEM(shape + (share, cols), LOW)
        for shape in (kept + (depth, 2, 2), (depth, 2, 2), (2, depth), (depth,), (depth - 1,))
    ]


def attention_back_kernel(remote, pairs, *refs):
    (q_ref, k_ref, v_ref, grad_ref, probs_ref, far_ref, order_ref, low_ref) = refs[:8]
    refs = refs[8:]
    sources, refs = (refs[:3], refs[3:]) if remote else ((), refs)
    (dq_ref, dk_ref, dv_ref, rate_ref, grad_qkv_ref), refs = refs[:5], refs[5:]
    (down_ref, *parts), refs = (refs[:3], refs[3:]) if remote else ((None,), refs)
    (keys, values, grad_keys, grad_values, all_q, all_k, all_v), refs = refs[:7], refs[7:]
    step = pl.program_id(0)
    tokens = q_ref.shape[2]
    turns = all_q.shape[0] * pairs

    def when(k, action):
        @pl.when(step == k)
        def _():
            action()

    if remote:
        rooms, (send, recv, own_sem, part_sem) = [refs[5 * g : 5 * g + 5] for g in range(3)], refs[15:]
        place = Place(rooms[0][0].shape[0])
        own = [
            pltpu.make_async_copy(source.at[:, :, place.core], room[0], own_sem.at[g])
            for g, (source, room) in enumerate(zip(sources, rooms))
        ]
        groups = [
            Scatter(place, source.at[:, :, 1 - place.core], room, send, recv, g)
            for g, (source, room) in enumerate(zip(sources, rooms))
        ]
        down, out, up = groups

        def begin():
            for copy in own:
                copy.start()
            meet(place)
            down.start(0)

        def first(k, go=True):
            own[k].wait()
            groups[k].fold(0, go)

        when(0, begin)
        def second():
            down.fold(1)
            out.start(1)
            up.start(1)

        when(1, lambda: (first(0), out.start(0), up.start(0)))
        when(3, lambda: (first(1, False), first(2, False)))
        when(7, second)
        when(11, lambda: down.fold(2))

    @pl.when(step < turns)
    def _():
        row, pair = lax.div(step, pairs), lax.rem(step, pairs)
        pad_rows(keys, k_ref[0, 0])
        pad_rows(values, v_ref[0, 0])
        grad_keys[...] = jnp.zeros_like(grad_keys)
        grad_values[...] = jnp.zeros_like(grad_values)
        sums = [jnp.zeros((8, BLOCK), F32)] * 4
        cols = pl.ds(pl.multiple_of(pair * BLOCK, BLOCK), BLOCK)
        for b in range(tokens // BLOCK):
            lanes = slice(b * BLOCK, (b + 1) * BLOCK)
            window = slice(b * BLOCK, b * BLOCK + SPAN)
            queries = pair_rows(q_ref[0, 0, lanes, :] * 0.125)
            grads = pair_rows(grad_ref[0, lanes, :])
            probs_low = probs_ref[0, 0, b]
            back = nt(values[window, :], grads)
            dist = jnp.where(far_ref[0, b] < FAR, far_ref[0, b], 0.0)
            order = order_ref[0, b]
            sides = []
            for h in range(2):
                probs = probs_low[:, h * BLOCK : (h + 1) * BLOCK].astype(F32)
                part = back[:, h * BLOCK : (h + 1) * BLOCK]
                delta = jnp.sum(probs * part, axis=0, keepdims=True)
                scores = probs * (part - delta)
                sums[2 * h] = sums[2 * h] - fold(scores * dist)
                sums[2 * h + 1] = sums[2 * h + 1] + fold(scores * order)
                sides.append(scores.astype(LOW))
            scores_low = jnp.concatenate(sides, axis=1)
            grad_values[window, :] += nn(probs_low, grads)
            grad_keys[window, :] += nn(scores_low, queries)
            grad_queries = (pair_pick(tn(scores_low, keys[window, :])) * 0.125).astype(LOW)
            dq_ref[0, lanes, :] = grad_queries
            all_q[row, lanes, cols] = grad_queries
        dk = grad_keys[pl.ds(RADIUS, tokens), :].astype(LOW)
        dv = grad_values[pl.ds(RADIUS, tokens), :].astype(LOW)
        dk_ref[0], all_k[row, :, cols] = dk, dk
        dv_ref[0], all_v[row, :, cols] = dv, dv
        for k in range(4):
            rate_ref[0, 0, k] = sums[k]

    for k, ref in enumerate((all_q, all_k, all_v)):
        @pl.when(step == turns + k)
        def _(ref=ref):
            flat = lambda v: v.reshape(-1, v.shape[-1])
            grad_qkv_ref[...] = tn(flat(low_ref[...]), flat(ref[...])).astype(LOW)

    if remote:
        def last():
            copies = []
            for k, (group, part) in enumerate(zip((out, up), parts)):
                group.fold(1, go=False)
                for side, (y, x) in enumerate(((place.first_y, place.first_x), (place.y, place.x))):
                    copies.append(pltpu.make_async_copy(group.total.at[:, y, x], part.at[side], part_sem.at[2 * k + side]))
                    copies[-1].start()
            down_ref[...] = down.finish()
            down.sent()
            out.sent(2)
            up.sent(2)
            for copy in copies:
                copy.wait()

        when(turns + 2, last)


def attention_backward(remote, depth, qkv, grad, probs, far, order, low, sources):
    pairs, rows, tokens = qkv.shape[0] // 3, qkv.shape[1], qkv.shape[2]
    width = pairs * BLOCK
    blocks = tokens // BLOCK
    turns = rows * pairs
    where = lambda s: (jnp.minimum(s, turns - 1) // pairs, jnp.minimum(s, turns - 1) % pairs)
    row_of, pair_of = lambda s: where(s)[0], lambda s: where(s)[1]
    part = lambda k: pl.BlockSpec((1, 1, tokens, BLOCK), lambda s: (k * pairs + pair_of(s), row_of(s), 0, 0))
    flat = pl.BlockSpec((1, tokens, BLOCK), lambda s: (row_of(s), 0, pair_of(s)))
    bias = pl.BlockSpec((1, blocks, SPAN, BLOCK), lambda s: (row_of(s), 0, 0, 0))
    grads = jax.ShapeDtypeStruct((rows, tokens, width), LOW)
    in_specs = [part(0), part(1), part(2), flat]
    in_specs += [pl.BlockSpec((1, 1, blocks, SPAN, 2 * BLOCK), lambda s: where(s) + (0, 0, 0)), bias, bias, whole(low.shape)]
    out_specs = [flat] * 3 + [
        pl.BlockSpec((1, 1, 4, 8, BLOCK), lambda s: where(s) + (0, 0, 0)),
        pl.BlockSpec((width, width), lambda s: (0, jnp.clip(s - turns, 0, 2))),
    ]
    out_shape = [grads] * 3 + [
        jax.ShapeDtypeStruct((rows, pairs, 4, 8, BLOCK), F32),
        jax.ShapeDtypeStruct((width, 3 * width), LOW),
    ]
    scratch = [pltpu.VMEM((tokens + 2 * RADIUS, BLOCK), LOW)] * 2
    scratch += [pltpu.VMEM((tokens + 2 * RADIUS, BLOCK), F32)] * 2
    scratch += [pltpu.VMEM((rows, tokens, width), LOW)] * 3
    more = {}
    if remote:
        in_specs += [pl.BlockSpec(memory_space=pl.ANY)] * 3
        for k, source in enumerate(sources):
            shape = source.shape[4:]
            if k == 0:
                out_specs.append(pl.BlockSpec(shape, lambda s: (0, 0)))
                out_shape.append(jax.ShapeDtypeStruct(shape, F32))
            else:
                out_specs.append(pl.BlockSpec(memory_space=pl.ANY))
                out_shape.append(jax.ShapeDtypeStruct((2, depth) + shape, LOW))
            scratch += scatter_room(depth, *shape)
        scratch += [pltpu.SemaphoreType.DMA((3, depth + 3))] * 2 + [pltpu.SemaphoreType.DMA((3,)), pltpu.SemaphoreType.DMA((4,))]
        more = {"collective_id": CALLS["attention"], "has_side_effects": True}
    return pl.pallas_call(
        functools.partial(attention_back_kernel, remote, pairs),
        grid=(turns + 3,),
        in_specs=in_specs,
        out_specs=out_specs,
        out_shape=out_shape,
        scratch_shapes=scratch,
        compiler_params=params(1, **more),
        name="attention_backward",
    )(qkv, qkv, qkv, grad, probs, far, order, low, *(sources if remote else ()))


def graph_back_kernel(remote, *refs):
    (dq_in, dk_in, dv_in, two_in, unit_in, rstd_in, slope_in, hidden_in, agg2_in, agg1_in, x_in, adj_in, cols_in,
     first_in, second_in, qkv_w_in, gain_ref, late_ref, rate_ref) = refs[:19]
    refs = refs[19:]
    (qkv_source, *parts), refs = (refs[:3], refs[3:]) if remote else ((None,), refs)
    (input_grad_out, edge_out, gains_out, shifts_out, rates_out), refs = refs[:5], refs[5:]
    owned, refs = (refs[:7], refs[7:]) if remote else (refs[:2], refs[2:])
    (dq, dk, dv, two, unit, rstd, slope, hidden, agg2, adj, cols, first_w, second_w, qkv_w,
     back, norms, edge_sums, row_sem, in_sem, out_sem), refs = refs[:20], refs[20:]
    rows, tokens, width = dq.shape
    blocks, chunk = tokens // BLOCK, 2 * BLOCK
    chunks = tokens // chunk
    agg1, x, branch, mean, pre, one = agg2, hidden, dq, dk, dv, two

    by_row = [(dq_in, dq), (dk_in, dk), (dv_in, dv), (two_in, two), (unit_in, unit), (rstd_in, rstd)]
    row_load = lambda k, row: pltpu.make_async_copy(by_row[k][0].at[row], by_row[k][1].at[row], row_sem.at[k, row])
    once = [(qkv_w_in, qkv_w), (second_in, second_w), (cols_in, cols), (hidden_in, hidden), (agg2_in, agg2),
            (adj_in, adj), (slope_in, slope), (first_in, first_w), (x_in, x), (agg1_in, agg1)]
    load = lambda k: pltpu.make_async_copy(*once[k], in_sem.at[k])
    load(0).start()
    for k in range(len(by_row)):
        row_load(k, 0).start()
    load(1).start()
    load(2).start()
    for row in range(1, rows):
        for k in range(len(by_row)):
            row_load(k, row).start()
    for k in range(3, 8):
        load(k).start()

    if remote:
        rooms = [refs[5 * g : 5 * g + 5] for g in range(3)]
        sums, s_land, s_far, send, recv, own_sem, s_send, s_recv = refs[15:23]
        tails = (refs[23:26], refs[26:29])
        depth = rooms[0][0].shape[0]
        place = Place(depth)
        own = pltpu.make_async_copy(qkv_source.at[:, :, place.core], rooms[0][0], own_sem.at[0])
        qkv = Scatter(place, qkv_source.at[:, :, 1 - place.core], rooms[0], send, recv, 0)
        late, early = [
            Scatter(place, room[0].at[1], (room[0].at[0],) + tuple(room[1:]), send, recv, 1 + g)
            for g, room in enumerate(rooms[1:])
        ]
        out, up = [
            Tail(place, part, room, send, recv, own_sem, 3 + g)
            for g, (part, room) in enumerate(zip(parts, tails))
        ]
        own.start()
        out.load.start()
        up.load.start()
        meet(place)
        qkv.start(0)
        out.across.start()
        up.across.start()

    norms[...] = jnp.zeros_like(norms)
    edge_sums[...] = jnp.zeros_like(edge_sums)
    flat = lambda ref: ref[...].reshape(rows * tokens, width)

    def weight_grad(dest, col, left, right):
        half = width // 2
        for part in range(2):
            grad = tn(left[:, :, part * half : (part + 1) * half].reshape(rows * tokens, half), flat(right))
            if not remote:
                dest[part * half : (part + 1) * half, col * width : (col + 1) * width] = grad.astype(LOW)
                continue
            share = dest.shape[4]
            for k in range(half // share):
                index = part * (half // share) + k
                z, y, core, x_at = index // 8, index // 4 % 2, index // 2 % 2, index % 2
                side = place.core if core == 0 else 1 - place.core
                dest[side, z, y, x_at, :, col * width : (col + 1) * width] = grad[k * share : (k + 1) * share].astype(LOW)

    def spread(row, source):
        back[...] = jnp.zeros_like(back)
        for b in range(blocks):
            back[b * BLOCK : b * BLOCK + WIDE, :] += nn(adj[row, b], source[row, b * BLOCK : (b + 1) * BLOCK, :])

    load(0).wait()
    load(1).wait()
    load(2).wait()

    @pl.loop(0, rows)
    def _(row):
        for k in range(len(by_row)):
            row_load(k, row).wait()
        for c in range(chunks):
            part = slice(c * chunk, (c + 1) * chunk)
            grad = two[row, part, :]
            for k, ref in enumerate((dq, dk, dv)):
                grad = grad + nt(ref[row, part, :], qkv_w[:, k * width : (k + 1) * width])
            plain = unit[row, part, :].astype(F32)
            norms[0] += fold(grad * plain)
            norms[1] += fold(grad)
            grad = norm_back(grad, plain, rstd[row, part, :], gain_ref[0:1, :])
            one[row, part, :] = grad
            low = grad.astype(LOW)
            branch[row, part, :] = low
            mean[row, part, :] = (nt(low, second_w[:, width : 2 * width]) * cols[row, part, 2:3]).astype(LOW)
            if remote and c == 0:
                @pl.when(row == 0)
                def _():
                    own.wait()
                    qkv.fold(0)

    load(3).wait()
    load(4).wait()
    second_dest, first_dest = (rooms[1][0], rooms[2][0]) if remote else (owned[1], owned[0])
    weight_grad(second_dest, 0, hidden, branch)
    weight_grad(second_dest, 1, agg2, branch)
    load(8).start()
    load(9).start()
    if remote:
        late.start(0)
        out.fold()
        up.fold()
        qkv.fold(1)
    for k in range(5, 8):
        load(k).wait()

    @pl.loop(0, rows)
    def _(row):
        spread(row, mean)
        for c in range(chunks):
            part = slice(c * chunk, (c + 1) * chunk)
            grad = back[REACH + c * chunk : REACH + (c + 1) * chunk, :]
            grad = grad + nt(branch[row, part, :], second_w[:, 0:width])
            grad = grad * slope[row, part, :].astype(F32)
            edge_sums[0] += fold(grad * cols[row, part, 0:1])
            edge_sums[1] += fold(grad * cols[row, part, 1:2])
            low = grad.astype(LOW)
            pre[row, part, :] = low
            mean[row, part, :] = (nt(low, first_w[:, width : 2 * width]) * cols[row, part, 2:3]).astype(LOW)
            if remote and c == 0:
                @pl.when(row == 0)
                def _():
                    late.fold(0)
    load(8).wait()
    load(9).wait()
    weight_grad(first_dest, 0, x, pre)
    weight_grad(first_dest, 1, agg1, pre)

    line = lambda v: jnp.sum(v, axis=0, keepdims=True)
    lines = jnp.concatenate(
        [line(edge_sums[0]), line(edge_sums[1]), line(norms[0]), line(late_ref[0]), line(late_ref[2]),
         line(norms[1]), line(late_ref[1]), line(late_ref[3])], axis=0,
    )
    rates = jnp.sum(jnp.sum(rate_ref[...], axis=0), axis=2).reshape(-1, BLOCK)

    if remote:
        early.start(0)
        pieces = width // BLOCK
        for k in range(pieces):
            sums[0, k] = lines[:, k * BLOCK : (k + 1) * BLOCK]
        for k in range(3):
            sums[0, pieces + k] = rates[8 * k : 8 * (k + 1)]
        turns = [
            (sums.at[k], s_land.at[k], k, device)
            for k, device in enumerate((
                place.at(place.z, place.y, 1 - place.core, place.x),
                place.at(place.z, place.y, place.core, 1 - place.x),
                place.at(place.z, 1 - place.y, place.core, place.x),
            ))
        ] + [
            (s_far.at[place.z], s_far.at[place.z], 2 + k, place.at(place.along(k), place.y, place.core, place.x))
            for k in range(1, depth)
        ]
        turns = [
            pltpu.make_async_remote_copy(
                src_ref=source, dst_ref=land, send_sem=s_send.at[slot], recv_sem=s_recv.at[slot],
                device_id=device, device_id_type=pl.DeviceIdType.MESH,
            )
            for source, land, slot, device in turns
        ]
        turns[0].start()
        qkv.fold(2)
        late.fold(1)

    writes = lambda row: pltpu.make_async_copy(one.at[row], input_grad_out.at[row], out_sem.at[row])

    @pl.loop(0, rows)
    def _(row):
        spread(row, mean)
        for c in range(chunks):
            part = slice(c * chunk, (c + 1) * chunk)
            grad = one[row, part, :] + back[REACH + c * chunk : REACH + (c + 1) * chunk, :]
            one[row, part, :] = grad + nt(pre[row, part, :], first_w[:, 0:width])
            if remote and c == 0:
                @pl.when(row == 0)
                def _():
                    early.fold(0)
                    turns[0].wait_recv()
                    sums[1] = sums[0] + s_land[0]
                    turns[1].start()
        writes(row).start()

    if remote:
        turns[1].wait_recv()
        sums[2] = sums[1] + s_land[1]
        turns[2].start()
        late.fold(2)
        early.fold(1)
        turns[2].wait_recv()
        s_far[place.z] = sums[2] + s_land[2]
        for turn in turns[3:]:
            turn.start()
        owned[5][...] = out.finish()
        owned[6][...] = up.finish()
        owned[4][...] = qkv.finish()
        early.fold(2)
        result = late.finish()
        owned[2][...] = result[:, :width]
        owned[3][...] = result[:, width:]
        for turn in turns[3:]:
            turn.wait_recv()
        total = s_far[0]
        for k in range(1, depth):
            total = total + s_far[k]
        for k in range(pieces):
            part = slice(k * BLOCK, (k + 1) * BLOCK)
            edge_out[:, part] = total[k, 0:2]
            gains_out[:, part] = total[k, 2:5]
            shifts_out[:, part] = total[k, 5:8]
        for k in range(3):
            rates_out[8 * k : 8 * (k + 1)] = jnp.sum(total[pieces + k], axis=1, keepdims=True)
        result = early.finish()
        owned[0][...] = result[:, :width]
        owned[1][...] = result[:, width:]
        for group in (qkv, late, early):
            group.sent()
        for turn in turns:
            turn.wait_send()
    else:
        edge_out[...], gains_out[...], shifts_out[...] = lines[0:2], lines[2:5], lines[5:8]
        rates_out[...] = jnp.sum(rates, axis=1, keepdims=True)
    for row in range(rows):
        writes(row).wait()


def graph_backward(remote, depth, arrays, gains, late, rates, sources):
    dq, two, unit, rstd, slope, hidden, adj, cols = (arrays[k] for k in (0, 3, 4, 5, 6, 7, 11, 12))
    rows, tokens, width = dq.shape
    vmem, hbm = pl.BlockSpec(memory_space=pltpu.VMEM), pl.BlockSpec(memory_space=pl.ANY)
    shape = lambda dtype, *dims: jax.ShapeDtypeStruct(dims, dtype)
    out_shape = [
        shape(F32, rows, tokens, width), shape(F32, 2, width), shape(F32, 3, width), shape(F32, 3, width),
        shape(F32, rates.shape[1] * 4, 1),
    ]
    like = lambda v: pltpu.VMEM(v.shape, v.dtype)
    scratch = [like(v) for v in (dq, dq, dq, two, unit, rstd, slope, hidden, hidden, adj, cols) + tuple(arrays[13:16])]
    scratch += [
        pltpu.VMEM((tokens + 2 * REACH, width), F32),
        pltpu.VMEM((2, 8, width), F32),
        pltpu.VMEM((2, 8, width), F32),
        pltpu.SemaphoreType.DMA((6, rows)),
        pltpu.SemaphoreType.DMA((10,)),
        pltpu.SemaphoreType.DMA((rows,)),
    ]
    more = {}
    if remote:
        share = sources[0].shape[4]
        out_shape += [shape(F32, share, width)] * 4 + [shape(F32, share, s.shape[-1]) for s in sources]
        scratch += scatter_room(depth, share, sources[0].shape[5])
        for _ in range(2):
            scratch += scatter_room(depth, share, 2 * width, (2,))
        lines = (width // BLOCK + 3, 8, BLOCK)
        scratch += [pltpu.VMEM((3,) + lines, F32), pltpu.VMEM((3,) + lines, F32), pltpu.VMEM((depth,) + lines, F32)]
        scratch += [pltpu.SemaphoreType.DMA((5, depth + 3))] * 2 + [pltpu.SemaphoreType.DMA((5,))]
        scratch += [pltpu.SemaphoreType.DMA((depth + 2,))] * 2
        for part in sources[1:]:
            scratch += [pltpu.VMEM((k, share, part.shape[3]), LOW) for k in (depth, depth, depth - 1)]
        more = {"collective_id": CALLS["graph"], "has_side_effects": True}
    else:
        out_shape += [shape(LOW, width, 2 * width)] * 2
    return pl.pallas_call(
        functools.partial(graph_back_kernel, remote),
        in_specs=[hbm] * 16 + [vmem] * 3 + [hbm] * (3 if remote else 0),
        out_specs=[hbm] + [vmem] * (len(out_shape) - 1),
        out_shape=out_shape,
        scratch_shapes=scratch,
        compiler_params=pltpu.CompilerParams(vmem_limit_bytes=VMEM, **more),
        name="graph_backward",
    )(*arrays, gains, late, rates, *(sources if remote else ()))


def local(
    sizes, inputs, coords, neighbours, counts, doc_length, self_one, near_one, self_two, near_two, edge_proj,
    qkv_proj, out_proj, up_proj, down_proj, norm_gains, norm_shifts, distance_rate, order_rate, cotangent,
):
    axes = ("wide", "narrow")
    rows, tokens, width = inputs.shape
    wide_size, narrow_size = sizes
    depth = wide_size // 4
    remote = wide_size % 4 == 0 and narrow_size == 2 and self_one.shape[0] % 8 == 0
    weights, shards = (self_one, near_one, self_two, near_two, qkv_proj), (out_proj, up_proj, down_proj)
    gather = lambda v: lax.all_gather(v, axes, axis=0, tiled=True)
    scatter = lambda v: lax.psum_scatter(v, axes, scatter_dimension=0, tiled=True).astype(F32)
    blocked = lambda v: v.reshape(depth, 2, 2, 2, -1, v.shape[1])
    flat = lambda v: v.reshape(rows * tokens, width)
    tall = lambda v: v.reshape(rows, tokens, width)
    if not remote:
        weights, shards = tuple(map(gather, weights)), tuple(map(gather, shards))
    results = front(
        remote, depth, doc_length[:, 0], distance_rate, order_rate, neighbours, counts[:, None, :], coords, inputs,
        edge_proj, norm_gains, norm_shifts, weights, shards if remote else (),
    )
    (adj, cols, agg1, slope, hidden, agg2, unit, rstd, normed, low, qkv, att, probs, far, order, first_w, second_w, qkv_w) = results[:18]
    out_w, up = (v.reshape(-1, v.shape[-1]) for v in results[18:20]) if remote else shards[:2]
    result, two, grad_att, grad_out, grad_up, grad_down, late = block_both(
        remote, depth, att.reshape(-1, rows * tokens, BLOCK), flat(normed), flat(cotangent), out_w, up, results[20] if remote else shards[2],
        norm_gains, norm_shifts,
    )
    first_sources = (blocked(grad_down), blocked(grad_out), blocked(grad_up)) if remote else ()
    dq, dk, dv, rates, grad_qkv, *summed = attention_backward(
        remote, depth, qkv, tall(grad_att), probs, far, order, low, first_sources
    )
    arrays = (dq, dk, dv, tall(two), unit, rstd, slope, hidden, agg2, agg1, inputs, adj, cols, first_w, second_w, qkv_w)
    sources = (blocked(grad_qkv), summed[1], summed[2]) if remote else ()
    input_grad, edge, gains, shifts, rates, *owned = graph_backward(remote, depth, arrays, norm_gains, late, rates, sources)
    if remote:
        down_own = summed[0]
        self1, near1, self2, near2, qkv_own, out_own, up_own = owned
    else:
        down_own, out_own, up_own, qkv_own = map(scatter, (grad_down, grad_out, grad_up, grad_qkv))
        self1, near1 = jnp.split(scatter(owned[0]), 2, axis=1)
        self2, near2 = jnp.split(scatter(owned[1]), 2, axis=1)
        edge, gains, shifts, rates = lax.psum((edge, gains, shifts, rates), axes)
    rates = rates.reshape(-1, 2, 2)
    return (
        tall(result), input_grad, self1, near1, self2, near2, edge, qkv_own, out_own, up_own, down_own, gains, shifts,
        rates[:, :, 0].reshape(-1), rates[:, :, 1].reshape(-1),
    )


def solution(mesh):
    axes = ("wide", "narrow")
    middle, last = P(None, axes, None), P(None, None, axes)
    count, weight, same = P(None, axes), P(axes, None), P()
    sizes = (mesh.shape["wide"], mesh.shape["narrow"])
    return jax.shard_map(
        functools.partial(local, sizes),
        mesh=mesh,
        in_specs=(middle, last, last, count, count)
        + (weight,) * 4
        + (same,)
        + (weight,) * 4
        + (same,) * 4
        + (middle,),
        out_specs=(middle, middle) + (weight,) * 4 + (same,) + (weight,) * 4 + (same,) * 4,
        check_vma=False,
    )
```

```python
import functools
import jax
import jax.numpy as jnp
from jax import lax
from jax.experimental import pallas as pl
from jax.experimental.pallas import tpu as pltpu
from jax.sharding import PartitionSpec as P

RADIUS = 128
REACH = 64
BLOCK = 128
WIDE = BLOCK + 2 * REACH
SPAN = BLOCK + 2 * RADIUS
FAR = 1e10
F32 = jnp.float32
LOW = jnp.bfloat16
VMEM = 62 * 2**20
CALLS = {"front": 0, "block": 1, "attention": 2, "graph": 3}


def dot(left, right, dims):
    return lax.dot_general(left, right, ((dims[:1], dims[1:]), ((), ())), preferred_element_type=F32)


def nn(left, right):
    return dot(left, right, (1, 0))


def nt(left, right):
    return dot(left, right, (1, 1))


def tn(left, right):
    return dot(left, right, (0, 0))


def gelu_pair(pre):
    slope = 0.7978845608028654
    square = pre * pre
    half = 0.5 + 0.5 * jnp.tanh(pre * (slope + (slope * 0.044715) * square))
    act = pre * half
    deriv = half + act * (1.0 - half) * (2.0 * slope + (6.0 * slope * 0.044715) * square)
    return act, deriv


def norm_parts(values):
    centre = values - jnp.mean(values, axis=-1, keepdims=True)
    rstd = lax.rsqrt(jnp.mean(centre * centre, axis=-1, keepdims=True) + 1e-05)
    return centre * rstd, rstd


def norm_back(grad, unit, rstd, gain):
    scaled = grad * gain
    mean = jnp.mean(scaled, axis=-1, keepdims=True)
    along = jnp.mean(scaled * unit, axis=-1, keepdims=True)
    return rstd * (scaled - mean - unit * along)


def fold(values):
    rows, cols = values.shape
    return jnp.sum(values.reshape(rows // 8, 8, cols), axis=0)


def whole(shape, space=None):
    return pl.BlockSpec(shape, lambda *_: (0,) * len(shape), pipeline_mode=pl.Buffered(1))


def params(grid_rank, **more):
    return pltpu.CompilerParams(
        vmem_limit_bytes=VMEM, dimension_semantics=("arbitrary",) * grid_rank, **more
    )


def fill_bias(length, point_ref, far_ref, order_ref, row):
    tokens = point_ref.shape[2]
    side = jnp.zeros((2, RADIUS), F32)
    padded = jnp.concatenate([side, point_ref[row], side], axis=1)
    tall = jnp.concatenate([padded, jnp.zeros((6, tokens + 2 * RADIUS), F32)], axis=0)
    for b in range(tokens // BLOCK):
        window = tall[:, b * BLOCK : b * BLOCK + SPAN].T
        key_x, key_y = window[:, 0:1], window[:, 1:2]
        lanes = slice(b * BLOCK, (b + 1) * BLOCK)
        delta_x = key_x - point_ref[row, 0:1, lanes]
        delta_y = key_y - point_ref[row, 1:2, lanes]
        dist = jnp.log(1.0 + 16.0 * (delta_x * delta_x + delta_y * delta_y))
        query = lax.broadcasted_iota(jnp.int32, (SPAN, BLOCK), 1) + b * BLOCK
        key = lax.broadcasted_iota(jnp.int32, (SPAN, BLOCK), 0) + (b * BLOCK - RADIUS)
        allowed = (jnp.abs(query - key) <= RADIUS) & ((query >= length) == (key >= length))
        allowed = allowed & (key >= 0) & (key < tokens)
        far_ref[row, b] = jnp.where(allowed, dist, FAR)
        order_ref[row, b] = jnp.tanh(4.0 * delta_x)


def pair_rows(values):
    lane = lax.broadcasted_iota(jnp.int32, values.shape, 1)
    zero = jnp.zeros_like(values)
    first = jnp.where(lane < BLOCK // 2, values, zero)
    second = jnp.where(lane < BLOCK // 2, zero, values)
    return jnp.concatenate([first, second], axis=0)


def pair_pick(values):
    lane = lax.broadcasted_iota(jnp.int32, (BLOCK, BLOCK), 1)
    return jnp.where(lane < BLOCK // 2, values[:BLOCK], values[BLOCK:])


def pad_rows(pad_ref, values):
    tokens = values.shape[0]
    zeros = jnp.zeros((RADIUS, values.shape[1]), pad_ref.dtype)
    pad_ref[pl.ds(0, RADIUS), :] = zeros
    pad_ref[pl.ds(RADIUS + tokens, RADIUS), :] = zeros
    pad_ref[pl.ds(RADIUS, tokens), :] = values


FIRST, OWN, PASSED, SIBLING = 0, 1, 2, 3


class Place:
    def __init__(self, depth):
        self.depth = depth
        wide, self.x = lax.axis_index("wide"), lax.axis_index("narrow")
        self.core = lax.rem(wide, 2)
        self.y = lax.rem(lax.div(wide, 2), 2)
        self.z = lax.div(wide, 4)
        core, y, x = self.core, self.y, self.x
        self.first_y = (1 - core) * (1 - y) + core * y
        self.first_x = core * (1 - x) + (1 - core) * x
        self.second_y = core * (1 - y) + (1 - core) * y
        self.second_x = (1 - core) * (1 - x) + core * x

    def at(self, z, y, core, x):
        return ((z * 2 + y) * 2 + core, x)

    def along(self, k):
        return lax.rem(self.z + k, self.depth)

    def partners(self):
        along = [self.at(self.along(k), self.y, self.core, self.x) for k in range(1, self.depth)]
        return along + [
            self.at(self.z, self.first_y, self.core, self.first_x),
            self.at(self.z, self.second_y, self.core, self.second_x),
            self.at(self.z, self.y, 1 - self.core, self.x),
        ]


def meet(place):
    barrier = pltpu.get_barrier_semaphore()
    partners = place.partners()
    for partner in partners:
        pl.semaphore_signal(barrier, inc=1, device_id=partner, device_id_type=pl.DeviceIdType.MESH)
    pl.semaphore_wait(barrier, len(partners))


class Gather:
    def __init__(self, place, land, send, recv, group):
        self.place, self.land, self.send, self.recv, self.group = place, land, send, recv, group

    def copy(self, view, slot, device):
        return pltpu.make_async_remote_copy(
            src_ref=view, dst_ref=view, send_sem=self.send.at[self.group, slot], recv_sem=self.recv.at[self.group, slot],
            device_id=device, device_id_type=pl.DeviceIdType.MESH,
        )

    def pieces(self, stage):
        p, land = self.place, self.land
        base = p.depth - 1
        mine = land.at[:, p.y, p.core, p.x]
        if stage == "along":
            here = land.at[p.z, p.y, p.core, p.x]
            found = []
            for k in range(1, p.depth):
                there = land.at[p.along(p.depth - k), p.y, p.core, p.x]
                found.append((here, there, k - 1, p.at(p.along(k), p.y, p.core, p.x)))
            return found
        first = p.at(p.z, p.first_y, p.core, p.first_x)
        second = p.at(p.z, p.second_y, p.core, p.second_x)
        if stage == FIRST:
            return [(mine, land.at[:, p.first_y, p.core, p.first_x], base, first)]
        if stage == OWN:
            return [(mine, land.at[:, p.second_y, p.core, p.second_x], base + 1, second)]
        if stage == PASSED:
            return [(land.at[:, p.first_y, p.core, p.first_x], land.at[:, 1 - p.y, p.core, 1 - p.x], base + 2, second)]
        return [(land.at[:, :, p.core], land.at[:, :, 1 - p.core], base + 3, p.at(p.z, p.y, 1 - p.core, p.x))]

    def start(self, *stages):
        for stage in stages:
            for leaves, _, slot, device in self.pieces(stage):
                self.copy(leaves, slot, device).start()

    def arrive(self, *stages):
        for stage in stages:
            for _, arrives, slot, device in self.pieces(stage):
                self.copy(arrives, slot, device).wait_recv()

    def sent(self, *stages):
        for stage in stages or ("along", FIRST, OWN, PASSED, SIBLING):
            for leaves, _, slot, device in self.pieces(stage):
                self.copy(leaves, slot, device).wait_send()


def merge_rows(full, land):
    depth, rows = land.shape[0], land.shape[4]

    @pl.loop(0, depth * 4)
    def _(k):
        z, y, core = lax.div(k, 4), lax.rem(lax.div(k, 2), 2), lax.rem(k, 2)
        pair = jnp.concatenate([land[z, y, core, 0].astype(F32), land[z, y, core, 1].astype(F32)], axis=0)
        full[pl.ds(pl.multiple_of(k * 2 * rows, 16), 2 * rows), :] = pair.astype(LOW)


def front_kernel(remote, *refs):
    (length_ref, dist_rate_ref, order_rate_ref, near_ref, count_ref, point_ref, x_ref, edge_w_ref, gain_ref, shift_ref,
     self1_ref, near1_ref, self2_ref, near2_ref, qkv_w_ref) = refs[:15]
    refs = refs[15:]
    shards, refs = (refs[:3], refs[3:]) if remote else ((), refs)
    outs, refs = refs[:18], refs[18:]
    fulls, refs = (refs[:3], refs[3:]) if remote else ((), refs)
    (adj, cols, agg1, slope, hidden, agg2, unit, rstd, normed, low, qkv, att, probs, far, order,
     first_w, second_w, third_w, pad, point_pad, rel, keys, values, out_sem, probs_sem, in_sem) = refs[:26]
    rows, slots, tokens = near_ref.shape
    width = x_ref.shape[2]
    pairs = width // BLOCK
    blocks = tokens // BLOCK
    chunk = 2 * BLOCK

    writes = {}

    def write(k, source, dest=None):
        writes[k] = pltpu.make_async_copy(source, outs[k] if dest is None else dest, out_sem.at[k])
        writes[k].start()

    if remote:
        land_a, land_b, land_q, send, recv = refs[26:]
        place = Place(land_a.shape[0])
        lands = (land_a, land_b, land_q) + tuple(fulls)
        groups = [Gather(place, land, send, recv, g) for g, land in enumerate(lands)]
        ga, gb, gq, go, gu, gd = groups
        column = lambda land, k: land.at[place.z, place.y, place.core, place.x, :, pl.ds(k * width, width)]
        own = lambda land: land.at[place.z, place.y, place.core, place.x]
        loads = [
            [pltpu.make_async_copy(ref, column(land_a, k), in_sem.at[k]) for k, ref in enumerate((self1_ref, near1_ref))],
            [pltpu.make_async_copy(ref, column(land_b, k), in_sem.at[2 + k]) for k, ref in enumerate((self2_ref, near2_ref))],
            [pltpu.make_async_copy(qkv_w_ref, own(land_q), in_sem.at[4])],
        ] + [[pltpu.make_async_copy(ref, own(full), in_sem.at[5 + k])] for k, (ref, full) in enumerate(zip(shards, fulls))]
        for load in loads:
            for copy in load:
                copy.start()
        meet(place)

        def begin(g):
            for copy in loads[g]:
                copy.wait()
            groups[g].start("along")

        begin(0)
    else:
        loads = [
            pltpu.make_async_copy(ref, dest, in_sem.at[k])
            for k, (ref, dest) in enumerate((
                (self1_ref, first_w.at[:, pl.ds(0, width)]), (near1_ref, first_w.at[:, pl.ds(width, width)]),
                (self2_ref, second_w.at[:, pl.ds(0, width)]), (near2_ref, second_w.at[:, pl.ds(width, width)]),
                (qkv_w_ref, third_w),
            ))
        ]
        for copy in loads:
            copy.start()

    side = jnp.zeros((REACH, width), LOW)
    pad[pl.ds(0, REACH), :] = side
    pad[pl.ds(tokens + REACH, REACH), :] = side

    @pl.loop(0, rows)
    def _(row):
        length = length_ref[row]
        pad[pl.ds(REACH, tokens), :] = x_ref[row]
        points = point_ref[row]
        high = points.astype(LOW).astype(F32)
        mid = (points - high).astype(LOW).astype(F32)
        tail = points - high - mid
        split = jnp.concatenate([high, mid, tail, jnp.ones((1, tokens), F32), jnp.zeros((9, tokens), F32)], axis=0)
        edge_side = jnp.zeros((16, REACH), F32)
        point_pad[...] = jnp.concatenate([edge_side, split, edge_side], axis=1).astype(LOW)

        @pl.loop(0, blocks)
        def _(b):
            start = pl.multiple_of(b * BLOCK, BLOCK)
            lanes = pl.ds(start, BLOCK)
            near = near_ref[row, :, lanes]
            count = count_ref[row, :, lanes]
            spot = lax.broadcasted_iota(jnp.int32, (1, BLOCK), 1) + start
            slot = lax.broadcasted_iota(jnp.int32, (slots, BLOCK), 0)
            same = (near >= length) == (spot >= length)
            rel[...] = jnp.where((slot < count) & same, near - (start - REACH), -1)
            target = lax.broadcasted_iota(jnp.int32, (WIDE, BLOCK), 0)
            total = jnp.zeros((WIDE, BLOCK), F32)
            for s in range(slots):
                total = total + jnp.where(rel[s : s + 1, :] == target, 1.0, 0.0)
            band = total.astype(LOW)
            adj[row, b] = band
            sums = nn(point_pad[:, pl.ds(start, WIDE)], band)
            inverse = 1.0 / count.astype(F32)
            here = point_ref[row, :, lanes]
            edge = (sums[0:2] + sums[2:4] + sums[4:6] - sums[6:7] * here) * inverse
            lines = jnp.concatenate([edge, inverse, jnp.zeros((5, BLOCK), F32)], axis=0).T
            cols[row, lanes, :] = lines
            agg = tn(band, pad[pl.ds(start, WIDE), :])
            agg1[row, lanes, :] = (agg * lines[:, 2:3]).astype(LOW)

        if remote:
            @pl.when(row == 0)
            def _():
                ga.arrive("along")
                ga.start(FIRST, OWN)
                begin(1)

    write(0, adj)
    write(1, cols)
    write(2, agg1)
    if remote:
        ga.arrive(FIRST)
        ga.start(PASSED)
        gb.arrive("along")
        gb.start(FIRST, OWN)
        begin(2)

    @pl.loop(0, rows)
    def _(row):
        fill_bias(length_ref[row], point_ref, far, order, row)

    write(13, far)
    write(14, order)
    if remote:
        ga.arrive(OWN, PASSED)
        ga.start(SIBLING)
        gb.arrive(FIRST)
        gb.start(PASSED)
        ga.arrive(SIBLING)
        merge_rows(first_w, land_a)
    else:
        for copy in loads:
            copy.wait()
        write(16, second_w)
        write(17, third_w)
    write(15, first_w)

    @pl.loop(0, rows)
    def _(row):
        for c in range(tokens // chunk):
            part = slice(c * chunk, (c + 1) * chunk)
            pre = nn(x_ref[row, part, :], first_w[:, 0:width])
            pre = pre + nn(agg1[row, part, :], first_w[:, width : 2 * width])
            pre = pre + cols[row, part, 0:1] * edge_w_ref[0:1, :] + cols[row, part, 1:2] * edge_w_ref[1:2, :]
            act, deriv = gelu_pair(pre)
            slope[row, part, :] = deriv.astype(LOW)
            hidden[row, part, :] = act.astype(LOW)
            pad[REACH + c * chunk : REACH + (c + 1) * chunk, :] = act.astype(LOW)
        for b in range(blocks):
            lanes = slice(b * BLOCK, (b + 1) * BLOCK)
            agg = tn(adj[row, b], pad[b * BLOCK : b * BLOCK + WIDE, :])
            agg2[row, lanes, :] = (agg * cols[row, lanes, 2:3]).astype(LOW)
        if remote:
            @pl.when(row == 0)
            def _():
                gb.arrive(OWN, PASSED)
                gb.start(SIBLING)
                gq.arrive("along")
                gq.start(FIRST, OWN)
                begin(3)
                begin(4)

    write(3, slope)
    write(4, hidden)
    write(5, agg2)
    if remote:
        gb.arrive(SIBLING)
        merge_rows(second_w, land_b)
        write(16, second_w)

    @pl.loop(0, rows)
    def _(row):
        for c in range(tokens // chunk):
            part = slice(c * chunk, (c + 1) * chunk)
            resid = x_ref[row, part, :].astype(F32) + nn(hidden[row, part, :], second_w[:, 0:width])
            resid = resid + nn(agg2[row, part, :], second_w[:, width : 2 * width])
            plain, scale = norm_parts(resid)
            unit[row, part, :] = plain.astype(LOW)
            rstd[row, part, :] = scale
            out = plain * gain_ref[0:1, :] + shift_ref[0:1, :]
            normed[row, part, :] = out
            low[row, part, :] = out.astype(LOW)
        if remote:
            @pl.when(row == 0)
            def _():
                gq.arrive(FIRST)
                gq.start(PASSED)
                for g in (go, gu):
                    g.arrive("along")
                    g.start(FIRST, OWN)
                begin(5)

    write(6, unit)
    write(7, rstd)
    write(8, normed)
    write(9, low)
    if remote:
        gq.arrive(OWN, PASSED)
        gq.start(SIBLING)
        gq.arrive(SIBLING)
        merge_rows(third_w, land_q)
        write(17, third_w)

    @pl.loop(0, rows)
    def _(row):
        for c in range(tokens // chunk):
            part = slice(c * chunk, (c + 1) * chunk)
            out = nn(low[row, part, :], third_w[...]).astype(LOW)
            for k in range(3 * pairs):
                qkv[k, row, part, :] = out[:, k * BLOCK : (k + 1) * BLOCK]

    write(10, qkv)
    zeros = jnp.zeros((RADIUS, BLOCK), LOW)
    for ref in (keys, values):
        ref[pl.ds(0, RADIUS), :] = zeros
        ref[pl.ds(RADIUS + tokens, RADIUS), :] = zeros

    @pl.loop(0, rows * pairs)
    def _(turn):
        row, pair, slot = lax.div(turn, pairs), lax.rem(turn, pairs), lax.rem(turn, 2)
        if remote:
            @pl.when(turn == 1)
            def _():
                for g in (go, gu):
                    g.arrive(FIRST)
                    g.start(PASSED)
                gd.arrive("along")
                gd.start(FIRST, OWN)

            @pl.when(turn == 6)
            def _():
                for g in (go, gu):
                    g.arrive(OWN, PASSED)
                    g.start(SIBLING)

        def probs_copy(t, s):
            return pltpu.make_async_copy(
                probs.at[s], outs[12].at[lax.div(t, pairs), lax.rem(t, pairs)], probs_sem.at[s]
            )

        @pl.when(turn >= 2)
        def _():
            probs_copy(turn - 2, slot).wait()

        keys[pl.ds(RADIUS, tokens), :] = qkv[pairs + pair, row]
        values[pl.ds(RADIUS, tokens), :] = qkv[2 * pairs + pair, row]
        for b in range(blocks):
            lanes = slice(b * BLOCK, (b + 1) * BLOCK)
            window = slice(b * BLOCK, b * BLOCK + SPAN)
            queries = pair_rows(qkv[pair, row, lanes, :] * 0.125)
            raw = nt(keys[window, :], queries)
            sides = []
            for h in range(2):
                bias = order_rate_ref[2 * pair + h] * order[row, b] - dist_rate_ref[2 * pair + h] * far[row, b]
                scores = raw[:, h * BLOCK : (h + 1) * BLOCK] + bias
                grown = jnp.exp(scores - jnp.max(scores, axis=0, keepdims=True))
                scale = 1.0 / jnp.sum(grown, axis=0, keepdims=True)
                sides.append((grown * scale).astype(LOW))
            both = jnp.concatenate(sides, axis=1)
            probs[slot, b] = both
            att[pair, row, lanes, :] = pair_pick(tn(both, values[window, :])).astype(LOW)
        probs_copy(turn, slot).start()

    last = rows * pairs
    for turn in (last - 2, last - 1):
        pltpu.make_async_copy(probs.at[turn % 2], outs[12].at[turn // pairs, turn % pairs], probs_sem.at[turn % 2]).wait()
    write(11, att)
    if remote:
        for g in (go, gu):
            g.arrive(SIBLING)
        gd.arrive(FIRST, OWN)
        for g in groups[:5]:
            g.sent()
        gd.sent("along", FIRST, OWN)
    for copy in writes.values():
        copy.wait()


def front(remote, depth, length, dist_rate, order_rate, near, count, point, x, edge_w, gains, shifts, weights, shards):
    rows, tokens, width = x.shape
    slots = near.shape[1]
    blocks, pairs = tokens // BLOCK, width // BLOCK
    smem, vmem, hbm = (pl.BlockSpec(memory_space=s) for s in (pltpu.SMEM, pltpu.VMEM, pl.ANY))
    each = lambda dtype, *shape: ((rows,) + shape, dtype)
    kept = [
        each(LOW, blocks, WIDE, BLOCK),
        each(F32, tokens, 8),
        each(LOW, tokens, width),
        each(LOW, tokens, width),
        each(LOW, tokens, width),
        each(LOW, tokens, width),
        each(LOW, tokens, width),
        each(F32, tokens, 1),
        each(F32, tokens, width),
        each(LOW, tokens, width),
        ((3 * pairs, rows, tokens, BLOCK), LOW),
        ((pairs, rows, tokens, BLOCK), LOW),
        each(LOW, pairs, blocks, SPAN, 2 * BLOCK),
        each(F32, blocks, SPAN, BLOCK),
        each(F32, blocks, SPAN, BLOCK),
        ((width, 2 * width), LOW),
        ((width, 2 * width), LOW),
        ((width, 3 * width), LOW),
    ]
    out_shape = [jax.ShapeDtypeStruct(*k) for k in kept]
    kept[12] = ((2, blocks, SPAN, 2 * BLOCK), LOW)
    scratch = [pltpu.VMEM(*k) for k in kept]
    scratch += [
        pltpu.VMEM((tokens + 2 * REACH, width), LOW),
        pltpu.VMEM((16, tokens + 2 * REACH), LOW),
        pltpu.VMEM((slots, BLOCK), jnp.int32),
        pltpu.VMEM((tokens + 2 * RADIUS, BLOCK), LOW),
        pltpu.VMEM((tokens + 2 * RADIUS, BLOCK), LOW),
        pltpu.SemaphoreType.DMA((18,)),
        pltpu.SemaphoreType.DMA((2,)),
        pltpu.SemaphoreType.DMA((8,)),
    ]
    more = {}
    if remote:
        blocked = lambda shape: (depth, 2, 2, 2) + shape
        out_shape += [jax.ShapeDtypeStruct(blocked(s.shape), LOW) for s in shards]
        share = weights[0].shape[0]
        scratch += [pltpu.VMEM(blocked((share, k * width)), LOW) for k in (2, 2, 3)]
        scratch += [pltpu.SemaphoreType.DMA((6, depth + 3))] * 2
        more = {"collective_id": CALLS["front"], "has_side_effects": True}
    return pl.pallas_call(
        functools.partial(front_kernel, remote),
        in_specs=[smem] * 3 + [vmem] * 7 + [hbm] * (len(weights) + len(shards)),
        out_specs=[hbm] * len(out_shape),
        out_shape=out_shape,
        scratch_shapes=scratch,
        compiler_params=pltpu.CompilerParams(vmem_limit_bytes=VMEM, **more),
        name="front",
    )(length, dist_rate, order_rate, near, count, point, x, edge_w, gains, shifts, *weights, *shards)


TILE = 512


def block_kernel(remote, steps, *refs):
    (att_ref, normed_in, cot_ref, out_w_ref, up_in, down_in, gain_ref, shift_ref,
     result_ref, two_out, grad_att_ref, grad_out_out, grad_up_ref, grad_down_ref, norms_ref,
     act_all, up_all, second_all, down_all, attn_all, normed_all, unit_all, rstd_all, down_w, up_ref, in_sem, normed_sem, up_sem, out_sem) = refs[:29]
    step = pl.program_id(0)
    turns, tokens, half = act_all.shape
    parts, piece = turns // 2, 2 * half
    width = normed_all.shape[1]
    tile = lambda k: pl.ds(pl.multiple_of(k * TILE, TILE), TILE)
    load_normed = lambda k: pltpu.make_async_copy(normed_in.at[tile(k)], normed_all.at[tile(k)], normed_sem.at[k])
    chunk = lambda c: (slice(None), pl.ds(c * piece, piece))
    load_up = [pltpu.make_async_copy(up_in.at[chunk(c)], up_ref.at[chunk(c)], up_sem.at[c]) for c in range(parts)]
    write_two = pltpu.make_async_copy(normed_all, two_out, out_sem.at[0])
    write_out = pltpu.make_async_copy(unit_all.at[pl.ds(0, width)], grad_out_out, out_sem.at[1])

    if remote:
        send, recv = refs[29:]
        place = Place(parts)
        mine, first, second, last = [
            down_w.at[:, y, place.core, x]
            for y, x in (
                (place.y, place.x), (place.first_y, place.first_x), (place.second_y, place.second_x), (1 - place.y, 1 - place.x)
            )
        ]
        loads = [
            pltpu.make_async_copy(down_in.at[:, y, place.core, x], view, in_sem.at[1 + k])
            for k, (y, x, view) in enumerate((
                (place.y, place.x, mine), (place.first_y, place.first_x, first), (place.second_y, place.second_x, second)
            ))
        ]

        def copy(view, slot, device):
            return pltpu.make_async_remote_copy(
                src_ref=view, dst_ref=view, send_sem=send.at[slot], recv_sem=recv.at[slot],
                device_id=device, device_id_type=pl.DeviceIdType.MESH,
            )

        partner = place.at(place.z, place.second_y, place.core, place.second_x)
        sibling = place.at(place.z, place.y, 1 - place.core, place.x)
        pass_on, arriving = copy(first, 4, partner), copy(last, 4, partner)
        across = [copy(view, k, sibling) for k, view in enumerate((mine, first, second, last))]
        theirs = [
            copy(down_w.at[:, y, 1 - place.core, x], k, sibling)
            for k, (y, x) in enumerate((
                (place.y, place.x), (place.second_y, place.second_x), (place.first_y, place.first_x), (1 - place.y, 1 - place.x)
            ))
        ]

        def begin():
            for item in loads:
                item.start()
            meet(place)
            loads[1].wait()
            pass_on.start()
            across[1].start()
            loads[0].wait()
            across[0].start()
            loads[2].wait()
            across[2].start()

        def finish():
            arriving.wait_recv()
            across[3].start()
            for item in theirs:
                item.wait_recv()
            for item in across:
                item.wait_send()
            pass_on.wait_send()
    else:
        full = pltpu.make_async_copy(down_in, down_w, in_sem.at[1])
        begin, finish = full.start, full.wait

    def put(ref, c, at, value):
        ref[2 * c, at, :], ref[2 * c + 1, at, :] = value[:, :half], value[:, half:]

    def get(ref, c, at):
        return jnp.concatenate([ref[2 * c, at, :], ref[2 * c + 1, at, :]], axis=1)

    def down_rows(c):
        return down_w[c].reshape(piece, width)

    @pl.when(step == 0)
    def _():
        load_normed(0).start()
        for copy_up in load_up:
            copy_up.start()
        for k in range(1, steps):
            load_normed(k).start()
        norms_ref[...] = jnp.zeros_like(norms_ref)
        begin()

    @pl.when(step < steps)
    def _():
        at = tile(step)
        load_normed(step).wait()
        att = jnp.concatenate([att_ref[k, at, :] for k in range(att_ref.shape[0])], axis=1)
        unit, rstd = norm_parts(normed_all[at, :] + nn(att, out_w_ref[...]))
        unit_all[at, :] = unit.astype(LOW)
        rstd_all[at, :] = rstd
        normed = unit * gain_ref[1:2, :] + shift_ref[1:2, :]
        normed_all[at, :] = normed
        second_all[at, :] = normed.astype(LOW)
        for c in range(parts):
            pl.when(step == 0)(load_up[c].wait)
            act, deriv = gelu_pair(nn(second_all[at, :], up_ref[:, c * piece : (c + 1) * piece]))
            put(act_all, c, at, act.astype(LOW))
            put(up_all, c, at, deriv.astype(LOW))

    @pl.when(step == steps)
    def _():
        finish()

    @pl.when((step >= steps) & (step < 2 * steps))
    def _():
        at = pl.ds(pl.multiple_of((step - steps) * TILE, TILE), TILE)
        resid = normed_all[at, :]
        for c in range(parts):
            resid = resid + nn(get(act_all, c, at), down_rows(c))
        unit, rstd = norm_parts(resid)
        result_ref[...] = (unit * gain_ref[2:3, :] + shift_ref[2:3, :]).astype(LOW)
        cot = cot_ref[...].astype(F32)
        norms_ref[2] += fold(cot * unit)
        norms_ref[3] += fold(cot)
        grad = norm_back(cot, unit, rstd, gain_ref[2:3, :])
        down_all[at, :] = grad.astype(LOW)
        for c in range(parts):
            up_low = (nt(down_all[at, :], down_rows(c)) * get(up_all, c, at).astype(F32)).astype(LOW)
            put(up_all, c, at, up_low)
            grad = grad + nt(up_low, up_ref[:, c * piece : (c + 1) * piece])
        unit = unit_all[at, :].astype(F32)
        norms_ref[0] += fold(grad * unit)
        norms_ref[1] += fold(grad)
        grad = norm_back(grad, unit, rstd_all[at, :], gain_ref[1:2, :])
        normed_all[at, :] = grad
        low = grad.astype(LOW)
        attn_all[at, :] = low
        grad_att_ref[...] = nt(low, out_w_ref[...]).astype(LOW)

    @pl.when(step == 2 * steps)
    def _():
        write_two.start()
        att = jnp.concatenate([att_ref[k] for k in range(att_ref.shape[0])], axis=1)
        unit_all[pl.ds(0, width), :] = tn(att, attn_all[...]).astype(LOW)
        write_out.start()

    @pl.when(step >= 2 * steps)
    def _():
        turn = step - 2 * steps
        grad_down_ref[...] = tn(act_all[turn], down_all[...]).astype(LOW)
        grad_up_ref[...] = tn(second_all[...], up_all[turn]).astype(LOW)

    @pl.when(step == 2 * steps + turns - 1)
    def _():
        write_two.wait()
        write_out.wait()


def block_both(remote, depth, att, normed, cot, out_w, up, down, gains, shifts):
    tokens, width = normed.shape
    wide = up.shape[1]
    steps = tokens // TILE
    parts = depth if remote else 4
    piece = wide // parts
    tile = pl.BlockSpec((TILE, width), lambda s: (jnp.clip(s - steps, 0, steps - 1), 0))
    late = lambda s: jnp.maximum(s - 2 * steps, 0)
    hbm = pl.BlockSpec(memory_space=pl.ANY)
    down = down if remote else down.reshape(parts, piece, width)
    more = {"collective_id": CALLS["block"], "has_side_effects": True} if remote else {}
    wide_low = pltpu.VMEM((2 * parts, tokens, piece // 2), LOW)
    tall_low = pltpu.VMEM((tokens, width), LOW)
    return pl.pallas_call(
        functools.partial(block_kernel, remote, steps),
        grid=(2 * steps + 2 * parts,),
        in_specs=[
            whole(att.shape), hbm, tile, whole((width, width)), hbm, hbm, whole(gains.shape), whole(shifts.shape),
        ],
        out_specs=[
            tile, hbm, tile, hbm,
            pl.BlockSpec((width, piece // 2), lambda s: (0, late(s))),
            pl.BlockSpec((piece // 2, width), lambda s: (late(s), 0)),
            pl.BlockSpec((4, 8, width), lambda s: (0, 0, 0)),
        ],
        out_shape=[
            jax.ShapeDtypeStruct((tokens, width), LOW),
            jax.ShapeDtypeStruct((tokens, width), F32),
            jax.ShapeDtypeStruct((tokens, width), LOW),
            jax.ShapeDtypeStruct((width, width), LOW),
            jax.ShapeDtypeStruct(up.shape, LOW),
            jax.ShapeDtypeStruct((wide, width), LOW),
            jax.ShapeDtypeStruct((4, 8, width), F32),
        ],
        scratch_shapes=[
            wide_low, wide_low, tall_low, tall_low, tall_low,
            pltpu.VMEM((tokens, width), F32),
            tall_low,
            pltpu.VMEM((tokens, 1), F32),
            pltpu.VMEM(down.shape, LOW),
            pltpu.VMEM(up.shape, LOW),
            pltpu.SemaphoreType.DMA((4,)),
            pltpu.SemaphoreType.DMA((steps,)),
            pltpu.SemaphoreType.DMA((parts,)),
            pltpu.SemaphoreType.DMA((2,)),
        ]
        + ([pltpu.SemaphoreType.DMA((5,))] * 2 if remote else []),
        compiler_params=params(1, **more),
        name="block_both",
    )(att, normed, cot, out_w, up, down, gains, shifts)


class Scatter:
    def __init__(self, place, leaving, room, send, recv, group):
        self.place, self.leaving, self.send, self.recv, self.group = place, leaving, send, recv, group
        self.total, self.lands = room[0], room[1:]

    def copies(self, stage):
        p, total = self.place, self.total
        if stage == 0:
            found = [(self.leaving, self.lands[0], 0, p.at(p.z, p.y, 1 - p.core, p.x))]
        elif stage == 1:
            second = p.at(p.z, p.second_y, p.core, p.second_x)
            found = [
                (total.at[:, p.second_y, p.second_x], self.lands[1].at[0], 1, second),
                (total.at[:, 1 - p.y, 1 - p.x], self.lands[1].at[1], 2, second),
            ]
        elif stage == 2:
            first = p.at(p.z, p.first_y, p.core, p.first_x)
            found = [(total.at[:, p.first_y, p.first_x], self.lands[2], 3, first)]
        else:
            found = [
                (total.at[p.along(k), p.y, p.x], self.lands[3].at[k - 1], 3 + k, p.at(p.along(k), p.y, p.core, p.x))
                for k in range(1, p.depth)
            ]
        return [
            pltpu.make_async_remote_copy(
                src_ref=source, dst_ref=land, send_sem=self.send.at[self.group, slot],
                recv_sem=self.recv.at[self.group, slot], device_id=device, device_id_type=pl.DeviceIdType.MESH,
            )
            for source, land, slot, device in found
        ]

    def start(self, stage):
        for copy in self.copies(stage):
            copy.start()

    def arrive(self, stage):
        for copy in self.copies(stage):
            copy.wait_recv()

    def add(self, y, x, land):
        @pl.loop(0, self.place.depth)
        def _(z):
            self.total[z, y, x] = (self.total[z, y, x].astype(F32) + land(z).astype(F32)).astype(LOW)

    def fold(self, stage, go=True):
        p = self.place
        self.arrive(stage)
        if stage == 0:
            add = lambda y, x: self.add(y, x, lambda z: self.lands[0][z, y, x])
            add(p.second_y, p.second_x)
            add(1 - p.y, 1 - p.x)
            if go:
                self.start(1)
            add(p.first_y, p.first_x)
            add(p.y, p.x)
        elif stage == 1:
            self.add(p.first_y, p.first_x, lambda z: self.lands[1][1, z])
            if go:
                self.start(2)
            self.add(p.y, p.x, lambda z: self.lands[1][0, z])
        else:
            self.add(p.y, p.x, lambda z: self.lands[2][z])
            if go:
                self.start(3)

    def finish(self):
        p = self.place
        self.arrive(3)
        result = self.total[p.z, p.y, p.x].astype(F32)
        for k in range(p.depth - 1):
            result = result + self.lands[3][k].astype(F32)
        return result

    def sent(self, stages=4):
        for stage in range(stages):
            for copy in self.copies(stage):
                copy.wait_send()


class Tail:
    def __init__(self, place, parts, room, send, recv, own_sem, group):
        self.place = place
        self.total, self.land, self.far = room
        self.load = pltpu.make_async_copy(parts.at[1], self.total, own_sem.at[group])
        make = lambda source, land, slot, device: pltpu.make_async_remote_copy(
            src_ref=source, dst_ref=land, send_sem=send.at[group, slot], recv_sem=recv.at[group, slot],
            device_id=device, device_id_type=pl.DeviceIdType.MESH,
        )
        p = place
        self.across = make(parts.at[0], self.land, 0, p.at(p.z, p.first_y, p.core, p.first_x))
        self.along = [
            make(self.total.at[p.along(k)], self.far.at[k - 1], k, p.at(p.along(k), p.y, p.core, p.x))
            for k in range(1, p.depth)
        ]

    def fold(self):
        self.load.wait()
        self.across.wait_recv()

        @pl.loop(0, self.place.depth)
        def _(z):
            self.total[z] = (self.total[z].astype(F32) + self.land[z].astype(F32)).astype(LOW)

        for copy in self.along:
            copy.start()

    def finish(self):
        for copy in self.along:
            copy.wait_recv()
        result = self.total[self.place.z].astype(F32)
        for k in range(self.place.depth - 1):
            result = result + self.far[k].astype(F32)
        for copy in [self.across] + self.along:
            copy.wait_send()
        return result


def scatter_room(depth, share, cols, kept=()):
    return [
        pltpu.VMEM(shape + (share, cols), LOW)
        for shape in (kept + (depth, 2, 2), (depth, 2, 2), (2, depth), (depth,), (depth - 1,))
    ]


def attention_back_kernel(remote, pairs, *refs):
    (q_ref, k_ref, v_ref, grad_ref, probs_ref, far_ref, order_ref, low_ref) = refs[:8]
    refs = refs[8:]
    sources, refs = (refs[:3], refs[3:]) if remote else ((), refs)
    (dq_ref, dk_ref, dv_ref, rate_ref, grad_qkv_ref), refs = refs[:5], refs[5:]
    (down_ref, *parts), refs = (refs[:3], refs[3:]) if remote else ((None,), refs)
    (keys, values, grad_keys, grad_values, all_q, all_k, all_v), refs = refs[:7], refs[7:]
    step = pl.program_id(0)
    tokens = q_ref.shape[2]
    turns = all_q.shape[0] * pairs

    def when(k, action):
        @pl.when(step == k)
        def _():
            action()

    if remote:
        rooms, (send, recv, own_sem, part_sem) = [refs[5 * g : 5 * g + 5] for g in range(3)], refs[15:]
        place = Place(rooms[0][0].shape[0])
        own = [
            pltpu.make_async_copy(source.at[:, :, place.core], room[0], own_sem.at[g])
            for g, (source, room) in enumerate(zip(sources, rooms))
        ]
        groups = [
            Scatter(place, source.at[:, :, 1 - place.core], room, send, recv, g)
            for g, (source, room) in enumerate(zip(sources, rooms))
        ]
        down, out, up = groups

        def begin():
            for copy in own:
                copy.start()
            meet(place)
            down.start(0)

        def first(k, go=True):
            own[k].wait()
            groups[k].fold(0, go)

        when(0, begin)
        when(1, lambda: (first(0), out.start(0), up.start(0)))
        when(3, lambda: (first(1, False), first(2, False)))
        when(6, lambda: down.fold(1))
        when(8, lambda: (out.start(1), up.start(1)))
        when(10, lambda: down.fold(2))

    @pl.when(step < turns)
    def _():
        row, pair = lax.div(step, pairs), lax.rem(step, pairs)
        pad_rows(keys, k_ref[0, 0])
        pad_rows(values, v_ref[0, 0])
        grad_keys[...] = jnp.zeros_like(grad_keys)
        grad_values[...] = jnp.zeros_like(grad_values)
        sums = [jnp.zeros((8, BLOCK), F32)] * 4
        cols = pl.ds(pl.multiple_of(pair * BLOCK, BLOCK), BLOCK)
        for b in range(tokens // BLOCK):
            lanes = slice(b * BLOCK, (b + 1) * BLOCK)
            window = slice(b * BLOCK, b * BLOCK + SPAN)
            queries = pair_rows(q_ref[0, 0, lanes, :] * 0.125)
            grads = pair_rows(grad_ref[0, lanes, :])
            probs_low = probs_ref[0, 0, b]
            back = nt(values[window, :], grads)
            dist = jnp.where(far_ref[0, b] < FAR, far_ref[0, b], 0.0)
            order = order_ref[0, b]
            sides = []
            for h in range(2):
                probs = probs_low[:, h * BLOCK : (h + 1) * BLOCK].astype(F32)
                part = back[:, h * BLOCK : (h + 1) * BLOCK]
                delta = jnp.sum(probs * part, axis=0, keepdims=True)
                scores = probs * (part - delta)
                sums[2 * h] = sums[2 * h] - fold(scores * dist)
                sums[2 * h + 1] = sums[2 * h + 1] + fold(scores * order)
                sides.append(scores.astype(LOW))
            scores_low = jnp.concatenate(sides, axis=1)
            grad_values[window, :] += nn(probs_low, grads)
            grad_keys[window, :] += nn(scores_low, queries)
            grad_queries = (pair_pick(tn(scores_low, keys[window, :])) * 0.125).astype(LOW)
            dq_ref[0, lanes, :] = grad_queries
            all_q[row, lanes, cols] = grad_queries
        dk = grad_keys[pl.ds(RADIUS, tokens), :].astype(LOW)
        dv = grad_values[pl.ds(RADIUS, tokens), :].astype(LOW)
        dk_ref[0], all_k[row, :, cols] = dk, dk
        dv_ref[0], all_v[row, :, cols] = dv, dv
        for k in range(4):
            rate_ref[0, 0, k] = sums[k]

    for k, ref in enumerate((all_q, all_k, all_v)):
        @pl.when(step == turns + k)
        def _(ref=ref):
            flat = lambda v: v.reshape(-1, v.shape[-1])
            grad_qkv_ref[...] = tn(flat(low_ref[...]), flat(ref[...])).astype(LOW)

    if remote:
        def last():
            copies = []
            for k, (group, part) in enumerate(zip((out, up), parts)):
                group.fold(1, go=False)
                for side, (y, x) in enumerate(((place.first_y, place.first_x), (place.y, place.x))):
                    copies.append(pltpu.make_async_copy(group.total.at[:, y, x], part.at[side], part_sem.at[2 * k + side]))
                    copies[-1].start()
            down_ref[...] = down.finish()
            down.sent()
            out.sent(2)
            up.sent(2)
            for copy in copies:
                copy.wait()

        when(turns + 2, last)


def attention_backward(remote, depth, qkv, grad, probs, far, order, low, sources):
    pairs, rows, tokens = qkv.shape[0] // 3, qkv.shape[1], qkv.shape[2]
    width = pairs * BLOCK
    blocks = tokens // BLOCK
    turns = rows * pairs
    where = lambda s: (jnp.minimum(s, turns - 1) // pairs, jnp.minimum(s, turns - 1) % pairs)
    row_of, pair_of = lambda s: where(s)[0], lambda s: where(s)[1]
    part = lambda k: pl.BlockSpec((1, 1, tokens, BLOCK), lambda s: (k * pairs + pair_of(s), row_of(s), 0, 0))
    flat = pl.BlockSpec((1, tokens, BLOCK), lambda s: (row_of(s), 0, pair_of(s)))
    bias = pl.BlockSpec((1, blocks, SPAN, BLOCK), lambda s: (row_of(s), 0, 0, 0))
    grads = jax.ShapeDtypeStruct((rows, tokens, width), LOW)
    in_specs = [part(0), part(1), part(2), flat]
    in_specs += [pl.BlockSpec((1, 1, blocks, SPAN, 2 * BLOCK), lambda s: where(s) + (0, 0, 0)), bias, bias, whole(low.shape)]
    out_specs = [flat] * 3 + [
        pl.BlockSpec((1, 1, 4, 8, BLOCK), lambda s: where(s) + (0, 0, 0)),
        pl.BlockSpec((width, width), lambda s: (0, jnp.clip(s - turns, 0, 2))),
    ]
    out_shape = [grads] * 3 + [
        jax.ShapeDtypeStruct((rows, pairs, 4, 8, BLOCK), F32),
        jax.ShapeDtypeStruct((width, 3 * width), LOW),
    ]
    scratch = [pltpu.VMEM((tokens + 2 * RADIUS, BLOCK), LOW)] * 2
    scratch += [pltpu.VMEM((tokens + 2 * RADIUS, BLOCK), F32)] * 2
    scratch += [pltpu.VMEM((rows, tokens, width), LOW)] * 3
    more = {}
    if remote:
        in_specs += [pl.BlockSpec(memory_space=pl.ANY)] * 3
        for k, source in enumerate(sources):
            shape = source.shape[4:]
            if k == 0:
                out_specs.append(pl.BlockSpec(shape, lambda s: (0, 0)))
                out_shape.append(jax.ShapeDtypeStruct(shape, F32))
            else:
                out_specs.append(pl.BlockSpec(memory_space=pl.ANY))
                out_shape.append(jax.ShapeDtypeStruct((2, depth) + shape, LOW))
            scratch += scatter_room(depth, *shape)
        scratch += [pltpu.SemaphoreType.DMA((3, depth + 3))] * 2 + [pltpu.SemaphoreType.DMA((3,)), pltpu.SemaphoreType.DMA((4,))]
        more = {"collective_id": CALLS["attention"], "has_side_effects": True}
    return pl.pallas_call(
        functools.partial(attention_back_kernel, remote, pairs),
        grid=(turns + 3,),
        in_specs=in_specs,
        out_specs=out_specs,
        out_shape=out_shape,
        scratch_shapes=scratch,
        compiler_params=params(1, **more),
        name="attention_backward",
    )(qkv, qkv, qkv, grad, probs, far, order, low, *(sources if remote else ()))


def graph_back_kernel(remote, *refs):
    (dq_in, dk_in, dv_in, two_in, unit_in, rstd_in, slope_in, hidden_in, agg2_in, agg1_in, x_in, adj_in, cols_in,
     first_in, second_in, qkv_w_in, gain_ref, late_ref, rate_ref) = refs[:19]
    refs = refs[19:]
    (qkv_source, *parts), refs = (refs[:3], refs[3:]) if remote else ((None,), refs)
    (input_grad_out, edge_out, gains_out, shifts_out, rates_out), refs = refs[:5], refs[5:]
    owned, refs = (refs[:7], refs[7:]) if remote else (refs[:2], refs[2:])
    (dq, dk, dv, two, unit, rstd, slope, hidden, agg2, adj, cols, first_w, second_w, qkv_w,
     back, norms, edge_sums, row_sem, in_sem, out_sem), refs = refs[:20], refs[20:]
    rows, tokens, width = dq.shape
    blocks, chunk = tokens // BLOCK, 2 * BLOCK
    chunks = tokens // chunk
    agg1, x, branch, mean, pre, one = agg2, hidden, dq, dk, dv, two

    by_row = [(dq_in, dq), (dk_in, dk), (dv_in, dv), (two_in, two), (unit_in, unit), (rstd_in, rstd)]
    row_load = lambda k, row: pltpu.make_async_copy(by_row[k][0].at[row], by_row[k][1].at[row], row_sem.at[k, row])
    once = [(qkv_w_in, qkv_w), (second_in, second_w), (cols_in, cols), (hidden_in, hidden), (agg2_in, agg2),
            (adj_in, adj), (slope_in, slope), (first_in, first_w), (x_in, x), (agg1_in, agg1)]
    load = lambda k: pltpu.make_async_copy(*once[k], in_sem.at[k])
    load(0).start()
    for k in range(len(by_row)):
        row_load(k, 0).start()
    load(1).start()
    load(2).start()
    for row in range(1, rows):
        for k in range(len(by_row)):
            row_load(k, row).start()
    for k in range(3, 8):
        load(k).start()

    if remote:
        rooms = [refs[5 * g : 5 * g + 5] for g in range(4)]
        sums, s_land, s_far, send, recv, own_sem, s_send, s_recv = refs[20:28]
        tails = (refs[28:31], refs[31:34])
        depth = rooms[0][0].shape[0]
        place = Place(depth)
        own = pltpu.make_async_copy(qkv_source.at[:, :, place.core], rooms[0][0], own_sem.at[0])
        qkv = Scatter(place, qkv_source.at[:, :, 1 - place.core], rooms[0], send, recv, 0)
        late, early, final = [
            Scatter(place, room[0].at[1], (room[0].at[0],) + tuple(room[1:]), send, recv, 1 + g)
            for g, room in enumerate(rooms[1:])
        ]
        out, up = [
            Tail(place, part, room, send, recv, own_sem, 4 + g)
            for g, (part, room) in enumerate(zip(parts, tails))
        ]
        own.start()
        out.load.start()
        up.load.start()
        meet(place)
        qkv.start(0)
        out.across.start()
        up.across.start()

    norms[...] = jnp.zeros_like(norms)
    edge_sums[...] = jnp.zeros_like(edge_sums)
    flat = lambda ref: ref[...].reshape(rows * tokens, width)

    def weight_grad(dest, col, left, right):
        half = width // 2
        for part in range(2):
            grad = tn(left[:, :, part * half : (part + 1) * half].reshape(rows * tokens, half), flat(right))
            if not remote:
                dest[part * half : (part + 1) * half, col * width : (col + 1) * width] = grad.astype(LOW)
                continue
            share = dest.shape[4]
            for k in range(half // share):
                index = part * (half // share) + k
                z, y, core, x_at = index // 8, index // 4 % 2, index // 2 % 2, index % 2
                side = place.core if core == 0 else 1 - place.core
                dest[side, z, y, x_at, :, col * width : (col + 1) * width] = grad[k * share : (k + 1) * share].astype(LOW)

    def spread(row, source):
        back[...] = jnp.zeros_like(back)
        for b in range(blocks):
            back[b * BLOCK : b * BLOCK + WIDE, :] += nn(adj[row, b], source[row, b * BLOCK : (b + 1) * BLOCK, :])

    load(0).wait()
    load(1).wait()
    load(2).wait()

    @pl.loop(0, rows)
    def _(row):
        for k in range(len(by_row)):
            row_load(k, row).wait()
        for c in range(chunks):
            part = slice(c * chunk, (c + 1) * chunk)
            grad = two[row, part, :]
            for k, ref in enumerate((dq, dk, dv)):
                grad = grad + nt(ref[row, part, :], qkv_w[:, k * width : (k + 1) * width])
            plain = unit[row, part, :].astype(F32)
            norms[0] += fold(grad * plain)
            norms[1] += fold(grad)
            grad = norm_back(grad, plain, rstd[row, part, :], gain_ref[0:1, :])
            one[row, part, :] = grad
            low = grad.astype(LOW)
            branch[row, part, :] = low
            mean[row, part, :] = (nt(low, second_w[:, width : 2 * width]) * cols[row, part, 2:3]).astype(LOW)
            if remote and c == 0:
                @pl.when(row == 0)
                def _():
                    own.wait()
                    qkv.fold(0)

    load(3).wait()
    load(4).wait()
    second_dest, first_dest = (rooms[1][0], rooms[2][0]) if remote else (owned[1], owned[0])
    weight_grad(second_dest, 0, hidden, branch)
    weight_grad(second_dest, 1, agg2, branch)
    load(8).start()
    load(9).start()
    if remote:
        late.start(0)
        out.fold()
        up.fold()
        qkv.fold(1)
    for k in range(5, 8):
        load(k).wait()

    @pl.loop(0, rows)
    def _(row):
        spread(row, mean)
        for c in range(chunks):
            part = slice(c * chunk, (c + 1) * chunk)
            grad = back[REACH + c * chunk : REACH + (c + 1) * chunk, :]
            grad = grad + nt(branch[row, part, :], second_w[:, 0:width])
            grad = grad * slope[row, part, :].astype(F32)
            edge_sums[0] += fold(grad * cols[row, part, 0:1])
            edge_sums[1] += fold(grad * cols[row, part, 1:2])
            low = grad.astype(LOW)
            pre[row, part, :] = low
            if remote and c == 0:
                @pl.when(row == 0)
                def _():
                    late.fold(0)
    load(8).wait()
    load(9).wait()
    weight_grad(first_dest, 0, x, pre)
    if remote:
        early.start(0)
    weight_grad(rooms[3][0] if remote else first_dest, 0 if remote else 1, agg1, pre)

    line = lambda v: jnp.sum(v, axis=0, keepdims=True)
    lines = jnp.concatenate(
        [line(edge_sums[0]), line(edge_sums[1]), line(norms[0]), line(late_ref[0]), line(late_ref[2]),
         line(norms[1]), line(late_ref[1]), line(late_ref[3])], axis=0,
    )
    rates = jnp.sum(jnp.sum(rate_ref[...], axis=0), axis=2).reshape(-1, BLOCK)

    if remote:
        final.start(0)
        early.fold(0)
        pieces = width // BLOCK
        for k in range(pieces):
            sums[0, k] = lines[:, k * BLOCK : (k + 1) * BLOCK]
        for k in range(3):
            sums[0, pieces + k] = rates[8 * k : 8 * (k + 1)]
        turns = [
            (sums.at[k], s_land.at[k], k, device)
            for k, device in enumerate((
                place.at(place.z, place.y, 1 - place.core, place.x),
                place.at(place.z, place.y, place.core, 1 - place.x),
                place.at(place.z, 1 - place.y, place.core, place.x),
            ))
        ] + [
            (s_far.at[place.z], s_far.at[place.z], 2 + k, place.at(place.along(k), place.y, place.core, place.x))
            for k in range(1, depth)
        ]
        turns = [
            pltpu.make_async_remote_copy(
                src_ref=source, dst_ref=land, send_sem=s_send.at[slot], recv_sem=s_recv.at[slot],
                device_id=device, device_id_type=pl.DeviceIdType.MESH,
            )
            for source, land, slot, device in turns
        ]
        turns[0].start()
        qkv.fold(2)
        late.fold(1)

    writes = lambda row: pltpu.make_async_copy(one.at[row], input_grad_out.at[row], out_sem.at[row])

    @pl.loop(0, rows)
    def _(row):
        for c in range(chunks):
            part = slice(c * chunk, (c + 1) * chunk)
            mean[row, part, :] = (nt(pre[row, part, :], first_w[:, width : 2 * width]) * cols[row, part, 2:3]).astype(LOW)
        if remote:
            @pl.when(row == 0)
            def _():
                final.fold(0)
                turns[0].wait_recv()
                sums[1] = sums[0] + s_land[0]
                turns[1].start()
        spread(row, mean)
        for c in range(chunks):
            part = slice(c * chunk, (c + 1) * chunk)
            grad = one[row, part, :] + back[REACH + c * chunk : REACH + (c + 1) * chunk, :]
            one[row, part, :] = grad + nt(pre[row, part, :], first_w[:, 0:width])
        writes(row).start()
        if remote:
            @pl.when(row == 0)
            def _():
                early.fold(1)

    if remote:
        turns[1].wait_recv()
        sums[2] = sums[1] + s_land[1]
        turns[2].start()
        late.fold(2)
        final.fold(1)
        early.fold(2)
        turns[2].wait_recv()
        s_far[place.z] = sums[2] + s_land[2]
        for turn in turns[3:]:
            turn.start()
        owned[5][...] = out.finish()
        owned[6][...] = up.finish()
        owned[4][...] = qkv.finish()
        final.fold(2)
        result = late.finish()
        owned[2][...] = result[:, :width]
        owned[3][...] = result[:, width:]
        for turn in turns[3:]:
            turn.wait_recv()
        total = s_far[0]
        for k in range(1, depth):
            total = total + s_far[k]
        for k in range(pieces):
            part = slice(k * BLOCK, (k + 1) * BLOCK)
            edge_out[:, part] = total[k, 0:2]
            gains_out[:, part] = total[k, 2:5]
            shifts_out[:, part] = total[k, 5:8]
        for k in range(3):
            rates_out[8 * k : 8 * (k + 1)] = jnp.sum(total[pieces + k], axis=1, keepdims=True)
        owned[0][...] = early.finish()
        owned[1][...] = final.finish()
        for group in (qkv, late, early, final):
            group.sent()
        for turn in turns:
            turn.wait_send()
    else:
        edge_out[...], gains_out[...], shifts_out[...] = lines[0:2], lines[2:5], lines[5:8]
        rates_out[...] = jnp.sum(rates, axis=1, keepdims=True)
    for row in range(rows):
        writes(row).wait()


def graph_backward(remote, depth, arrays, gains, late, rates, sources):
    dq, two, unit, rstd, slope, hidden, adj, cols = (arrays[k] for k in (0, 3, 4, 5, 6, 7, 11, 12))
    rows, tokens, width = dq.shape
    vmem, hbm = pl.BlockSpec(memory_space=pltpu.VMEM), pl.BlockSpec(memory_space=pl.ANY)
    shape = lambda dtype, *dims: jax.ShapeDtypeStruct(dims, dtype)
    out_shape = [
        shape(F32, rows, tokens, width), shape(F32, 2, width), shape(F32, 3, width), shape(F32, 3, width),
        shape(F32, rates.shape[1] * 4, 1),
    ]
    like = lambda v: pltpu.VMEM(v.shape, v.dtype)
    scratch = [like(v) for v in (dq, dq, dq, two, unit, rstd, slope, hidden, hidden, adj, cols) + tuple(arrays[13:16])]
    scratch += [
        pltpu.VMEM((tokens + 2 * REACH, width), F32),
        pltpu.VMEM((2, 8, width), F32),
        pltpu.VMEM((2, 8, width), F32),
        pltpu.SemaphoreType.DMA((6, rows)),
        pltpu.SemaphoreType.DMA((10,)),
        pltpu.SemaphoreType.DMA((rows,)),
    ]
    more = {}
    if remote:
        share = sources[0].shape[4]
        out_shape += [shape(F32, share, width)] * 4 + [shape(F32, share, s.shape[-1]) for s in sources]
        scratch += scatter_room(depth, share, sources[0].shape[5])
        for cols in (2 * width, width, width):
            scratch += scatter_room(depth, share, cols, (2,))
        lines = (width // BLOCK + 3, 8, BLOCK)
        scratch += [pltpu.VMEM((3,) + lines, F32), pltpu.VMEM((3,) + lines, F32), pltpu.VMEM((depth,) + lines, F32)]
        scratch += [pltpu.SemaphoreType.DMA((6, depth + 3))] * 2 + [pltpu.SemaphoreType.DMA((6,))]
        scratch += [pltpu.SemaphoreType.DMA((depth + 2,))] * 2
        for part in sources[1:]:
            scratch += [pltpu.VMEM((k, share, part.shape[3]), LOW) for k in (depth, depth, depth - 1)]
        more = {"collective_id": CALLS["graph"], "has_side_effects": True}
    else:
        out_shape += [shape(LOW, width, 2 * width)] * 2
    return pl.pallas_call(
        functools.partial(graph_back_kernel, remote),
        in_specs=[hbm] * 16 + [vmem] * 3 + [hbm] * (3 if remote else 0),
        out_specs=[hbm] + [vmem] * (len(out_shape) - 1),
        out_shape=out_shape,
        scratch_shapes=scratch,
        compiler_params=pltpu.CompilerParams(vmem_limit_bytes=VMEM, **more),
        name="graph_backward",
    )(*arrays, gains, late, rates, *(sources if remote else ()))


def local(
    sizes, inputs, coords, neighbours, counts, doc_length, self_one, near_one, self_two, near_two, edge_proj,
    qkv_proj, out_proj, up_proj, down_proj, norm_gains, norm_shifts, distance_rate, order_rate, cotangent,
):
    axes = ("wide", "narrow")
    rows, tokens, width = inputs.shape
    wide_size, narrow_size = sizes
    depth = wide_size // 4
    remote = wide_size % 4 == 0 and narrow_size == 2 and self_one.shape[0] % 8 == 0
    weights, shards = (self_one, near_one, self_two, near_two, qkv_proj), (out_proj, up_proj, down_proj)
    gather = lambda v: lax.all_gather(v, axes, axis=0, tiled=True)
    scatter = lambda v: lax.psum_scatter(v, axes, scatter_dimension=0, tiled=True).astype(F32)
    blocked = lambda v: v.reshape(depth, 2, 2, 2, -1, v.shape[1])
    flat = lambda v: v.reshape(rows * tokens, width)
    tall = lambda v: v.reshape(rows, tokens, width)
    if not remote:
        weights, shards = tuple(map(gather, weights)), tuple(map(gather, shards))
    results = front(
        remote, depth, doc_length[:, 0], distance_rate, order_rate, neighbours, counts[:, None, :], coords, inputs,
        edge_proj, norm_gains, norm_shifts, weights, shards if remote else (),
    )
    (adj, cols, agg1, slope, hidden, agg2, unit, rstd, normed, low, qkv, att, probs, far, order, first_w, second_w, qkv_w) = results[:18]
    out_w, up = (v.reshape(-1, v.shape[-1]) for v in results[18:20]) if remote else shards[:2]
    result, two, grad_att, grad_out, grad_up, grad_down, late = block_both(
        remote, depth, att.reshape(-1, rows * tokens, BLOCK), flat(normed), flat(cotangent), out_w, up, results[20] if remote else shards[2],
        norm_gains, norm_shifts,
    )
    first_sources = (blocked(grad_down), blocked(grad_out), blocked(grad_up)) if remote else ()
    dq, dk, dv, rates, grad_qkv, *summed = attention_backward(
        remote, depth, qkv, tall(grad_att), probs, far, order, low, first_sources
    )
    arrays = (dq, dk, dv, tall(two), unit, rstd, slope, hidden, agg2, agg1, inputs, adj, cols, first_w, second_w, qkv_w)
    sources = (blocked(grad_qkv), summed[1], summed[2]) if remote else ()
    input_grad, edge, gains, shifts, rates, *owned = graph_backward(remote, depth, arrays, norm_gains, late, rates, sources)
    if remote:
        down_own = summed[0]
        self1, near1, self2, near2, qkv_own, out_own, up_own = owned
    else:
        down_own, out_own, up_own, qkv_own = map(scatter, (grad_down, grad_out, grad_up, grad_qkv))
        self1, near1 = jnp.split(scatter(owned[0]), 2, axis=1)
        self2, near2 = jnp.split(scatter(owned[1]), 2, axis=1)
        edge, gains, shifts, rates = lax.psum((edge, gains, shifts, rates), axes)
    rates = rates.reshape(-1, 2, 2)
    return (
        tall(result), input_grad, self1, near1, self2, near2, edge, qkv_own, out_own, up_own, down_own, gains, shifts,
        rates[:, :, 0].reshape(-1), rates[:, :, 1].reshape(-1),
    )


def solution(mesh):
    axes = ("wide", "narrow")
    middle, last = P(None, axes, None), P(None, None, axes)
    count, weight, same = P(None, axes), P(axes, None), P()
    sizes = (mesh.shape["wide"], mesh.shape["narrow"])
    return jax.shard_map(
        functools.partial(local, sizes),
        mesh=mesh,
        in_specs=(middle, last, last, count, count)
        + (weight,) * 4
        + (same,)
        + (weight,) * 4
        + (same,) * 4
        + (middle,),
        out_specs=(middle, middle) + (weight,) * 4 + (same,) + (weight,) * 4 + (same,) * 4,
        check_vma=False,
    )
```

```python
import functools
import jax
import jax.numpy as jnp
from jax import lax
from jax.experimental import pallas as pl
from jax.experimental.pallas import tpu as pltpu
from jax.sharding import PartitionSpec as P

RADIUS = 128
REACH = 64
BLOCK = 128
WIDE = BLOCK + 2 * REACH
SPAN = BLOCK + 2 * RADIUS
FAR = 1e10
F32 = jnp.float32
LOW = jnp.bfloat16
VMEM = 62 * 2**20
CALLS = {"front": 0, "block": 1, "attention": 2, "graph": 3}


def dot(left, right, dims):
    return lax.dot_general(left, right, ((dims[:1], dims[1:]), ((), ())), preferred_element_type=F32)


def nn(left, right):
    return dot(left, right, (1, 0))


def nt(left, right):
    return dot(left, right, (1, 1))


def tn(left, right):
    return dot(left, right, (0, 0))


def gelu_pair(pre):
    slope = 0.7978845608028654
    square = pre * pre
    half = 0.5 + 0.5 * jnp.tanh(pre * (slope + (slope * 0.044715) * square))
    act = pre * half
    deriv = half + act * (1.0 - half) * (2.0 * slope + (6.0 * slope * 0.044715) * square)
    return act, deriv


def norm_parts(values):
    centre = values - jnp.mean(values, axis=-1, keepdims=True)
    rstd = lax.rsqrt(jnp.mean(centre * centre, axis=-1, keepdims=True) + 1e-05)
    return centre * rstd, rstd


def norm_back(grad, unit, rstd, gain):
    scaled = grad * gain
    mean = jnp.mean(scaled, axis=-1, keepdims=True)
    along = jnp.mean(scaled * unit, axis=-1, keepdims=True)
    return rstd * (scaled - mean - unit * along)


def fold(values):
    rows, cols = values.shape
    return jnp.sum(values.reshape(rows // 8, 8, cols), axis=0)


def whole(shape, space=None):
    return pl.BlockSpec(shape, lambda *_: (0,) * len(shape), pipeline_mode=pl.Buffered(1))


def params(grid_rank, **more):
    return pltpu.CompilerParams(
        vmem_limit_bytes=VMEM, dimension_semantics=("arbitrary",) * grid_rank, **more
    )


def fill_bias(length, point_ref, far_ref, order_ref, row):
    tokens = point_ref.shape[2]
    side = jnp.zeros((2, RADIUS), F32)
    padded = jnp.concatenate([side, point_ref[row], side], axis=1)
    tall = jnp.concatenate([padded, jnp.zeros((6, tokens + 2 * RADIUS), F32)], axis=0)
    for b in range(tokens // BLOCK):
        window = tall[:, b * BLOCK : b * BLOCK + SPAN].T
        key_x, key_y = window[:, 0:1], window[:, 1:2]
        lanes = slice(b * BLOCK, (b + 1) * BLOCK)
        delta_x = key_x - point_ref[row, 0:1, lanes]
        delta_y = key_y - point_ref[row, 1:2, lanes]
        dist = jnp.log(1.0 + 16.0 * (delta_x * delta_x + delta_y * delta_y))
        query = lax.broadcasted_iota(jnp.int32, (SPAN, BLOCK), 1) + b * BLOCK
        key = lax.broadcasted_iota(jnp.int32, (SPAN, BLOCK), 0) + (b * BLOCK - RADIUS)
        allowed = (jnp.abs(query - key) <= RADIUS) & ((query >= length) == (key >= length))
        allowed = allowed & (key >= 0) & (key < tokens)
        far_ref[row, b] = jnp.where(allowed, dist, FAR)
        order_ref[row, b] = jnp.tanh(4.0 * delta_x)


def pair_rows(values):
    lane = lax.broadcasted_iota(jnp.int32, values.shape, 1)
    zero = jnp.zeros_like(values)
    first = jnp.where(lane < BLOCK // 2, values, zero)
    second = jnp.where(lane < BLOCK // 2, zero, values)
    return jnp.concatenate([first, second], axis=0)


def pair_pick(values):
    lane = lax.broadcasted_iota(jnp.int32, (BLOCK, BLOCK), 1)
    return jnp.where(lane < BLOCK // 2, values[:BLOCK], values[BLOCK:])


def pad_rows(pad_ref, values):
    tokens = values.shape[0]
    zeros = jnp.zeros((RADIUS, values.shape[1]), pad_ref.dtype)
    pad_ref[pl.ds(0, RADIUS), :] = zeros
    pad_ref[pl.ds(RADIUS + tokens, RADIUS), :] = zeros
    pad_ref[pl.ds(RADIUS, tokens), :] = values


FIRST, OWN, PASSED, SIBLING = 0, 1, 2, 3


class Place:
    def __init__(self, depth):
        self.depth = depth
        wide, self.x = lax.axis_index("wide"), lax.axis_index("narrow")
        self.core = lax.rem(wide, 2)
        self.y = lax.rem(lax.div(wide, 2), 2)
        self.z = lax.div(wide, 4)
        core, y, x = self.core, self.y, self.x
        self.first_y = (1 - core) * (1 - y) + core * y
        self.first_x = core * (1 - x) + (1 - core) * x
        self.second_y = core * (1 - y) + (1 - core) * y
        self.second_x = (1 - core) * (1 - x) + core * x

    def at(self, z, y, core, x):
        return ((z * 2 + y) * 2 + core, x)

    def along(self, k):
        return lax.rem(self.z + k, self.depth)

    def partners(self):
        along = [self.at(self.along(k), self.y, self.core, self.x) for k in range(1, self.depth)]
        return along + [
            self.at(self.z, self.first_y, self.core, self.first_x),
            self.at(self.z, self.second_y, self.core, self.second_x),
            self.at(self.z, self.y, 1 - self.core, self.x),
        ]


def meet(place):
    barrier = pltpu.get_barrier_semaphore()
    partners = place.partners()
    for partner in partners:
        pl.semaphore_signal(barrier, inc=1, device_id=partner, device_id_type=pl.DeviceIdType.MESH)
    pl.semaphore_wait(barrier, len(partners))


class Gather:
    def __init__(self, place, land, send, recv, group):
        self.place, self.land, self.send, self.recv, self.group = place, land, send, recv, group

    def copy(self, view, slot, device):
        return pltpu.make_async_remote_copy(
            src_ref=view, dst_ref=view, send_sem=self.send.at[self.group, slot], recv_sem=self.recv.at[self.group, slot],
            device_id=device, device_id_type=pl.DeviceIdType.MESH,
        )

    def pieces(self, stage):
        p, land = self.place, self.land
        base = p.depth - 1
        mine = land.at[:, p.y, p.core, p.x]
        if stage == "along":
            here = land.at[p.z, p.y, p.core, p.x]
            found = []
            for k in range(1, p.depth):
                there = land.at[p.along(p.depth - k), p.y, p.core, p.x]
                found.append((here, there, k - 1, p.at(p.along(k), p.y, p.core, p.x)))
            return found
        first = p.at(p.z, p.first_y, p.core, p.first_x)
        second = p.at(p.z, p.second_y, p.core, p.second_x)
        if stage == FIRST:
            return [(mine, land.at[:, p.first_y, p.core, p.first_x], base, first)]
        if stage == OWN:
            return [(mine, land.at[:, p.second_y, p.core, p.second_x], base + 1, second)]
        if stage == PASSED:
            return [(land.at[:, p.first_y, p.core, p.first_x], land.at[:, 1 - p.y, p.core, 1 - p.x], base + 2, second)]
        return [(land.at[:, :, p.core], land.at[:, :, 1 - p.core], base + 3, p.at(p.z, p.y, 1 - p.core, p.x))]

    def start(self, *stages):
        for stage in stages:
            for leaves, _, slot, device in self.pieces(stage):
                self.copy(leaves, slot, device).start()

    def arrive(self, *stages):
        for stage in stages:
            for _, arrives, slot, device in self.pieces(stage):
                self.copy(arrives, slot, device).wait_recv()

    def sent(self, *stages):
        for stage in stages or ("along", FIRST, OWN, PASSED, SIBLING):
            for leaves, _, slot, device in self.pieces(stage):
                self.copy(leaves, slot, device).wait_send()


def merge_rows(full, land):
    depth, rows = land.shape[0], land.shape[4]

    @pl.loop(0, depth * 4)
    def _(k):
        z, y, core = lax.div(k, 4), lax.rem(lax.div(k, 2), 2), lax.rem(k, 2)
        pair = jnp.concatenate([land[z, y, core, 0].astype(F32), land[z, y, core, 1].astype(F32)], axis=0)
        full[pl.ds(pl.multiple_of(k * 2 * rows, 16), 2 * rows), :] = pair.astype(LOW)


def front_kernel(remote, *refs):
    (length_ref, dist_rate_ref, order_rate_ref, near_ref, count_ref, point_ref, x_ref, edge_w_ref, gain_ref, shift_ref,
     self1_ref, near1_ref, self2_ref, near2_ref, qkv_w_ref) = refs[:15]
    refs = refs[15:]
    shards, refs = (refs[:3], refs[3:]) if remote else ((), refs)
    outs, refs = refs[:18], refs[18:]
    fulls, refs = (refs[:3], refs[3:]) if remote else ((), refs)
    (adj, cols, agg1, slope, hidden, agg2, unit, rstd, normed, low, qkv, att, probs, far, order,
     first_w, second_w, third_w, pad, point_pad, rel, keys, values, out_sem, probs_sem, in_sem) = refs[:26]
    rows, slots, tokens = near_ref.shape
    width = x_ref.shape[2]
    pairs = width // BLOCK
    blocks = tokens // BLOCK
    chunk = 2 * BLOCK

    writes = {}

    def write(k, source, dest=None):
        writes[k] = pltpu.make_async_copy(source, outs[k] if dest is None else dest, out_sem.at[k])
        writes[k].start()

    if remote:
        land_a, land_b, land_q, send, recv = refs[26:]
        place = Place(land_a.shape[0])
        lands = (land_a, land_b, land_q) + tuple(fulls)
        groups = [Gather(place, land, send, recv, g) for g, land in enumerate(lands)]
        ga, gb, gq, go, gu, gd = groups
        column = lambda land, k: land.at[place.z, place.y, place.core, place.x, :, pl.ds(k * width, width)]
        own = lambda land: land.at[place.z, place.y, place.core, place.x]
        loads = [
            [pltpu.make_async_copy(ref, column(land_a, k), in_sem.at[k]) for k, ref in enumerate((self1_ref, near1_ref))],
            [pltpu.make_async_copy(ref, column(land_b, k), in_sem.at[2 + k]) for k, ref in enumerate((self2_ref, near2_ref))],
            [pltpu.make_async_copy(qkv_w_ref, own(land_q), in_sem.at[4])],
        ] + [[pltpu.make_async_copy(ref, own(full), in_sem.at[5 + k])] for k, (ref, full) in enumerate(zip(shards, fulls))]
        for load in loads:
            for copy in load:
                copy.start()
        meet(place)

        def begin(g):
            for copy in loads[g]:
                copy.wait()
            groups[g].start("along")

        begin(0)
    else:
        loads = [
            pltpu.make_async_copy(ref, dest, in_sem.at[k])
            for k, (ref, dest) in enumerate((
                (self1_ref, first_w.at[:, pl.ds(0, width)]), (near1_ref, first_w.at[:, pl.ds(width, width)]),
                (self2_ref, second_w.at[:, pl.ds(0, width)]), (near2_ref, second_w.at[:, pl.ds(width, width)]),
                (qkv_w_ref, third_w),
            ))
        ]
        for copy in loads:
            copy.start()

    side = jnp.zeros((REACH, width), LOW)
    pad[pl.ds(0, REACH), :] = side
    pad[pl.ds(tokens + REACH, REACH), :] = side

    @pl.loop(0, rows)
    def _(row):
        length = length_ref[row]
        pad[pl.ds(REACH, tokens), :] = x_ref[row]
        points = point_ref[row]
        high = points.astype(LOW).astype(F32)
        mid = (points - high).astype(LOW).astype(F32)
        tail = points - high - mid
        split = jnp.concatenate([high, mid, tail, jnp.ones((1, tokens), F32), jnp.zeros((9, tokens), F32)], axis=0)
        edge_side = jnp.zeros((16, REACH), F32)
        point_pad[...] = jnp.concatenate([edge_side, split, edge_side], axis=1).astype(LOW)

        @pl.loop(0, blocks)
        def _(b):
            start = pl.multiple_of(b * BLOCK, BLOCK)
            lanes = pl.ds(start, BLOCK)
            near = near_ref[row, :, lanes]
            count = count_ref[row, :, lanes]
            spot = lax.broadcasted_iota(jnp.int32, (1, BLOCK), 1) + start
            slot = lax.broadcasted_iota(jnp.int32, (slots, BLOCK), 0)
            same = (near >= length) == (spot >= length)
            rel[...] = jnp.where((slot < count) & same, near - (start - REACH), -1)
            target = lax.broadcasted_iota(jnp.int32, (WIDE, BLOCK), 0)
            total = jnp.zeros((WIDE, BLOCK), F32)
            for s in range(slots):
                total = total + jnp.where(rel[s : s + 1, :] == target, 1.0, 0.0)
            band = total.astype(LOW)
            adj[row, b] = band
            sums = nn(point_pad[:, pl.ds(start, WIDE)], band)
            inverse = 1.0 / count.astype(F32)
            here = point_ref[row, :, lanes]
            edge = (sums[0:2] + sums[2:4] + sums[4:6] - sums[6:7] * here) * inverse
            lines = jnp.concatenate([edge, inverse, jnp.zeros((5, BLOCK), F32)], axis=0).T
            cols[row, lanes, :] = lines
            agg = tn(band, pad[pl.ds(start, WIDE), :])
            agg1[row, lanes, :] = (agg * lines[:, 2:3]).astype(LOW)

        if remote:
            @pl.when(row == 0)
            def _():
                ga.arrive("along")
                ga.start(FIRST, OWN)
                begin(1)

    write(0, adj)
    write(1, cols)
    write(2, agg1)
    if remote:
        ga.arrive(FIRST)
        ga.start(PASSED)
        gb.arrive("along")
        gb.start(FIRST, OWN)
        begin(2)

    @pl.loop(0, rows)
    def _(row):
        fill_bias(length_ref[row], point_ref, far, order, row)

    write(13, far)
    write(14, order)
    if remote:
        ga.arrive(OWN, PASSED)
        ga.start(SIBLING)
        gb.arrive(FIRST)
        gb.start(PASSED)
        ga.arrive(SIBLING)
        merge_rows(first_w, land_a)
    else:
        for copy in loads:
            copy.wait()
        write(16, second_w)
        write(17, third_w)
    write(15, first_w)

    @pl.loop(0, rows)
    def _(row):
        for c in range(tokens // chunk):
            part = slice(c * chunk, (c + 1) * chunk)
            pre = nn(x_ref[row, part, :], first_w[:, 0:width])
            pre = pre + nn(agg1[row, part, :], first_w[:, width : 2 * width])
            pre = pre + cols[row, part, 0:1] * edge_w_ref[0:1, :] + cols[row, part, 1:2] * edge_w_ref[1:2, :]
            act, deriv = gelu_pair(pre)
            slope[row, part, :] = deriv.astype(LOW)
            hidden[row, part, :] = act.astype(LOW)
            pad[REACH + c * chunk : REACH + (c + 1) * chunk, :] = act.astype(LOW)
        for b in range(blocks):
            lanes = slice(b * BLOCK, (b + 1) * BLOCK)
            agg = tn(adj[row, b], pad[b * BLOCK : b * BLOCK + WIDE, :])
            agg2[row, lanes, :] = (agg * cols[row, lanes, 2:3]).astype(LOW)
        if remote:
            @pl.when(row == 0)
            def _():
                gb.arrive(OWN, PASSED)
                gb.start(SIBLING)
                gq.arrive("along")
                gq.start(FIRST, OWN)
                begin(3)
                begin(4)

    write(3, slope)
    write(4, hidden)
    write(5, agg2)
    if remote:
        gb.arrive(SIBLING)
        merge_rows(second_w, land_b)
        write(16, second_w)

    @pl.loop(0, rows)
    def _(row):
        for c in range(tokens // chunk):
            part = slice(c * chunk, (c + 1) * chunk)
            resid = x_ref[row, part, :].astype(F32) + nn(hidden[row, part, :], second_w[:, 0:width])
            resid = resid + nn(agg2[row, part, :], second_w[:, width : 2 * width])
            plain, scale = norm_parts(resid)
            unit[row, part, :] = plain.astype(LOW)
            rstd[row, part, :] = scale
            out = plain * gain_ref[0:1, :] + shift_ref[0:1, :]
            normed[row, part, :] = out
            low[row, part, :] = out.astype(LOW)
        if remote:
            @pl.when(row == 0)
            def _():
                gq.arrive(FIRST)
                gq.start(PASSED)
                for g in (go, gu):
                    g.arrive("along")
                    g.start(FIRST, OWN)
                begin(5)

    write(6, unit)
    write(7, rstd)
    write(8, normed)
    write(9, low)
    if remote:
        gq.arrive(OWN, PASSED)
        gq.start(SIBLING)
        gq.arrive(SIBLING)
        merge_rows(third_w, land_q)
        write(17, third_w)

    @pl.loop(0, rows)
    def _(row):
        for c in range(tokens // chunk):
            part = slice(c * chunk, (c + 1) * chunk)
            out = nn(low[row, part, :], third_w[...]).astype(LOW)
            for k in range(3 * pairs):
                qkv[k, row, part, :] = out[:, k * BLOCK : (k + 1) * BLOCK]

    write(10, qkv)
    zeros = jnp.zeros((RADIUS, BLOCK), LOW)
    for ref in (keys, values):
        ref[pl.ds(0, RADIUS), :] = zeros
        ref[pl.ds(RADIUS + tokens, RADIUS), :] = zeros

    @pl.loop(0, rows * pairs)
    def _(turn):
        row, pair, slot = lax.div(turn, pairs), lax.rem(turn, pairs), lax.rem(turn, 2)
        if remote:
            @pl.when(turn == 1)
            def _():
                for g in (go, gu):
                    g.arrive(FIRST)
                    g.start(PASSED)
                gd.arrive("along")
                gd.start(FIRST, OWN)

            @pl.when(turn == 8)
            def _():
                for g in (go, gu):
                    g.arrive(OWN, PASSED)
                    g.start(SIBLING)

        def probs_copy(t, s):
            return pltpu.make_async_copy(
                probs.at[s], outs[12].at[lax.div(t, pairs), lax.rem(t, pairs)], probs_sem.at[s]
            )

        @pl.when(turn >= 2)
        def _():
            probs_copy(turn - 2, slot).wait()

        keys[pl.ds(RADIUS, tokens), :] = qkv[pairs + pair, row]
        values[pl.ds(RADIUS, tokens), :] = qkv[2 * pairs + pair, row]
        for b in range(blocks):
            lanes = slice(b * BLOCK, (b + 1) * BLOCK)
            window = slice(b * BLOCK, b * BLOCK + SPAN)
            queries = pair_rows(qkv[pair, row, lanes, :] * 0.125)
            raw = nt(keys[window, :], queries)
            sides = []
            for h in range(2):
                bias = order_rate_ref[2 * pair + h] * order[row, b] - dist_rate_ref[2 * pair + h] * far[row, b]
                scores = raw[:, h * BLOCK : (h + 1) * BLOCK] + bias
                grown = jnp.exp(scores - jnp.max(scores, axis=0, keepdims=True))
                scale = 1.0 / jnp.sum(grown, axis=0, keepdims=True)
                sides.append((grown * scale).astype(LOW))
            both = jnp.concatenate(sides, axis=1)
            probs[slot, b] = both
            att[pair, row, lanes, :] = pair_pick(tn(both, values[window, :])).astype(LOW)
        probs_copy(turn, slot).start()

    last = rows * pairs
    for turn in (last - 2, last - 1):
        pltpu.make_async_copy(probs.at[turn % 2], outs[12].at[turn // pairs, turn % pairs], probs_sem.at[turn % 2]).wait()
    write(11, att)
    if remote:
        for g in (go, gu):
            g.arrive(SIBLING)
        gd.arrive(FIRST, OWN)
        for g in groups[:5]:
            g.sent()
        gd.sent("along", FIRST, OWN)
    for copy in writes.values():
        copy.wait()


def front(remote, depth, length, dist_rate, order_rate, near, count, point, x, edge_w, gains, shifts, weights, shards):
    rows, tokens, width = x.shape
    slots = near.shape[1]
    blocks, pairs = tokens // BLOCK, width // BLOCK
    smem, vmem, hbm = (pl.BlockSpec(memory_space=s) for s in (pltpu.SMEM, pltpu.VMEM, pl.ANY))
    each = lambda dtype, *shape: ((rows,) + shape, dtype)
    kept = [
        each(LOW, blocks, WIDE, BLOCK),
        each(F32, tokens, 8),
        each(LOW, tokens, width),
        each(LOW, tokens, width),
        each(LOW, tokens, width),
        each(LOW, tokens, width),
        each(LOW, tokens, width),
        each(F32, tokens, 1),
        each(F32, tokens, width),
        each(LOW, tokens, width),
        ((3 * pairs, rows, tokens, BLOCK), LOW),
        ((pairs, rows, tokens, BLOCK), LOW),
        each(LOW, pairs, blocks, SPAN, 2 * BLOCK),
        each(F32, blocks, SPAN, BLOCK),
        each(F32, blocks, SPAN, BLOCK),
        ((width, 2 * width), LOW),
        ((width, 2 * width), LOW),
        ((width, 3 * width), LOW),
    ]
    out_shape = [jax.ShapeDtypeStruct(*k) for k in kept]
    kept[12] = ((2, blocks, SPAN, 2 * BLOCK), LOW)
    scratch = [pltpu.VMEM(*k) for k in kept]
    scratch += [
        pltpu.VMEM((tokens + 2 * REACH, width), LOW),
        pltpu.VMEM((16, tokens + 2 * REACH), LOW),
        pltpu.VMEM((slots, BLOCK), jnp.int32),
        pltpu.VMEM((tokens + 2 * RADIUS, BLOCK), LOW),
        pltpu.VMEM((tokens + 2 * RADIUS, BLOCK), LOW),
        pltpu.SemaphoreType.DMA((18,)),
        pltpu.SemaphoreType.DMA((2,)),
        pltpu.SemaphoreType.DMA((8,)),
    ]
    more = {}
    if remote:
        blocked = lambda shape: (depth, 2, 2, 2) + shape
        out_shape += [jax.ShapeDtypeStruct(blocked(s.shape), LOW) for s in shards]
        share = weights[0].shape[0]
        scratch += [pltpu.VMEM(blocked((share, k * width)), LOW) for k in (2, 2, 3)]
        scratch += [pltpu.SemaphoreType.DMA((6, depth + 3))] * 2
        more = {"collective_id": CALLS["front"], "has_side_effects": True}
    return pl.pallas_call(
        functools.partial(front_kernel, remote),
        in_specs=[smem] * 3 + [vmem] * 7 + [hbm] * (len(weights) + len(shards)),
        out_specs=[hbm] * len(out_shape),
        out_shape=out_shape,
        scratch_shapes=scratch,
        compiler_params=pltpu.CompilerParams(vmem_limit_bytes=VMEM, **more),
        name="front",
    )(length, dist_rate, order_rate, near, count, point, x, edge_w, gains, shifts, *weights, *shards)


TILE = 512


def block_kernel(remote, steps, *refs):
    (att_ref, normed_in, cot_ref, out_w_ref, up_in, down_in, gain_ref, shift_ref,
     result_ref, two_out, grad_att_ref, grad_out_out, grad_up_ref, grad_down_ref, norms_ref,
     act_all, up_all, second_all, down_all, attn_all, normed_all, unit_all, rstd_all, down_w, up_ref, in_sem, normed_sem, up_sem, out_sem) = refs[:29]
    step = pl.program_id(0)
    turns, tokens, half = act_all.shape
    parts, piece = turns // 2, 2 * half
    width = normed_all.shape[1]
    tile = lambda k: pl.ds(pl.multiple_of(k * TILE, TILE), TILE)
    load_normed = lambda k: pltpu.make_async_copy(normed_in.at[tile(k)], normed_all.at[tile(k)], normed_sem.at[k])
    chunk = lambda c: (slice(None), pl.ds(c * piece, piece))
    load_up = [pltpu.make_async_copy(up_in.at[chunk(c)], up_ref.at[chunk(c)], up_sem.at[c]) for c in range(parts)]
    write_two = pltpu.make_async_copy(normed_all, two_out, out_sem.at[0])
    write_out = pltpu.make_async_copy(unit_all.at[pl.ds(0, width)], grad_out_out, out_sem.at[1])

    if remote:
        send, recv = refs[29:]
        place = Place(parts)
        mine, first, second, last = [
            down_w.at[:, y, place.core, x]
            for y, x in (
                (place.y, place.x), (place.first_y, place.first_x), (place.second_y, place.second_x), (1 - place.y, 1 - place.x)
            )
        ]
        loads = [
            pltpu.make_async_copy(down_in.at[:, y, place.core, x], view, in_sem.at[1 + k])
            for k, (y, x, view) in enumerate((
                (place.y, place.x, mine), (place.first_y, place.first_x, first), (place.second_y, place.second_x, second)
            ))
        ]

        def copy(view, slot, device):
            return pltpu.make_async_remote_copy(
                src_ref=view, dst_ref=view, send_sem=send.at[slot], recv_sem=recv.at[slot],
                device_id=device, device_id_type=pl.DeviceIdType.MESH,
            )

        partner = place.at(place.z, place.second_y, place.core, place.second_x)
        sibling = place.at(place.z, place.y, 1 - place.core, place.x)
        pass_on, arriving = copy(first, 4, partner), copy(last, 4, partner)
        across = [copy(view, k, sibling) for k, view in enumerate((mine, first, second, last))]
        theirs = [
            copy(down_w.at[:, y, 1 - place.core, x], k, sibling)
            for k, (y, x) in enumerate((
                (place.y, place.x), (place.second_y, place.second_x), (place.first_y, place.first_x), (1 - place.y, 1 - place.x)
            ))
        ]

        def begin():
            for item in loads:
                item.start()
            meet(place)
            loads[1].wait()
            pass_on.start()
            across[1].start()
            loads[0].wait()
            across[0].start()
            loads[2].wait()
            across[2].start()

        def finish():
            arriving.wait_recv()
            across[3].start()
            for item in theirs:
                item.wait_recv()
            for item in across:
                item.wait_send()
            pass_on.wait_send()
    else:
        full = pltpu.make_async_copy(down_in, down_w, in_sem.at[1])
        begin, finish = full.start, full.wait

    def put(ref, c, at, value):
        ref[2 * c, at, :], ref[2 * c + 1, at, :] = value[:, :half], value[:, half:]

    def get(ref, c, at):
        return jnp.concatenate([ref[2 * c, at, :], ref[2 * c + 1, at, :]], axis=1)

    def down_rows(c):
        return down_w[c].reshape(piece, width)

    @pl.when(step == 0)
    def _():
        load_normed(0).start()
        for copy_up in load_up:
            copy_up.start()
        for k in range(1, steps):
            load_normed(k).start()
        norms_ref[...] = jnp.zeros_like(norms_ref)
        begin()

    @pl.when(step < steps)
    def _():
        at = tile(step)
        load_normed(step).wait()
        att = jnp.concatenate([att_ref[k, at, :] for k in range(att_ref.shape[0])], axis=1)
        unit, rstd = norm_parts(normed_all[at, :] + nn(att, out_w_ref[...]))
        unit_all[at, :] = unit.astype(LOW)
        rstd_all[at, :] = rstd
        normed = unit * gain_ref[1:2, :] + shift_ref[1:2, :]
        normed_all[at, :] = normed
        second_all[at, :] = normed.astype(LOW)
        for c in range(parts):
            pl.when(step == 0)(load_up[c].wait)
            act, deriv = gelu_pair(nn(second_all[at, :], up_ref[:, c * piece : (c + 1) * piece]))
            put(act_all, c, at, act.astype(LOW))
            put(up_all, c, at, deriv.astype(LOW))

    @pl.when(step == steps)
    def _():
        finish()

    @pl.when((step >= steps) & (step < 2 * steps))
    def _():
        at = pl.ds(pl.multiple_of((step - steps) * TILE, TILE), TILE)
        resid = normed_all[at, :]
        for c in range(parts):
            resid = resid + nn(get(act_all, c, at), down_rows(c))
        unit, rstd = norm_parts(resid)
        result_ref[...] = (unit * gain_ref[2:3, :] + shift_ref[2:3, :]).astype(LOW)
        cot = cot_ref[...].astype(F32)
        norms_ref[2] += fold(cot * unit)
        norms_ref[3] += fold(cot)
        grad = norm_back(cot, unit, rstd, gain_ref[2:3, :])
        down_all[at, :] = grad.astype(LOW)
        for c in range(parts):
            up_low = (nt(down_all[at, :], down_rows(c)) * get(up_all, c, at).astype(F32)).astype(LOW)
            put(up_all, c, at, up_low)
            grad = grad + nt(up_low, up_ref[:, c * piece : (c + 1) * piece])
        unit = unit_all[at, :].astype(F32)
        norms_ref[0] += fold(grad * unit)
        norms_ref[1] += fold(grad)
        grad = norm_back(grad, unit, rstd_all[at, :], gain_ref[1:2, :])
        normed_all[at, :] = grad
        low = grad.astype(LOW)
        attn_all[at, :] = low
        grad_att_ref[...] = nt(low, out_w_ref[...]).astype(LOW)

    @pl.when(step == 2 * steps)
    def _():
        write_two.start()
        att = jnp.concatenate([att_ref[k] for k in range(att_ref.shape[0])], axis=1)
        unit_all[pl.ds(0, width), :] = tn(att, attn_all[...]).astype(LOW)
        write_out.start()

    @pl.when(step >= 2 * steps)
    def _():
        turn = step - 2 * steps
        grad_down_ref[...] = tn(act_all[turn], down_all[...]).astype(LOW)
        grad_up_ref[...] = tn(second_all[...], up_all[turn]).astype(LOW)

    @pl.when(step == 2 * steps + turns - 1)
    def _():
        write_two.wait()
        write_out.wait()


def block_both(remote, depth, att, normed, cot, out_w, up, down, gains, shifts):
    tokens, width = normed.shape
    wide = up.shape[1]
    steps = tokens // TILE
    parts = depth if remote else 4
    piece = wide // parts
    tile = pl.BlockSpec((TILE, width), lambda s: (jnp.clip(s - steps, 0, steps - 1), 0))
    late = lambda s: jnp.maximum(s - 2 * steps, 0)
    hbm = pl.BlockSpec(memory_space=pl.ANY)
    down = down if remote else down.reshape(parts, piece, width)
    more = {"collective_id": CALLS["block"], "has_side_effects": True} if remote else {}
    wide_low = pltpu.VMEM((2 * parts, tokens, piece // 2), LOW)
    tall_low = pltpu.VMEM((tokens, width), LOW)
    return pl.pallas_call(
        functools.partial(block_kernel, remote, steps),
        grid=(2 * steps + 2 * parts,),
        in_specs=[
            whole(att.shape), hbm, tile, whole((width, width)), hbm, hbm, whole(gains.shape), whole(shifts.shape),
        ],
        out_specs=[
            tile, hbm, tile, hbm,
            pl.BlockSpec((width, piece // 2), lambda s: (0, late(s))),
            pl.BlockSpec((piece // 2, width), lambda s: (late(s), 0)),
            pl.BlockSpec((4, 8, width), lambda s: (0, 0, 0)),
        ],
        out_shape=[
            jax.ShapeDtypeStruct((tokens, width), LOW),
            jax.ShapeDtypeStruct((tokens, width), F32),
            jax.ShapeDtypeStruct((tokens, width), LOW),
            jax.ShapeDtypeStruct((width, width), LOW),
            jax.ShapeDtypeStruct(up.shape, LOW),
            jax.ShapeDtypeStruct((wide, width), LOW),
            jax.ShapeDtypeStruct((4, 8, width), F32),
        ],
        scratch_shapes=[
            wide_low, wide_low, tall_low, tall_low, tall_low,
            pltpu.VMEM((tokens, width), F32),
            tall_low,
            pltpu.VMEM((tokens, 1), F32),
            pltpu.VMEM(down.shape, LOW),
            pltpu.VMEM(up.shape, LOW),
            pltpu.SemaphoreType.DMA((4,)),
            pltpu.SemaphoreType.DMA((steps,)),
            pltpu.SemaphoreType.DMA((parts,)),
            pltpu.SemaphoreType.DMA((2,)),
        ]
        + ([pltpu.SemaphoreType.DMA((5,))] * 2 if remote else []),
        compiler_params=params(1, **more),
        name="block_both",
    )(att, normed, cot, out_w, up, down, gains, shifts)


class Scatter:
    def __init__(self, place, leaving, room, send, recv, group):
        self.place, self.leaving, self.send, self.recv, self.group = place, leaving, send, recv, group
        self.total, self.lands = room[0], room[1:]

    def copies(self, stage):
        p, total = self.place, self.total
        if stage == 0:
            found = [(self.leaving, self.lands[0], 0, p.at(p.z, p.y, 1 - p.core, p.x))]
        elif stage == 1:
            second = p.at(p.z, p.second_y, p.core, p.second_x)
            found = [
                (total.at[:, p.second_y, p.second_x], self.lands[1].at[0], 1, second),
                (total.at[:, 1 - p.y, 1 - p.x], self.lands[1].at[1], 2, second),
            ]
        elif stage == 2:
            first = p.at(p.z, p.first_y, p.core, p.first_x)
            found = [(total.at[:, p.first_y, p.first_x], self.lands[2], 3, first)]
        else:
            found = [
                (total.at[p.along(k), p.y, p.x], self.lands[3].at[k - 1], 3 + k, p.at(p.along(k), p.y, p.core, p.x))
                for k in range(1, p.depth)
            ]
        return [
            pltpu.make_async_remote_copy(
                src_ref=source, dst_ref=land, send_sem=self.send.at[self.group, slot],
                recv_sem=self.recv.at[self.group, slot], device_id=device, device_id_type=pl.DeviceIdType.MESH,
            )
            for source, land, slot, device in found
        ]

    def start(self, stage):
        for copy in self.copies(stage):
            copy.start()

    def arrive(self, stage):
        for copy in self.copies(stage):
            copy.wait_recv()

    def add(self, y, x, land):
        @pl.loop(0, self.place.depth)
        def _(z):
            self.total[z, y, x] = (self.total[z, y, x].astype(F32) + land(z).astype(F32)).astype(LOW)

    def fold(self, stage, go=True):
        p = self.place
        self.arrive(stage)
        if stage == 0:
            add = lambda y, x: self.add(y, x, lambda z: self.lands[0][z, y, x])
            add(p.second_y, p.second_x)
            add(1 - p.y, 1 - p.x)
            if go:
                self.start(1)
            add(p.first_y, p.first_x)
            add(p.y, p.x)
        elif stage == 1:
            self.add(p.first_y, p.first_x, lambda z: self.lands[1][1, z])
            if go:
                self.start(2)
            self.add(p.y, p.x, lambda z: self.lands[1][0, z])
        else:
            self.add(p.y, p.x, lambda z: self.lands[2][z])
            if go:
                self.start(3)

    def finish(self):
        p = self.place
        self.arrive(3)
        result = self.total[p.z, p.y, p.x].astype(F32)
        for k in range(p.depth - 1):
            result = result + self.lands[3][k].astype(F32)
        return result

    def sent(self, stages=4):
        for stage in range(stages):
            for copy in self.copies(stage):
                copy.wait_send()


class Tail:
    def __init__(self, place, parts, room, send, recv, own_sem, group):
        self.place = place
        self.total, self.land, self.far = room
        self.load = pltpu.make_async_copy(parts.at[1], self.total, own_sem.at[group])
        make = lambda source, land, slot, device: pltpu.make_async_remote_copy(
            src_ref=source, dst_ref=land, send_sem=send.at[group, slot], recv_sem=recv.at[group, slot],
            device_id=device, device_id_type=pl.DeviceIdType.MESH,
        )
        p = place
        self.across = make(parts.at[0], self.land, 0, p.at(p.z, p.first_y, p.core, p.first_x))
        self.along = [
            make(self.total.at[p.along(k)], self.far.at[k - 1], k, p.at(p.along(k), p.y, p.core, p.x))
            for k in range(1, p.depth)
        ]

    def fold(self):
        self.load.wait()
        self.across.wait_recv()

        @pl.loop(0, self.place.depth)
        def _(z):
            self.total[z] = (self.total[z].astype(F32) + self.land[z].astype(F32)).astype(LOW)

        for copy in self.along:
            copy.start()

    def finish(self):
        for copy in self.along:
            copy.wait_recv()
        result = self.total[self.place.z].astype(F32)
        for k in range(self.place.depth - 1):
            result = result + self.far[k].astype(F32)
        for copy in [self.across] + self.along:
            copy.wait_send()
        return result


def scatter_room(depth, share, cols, kept=()):
    return [
        pltpu.VMEM(shape + (share, cols), LOW)
        for shape in (kept + (depth, 2, 2), (depth, 2, 2), (2, depth), (depth,), (depth - 1,))
    ]


def attention_back_kernel(remote, pairs, *refs):
    (q_ref, k_ref, v_ref, grad_ref, probs_ref, far_ref, order_ref, low_ref) = refs[:8]
    refs = refs[8:]
    sources, refs = (refs[:3], refs[3:]) if remote else ((), refs)
    (dq_ref, dk_ref, dv_ref, rate_ref, grad_qkv_ref), refs = refs[:5], refs[5:]
    (down_ref, *parts), refs = (refs[:3], refs[3:]) if remote else ((None,), refs)
    (keys, values, grad_keys, grad_values, all_q, all_k, all_v), refs = refs[:7], refs[7:]
    step = pl.program_id(0)
    tokens = q_ref.shape[2]
    turns = all_q.shape[0] * pairs

    def when(k, action):
        @pl.when(step == k)
        def _():
            action()

    if remote:
        rooms, (send, recv, own_sem, part_sem) = [refs[5 * g : 5 * g + 5] for g in range(3)], refs[15:]
        place = Place(rooms[0][0].shape[0])
        own = [
            pltpu.make_async_copy(source.at[:, :, place.core], room[0], own_sem.at[g])
            for g, (source, room) in enumerate(zip(sources, rooms))
        ]
        groups = [
            Scatter(place, source.at[:, :, 1 - place.core], room, send, recv, g)
            for g, (source, room) in enumerate(zip(sources, rooms))
        ]
        down, out, up = groups

        def begin():
            for copy in own:
                copy.start()
            meet(place)
            down.start(0)

        def first(k, go=True):
            own[k].wait()
            groups[k].fold(0, go)

        when(0, begin)
        when(1, lambda: (first(0), out.start(0), up.start(0)))
        when(3, lambda: (first(1, False), first(2, False)))
        when(6, lambda: down.fold(1))
        when(8, lambda: (out.start(1), up.start(1)))
        when(10, lambda: down.fold(2))

    @pl.when(step < turns)
    def _():
        row, pair = lax.div(step, pairs), lax.rem(step, pairs)
        pad_rows(keys, k_ref[0, 0])
        pad_rows(values, v_ref[0, 0])
        grad_keys[...] = jnp.zeros_like(grad_keys)
        grad_values[...] = jnp.zeros_like(grad_values)
        sums = [jnp.zeros((8, BLOCK), F32)] * 4
        cols = pl.ds(pl.multiple_of(pair * BLOCK, BLOCK), BLOCK)
        for b in range(tokens // BLOCK):
            lanes = slice(b * BLOCK, (b + 1) * BLOCK)
            window = slice(b * BLOCK, b * BLOCK + SPAN)
            queries = pair_rows(q_ref[0, 0, lanes, :] * 0.125)
            grads = pair_rows(grad_ref[0, lanes, :])
            probs_low = probs_ref[0, 0, b]
            back = nt(values[window, :], grads)
            dist = jnp.where(far_ref[0, b] < FAR, far_ref[0, b], 0.0)
            order = order_ref[0, b]
            sides = []
            for h in range(2):
                probs = probs_low[:, h * BLOCK : (h + 1) * BLOCK].astype(F32)
                part = back[:, h * BLOCK : (h + 1) * BLOCK]
                delta = jnp.sum(probs * part, axis=0, keepdims=True)
                scores = probs * (part - delta)
                sums[2 * h] = sums[2 * h] - fold(scores * dist)
                sums[2 * h + 1] = sums[2 * h + 1] + fold(scores * order)
                sides.append(scores.astype(LOW))
            scores_low = jnp.concatenate(sides, axis=1)
            grad_values[window, :] += nn(probs_low, grads)
            grad_keys[window, :] += nn(scores_low, queries)
            grad_queries = (pair_pick(tn(scores_low, keys[window, :])) * 0.125).astype(LOW)
            dq_ref[0, lanes, :] = grad_queries
            all_q[row, lanes, cols] = grad_queries
        dk = grad_keys[pl.ds(RADIUS, tokens), :].astype(LOW)
        dv = grad_values[pl.ds(RADIUS, tokens), :].astype(LOW)
        dk_ref[0], all_k[row, :, cols] = dk, dk
        dv_ref[0], all_v[row, :, cols] = dv, dv
        for k in range(4):
            rate_ref[0, 0, k] = sums[k]

    for k, ref in enumerate((all_q, all_k, all_v)):
        @pl.when(step == turns + k)
        def _(ref=ref):
            flat = lambda v: v.reshape(-1, v.shape[-1])
            grad_qkv_ref[...] = tn(flat(low_ref[...]), flat(ref[...])).astype(LOW)

    if remote:
        def last():
            copies = []
            for k, (group, part) in enumerate(zip((out, up), parts)):
                group.fold(1, go=False)
                for side, (y, x) in enumerate(((place.first_y, place.first_x), (place.y, place.x))):
                    copies.append(pltpu.make_async_copy(group.total.at[:, y, x], part.at[side], part_sem.at[2 * k + side]))
                    copies[-1].start()
            down_ref[...] = down.finish()
            down.sent()
            out.sent(2)
            up.sent(2)
            for copy in copies:
                copy.wait()

        when(turns + 2, last)


def attention_backward(remote, depth, qkv, grad, probs, far, order, low, sources):
    pairs, rows, tokens = qkv.shape[0] // 3, qkv.shape[1], qkv.shape[2]
    width = pairs * BLOCK
    blocks = tokens // BLOCK
    turns = rows * pairs
    where = lambda s: (jnp.minimum(s, turns - 1) // pairs, jnp.minimum(s, turns - 1) % pairs)
    row_of, pair_of = lambda s: where(s)[0], lambda s: where(s)[1]
    part = lambda k: pl.BlockSpec((1, 1, tokens, BLOCK), lambda s: (k * pairs + pair_of(s), row_of(s), 0, 0))
    flat = pl.BlockSpec((1, tokens, BLOCK), lambda s: (row_of(s), 0, pair_of(s)))
    bias = pl.BlockSpec((1, blocks, SPAN, BLOCK), lambda s: (row_of(s), 0, 0, 0))
    grads = jax.ShapeDtypeStruct((rows, tokens, width), LOW)
    in_specs = [part(0), part(1), part(2), flat]
    in_specs += [pl.BlockSpec((1, 1, blocks, SPAN, 2 * BLOCK), lambda s: where(s) + (0, 0, 0)), bias, bias, whole(low.shape)]
    out_specs = [flat] * 3 + [
        pl.BlockSpec((1, 1, 4, 8, BLOCK), lambda s: where(s) + (0, 0, 0)),
        pl.BlockSpec((width, width), lambda s: (0, jnp.clip(s - turns, 0, 2))),
    ]
    out_shape = [grads] * 3 + [
        jax.ShapeDtypeStruct((rows, pairs, 4, 8, BLOCK), F32),
        jax.ShapeDtypeStruct((width, 3 * width), LOW),
    ]
    scratch = [pltpu.VMEM((tokens + 2 * RADIUS, BLOCK), LOW)] * 2
    scratch += [pltpu.VMEM((tokens + 2 * RADIUS, BLOCK), F32)] * 2
    scratch += [pltpu.VMEM((rows, tokens, width), LOW)] * 3
    more = {}
    if remote:
        in_specs += [pl.BlockSpec(memory_space=pl.ANY)] * 3
        for k, source in enumerate(sources):
            shape = source.shape[4:]
            if k == 0:
                out_specs.append(pl.BlockSpec(shape, lambda s: (0, 0)))
                out_shape.append(jax.ShapeDtypeStruct(shape, F32))
            else:
                out_specs.append(pl.BlockSpec(memory_space=pl.ANY))
                out_shape.append(jax.ShapeDtypeStruct((2, depth) + shape, LOW))
            scratch += scatter_room(depth, *shape)
        scratch += [pltpu.SemaphoreType.DMA((3, depth + 3))] * 2 + [pltpu.SemaphoreType.DMA((3,)), pltpu.SemaphoreType.DMA((4,))]
        more = {"collective_id": CALLS["attention"], "has_side_effects": True}
    return pl.pallas_call(
        functools.partial(attention_back_kernel, remote, pairs),
        grid=(turns + 3,),
        in_specs=in_specs,
        out_specs=out_specs,
        out_shape=out_shape,
        scratch_shapes=scratch,
        compiler_params=params(1, **more),
        name="attention_backward",
    )(qkv, qkv, qkv, grad, probs, far, order, low, *(sources if remote else ()))


def graph_back_kernel(remote, *refs):
    (dq_in, dk_in, dv_in, two_in, unit_in, rstd_in, slope_in, hidden_in, agg2_in, agg1_in, x_in, adj_in, cols_in,
     first_in, second_in, qkv_w_in, gain_ref, late_ref, rate_ref) = refs[:19]
    refs = refs[19:]
    (qkv_source, *parts), refs = (refs[:3], refs[3:]) if remote else ((None,), refs)
    (input_grad_out, edge_out, gains_out, shifts_out, rates_out), refs = refs[:5], refs[5:]
    owned, refs = (refs[:7], refs[7:]) if remote else (refs[:2], refs[2:])
    (dq, dk, dv, two, unit, rstd, slope, hidden, agg2, adj, cols, first_w, second_w, qkv_w,
     back, norms, edge_sums, row_sem, in_sem, out_sem), refs = refs[:20], refs[20:]
    rows, tokens, width = dq.shape
    blocks, chunk = tokens // BLOCK, 2 * BLOCK
    chunks = tokens // chunk
    agg1, x, branch, mean, pre, one = agg2, hidden, dq, dk, dv, two

    by_row = [(dq_in, dq), (dk_in, dk), (dv_in, dv), (two_in, two), (unit_in, unit), (rstd_in, rstd)]
    row_load = lambda k, row: pltpu.make_async_copy(by_row[k][0].at[row], by_row[k][1].at[row], row_sem.at[k, row])
    once = [(qkv_w_in, qkv_w), (second_in, second_w), (cols_in, cols), (hidden_in, hidden), (agg2_in, agg2),
            (adj_in, adj), (slope_in, slope), (first_in, first_w), (x_in, x), (agg1_in, agg1)]
    load = lambda k: pltpu.make_async_copy(*once[k], in_sem.at[k])
    load(0).start()
    for k in range(len(by_row)):
        row_load(k, 0).start()
    load(1).start()
    load(2).start()
    for row in range(1, rows):
        for k in range(len(by_row)):
            row_load(k, row).start()
    for k in range(3, 8):
        load(k).start()

    if remote:
        rooms = [refs[5 * g : 5 * g + 5] for g in range(4)]
        sums, s_land, s_far, send, recv, own_sem, s_send, s_recv = refs[20:28]
        tails = (refs[28:31], refs[31:34])
        depth = rooms[0][0].shape[0]
        place = Place(depth)
        own = pltpu.make_async_copy(qkv_source.at[:, :, place.core], rooms[0][0], own_sem.at[0])
        qkv = Scatter(place, qkv_source.at[:, :, 1 - place.core], rooms[0], send, recv, 0)
        late, early, final = [
            Scatter(place, room[0].at[1], (room[0].at[0],) + tuple(room[1:]), send, recv, 1 + g)
            for g, room in enumerate(rooms[1:])
        ]
        out, up = [
            Tail(place, part, room, send, recv, own_sem, 4 + g)
            for g, (part, room) in enumerate(zip(parts, tails))
        ]
        own.start()
        out.load.start()
        up.load.start()
        meet(place)
        qkv.start(0)
        out.across.start()
        up.across.start()

    norms[...] = jnp.zeros_like(norms)
    edge_sums[...] = jnp.zeros_like(edge_sums)
    flat = lambda ref: ref[...].reshape(rows * tokens, width)

    def weight_grad(dest, col, left, right):
        half = width // 2
        for part in range(2):
            grad = tn(left[:, :, part * half : (part + 1) * half].reshape(rows * tokens, half), flat(right))
            if not remote:
                dest[part * half : (part + 1) * half, col * width : (col + 1) * width] = grad.astype(LOW)
                continue
            share = dest.shape[4]
            for k in range(half // share):
                index = part * (half // share) + k
                z, y, core, x_at = index // 8, index // 4 % 2, index // 2 % 2, index % 2
                side = place.core if core == 0 else 1 - place.core
                dest[side, z, y, x_at, :, col * width : (col + 1) * width] = grad[k * share : (k + 1) * share].astype(LOW)

    def spread(row, source):
        back[...] = jnp.zeros_like(back)
        for b in range(blocks):
            back[b * BLOCK : b * BLOCK + WIDE, :] += nn(adj[row, b], source[row, b * BLOCK : (b + 1) * BLOCK, :])

    load(0).wait()
    load(1).wait()
    load(2).wait()

    @pl.loop(0, rows)
    def _(row):
        for k in range(len(by_row)):
            row_load(k, row).wait()
        for c in range(chunks):
            part = slice(c * chunk, (c + 1) * chunk)
            grad = two[row, part, :]
            for k, ref in enumerate((dq, dk, dv)):
                grad = grad + nt(ref[row, part, :], qkv_w[:, k * width : (k + 1) * width])
            plain = unit[row, part, :].astype(F32)
            norms[0] += fold(grad * plain)
            norms[1] += fold(grad)
            grad = norm_back(grad, plain, rstd[row, part, :], gain_ref[0:1, :])
            one[row, part, :] = grad
            low = grad.astype(LOW)
            branch[row, part, :] = low
            mean[row, part, :] = (nt(low, second_w[:, width : 2 * width]) * cols[row, part, 2:3]).astype(LOW)
            if remote and c == 0:
                @pl.when(row == 0)
                def _():
                    own.wait()
                    qkv.fold(0)

    load(3).wait()
    load(4).wait()
    second_dest, first_dest = (rooms[1][0], rooms[2][0]) if remote else (owned[1], owned[0])
    weight_grad(second_dest, 0, hidden, branch)
    weight_grad(second_dest, 1, agg2, branch)
    load(8).start()
    load(9).start()
    if remote:
        late.start(0)
        out.fold()
        up.fold()
        qkv.fold(1)
    for k in range(5, 8):
        load(k).wait()

    @pl.loop(0, rows)
    def _(row):
        spread(row, mean)
        for c in range(chunks):
            part = slice(c * chunk, (c + 1) * chunk)
            grad = back[REACH + c * chunk : REACH + (c + 1) * chunk, :]
            grad = grad + nt(branch[row, part, :], second_w[:, 0:width])
            grad = grad * slope[row, part, :].astype(F32)
            edge_sums[0] += fold(grad * cols[row, part, 0:1])
            edge_sums[1] += fold(grad * cols[row, part, 1:2])
            low = grad.astype(LOW)
            pre[row, part, :] = low
            if remote and c == 0:
                @pl.when(row == 0)
                def _():
                    late.fold(0)
    load(8).wait()
    load(9).wait()
    weight_grad(first_dest, 0, x, pre)
    if remote:
        early.start(0)
    weight_grad(rooms[3][0] if remote else first_dest, 0 if remote else 1, agg1, pre)

    line = lambda v: jnp.sum(v, axis=0, keepdims=True)
    lines = jnp.concatenate(
        [line(edge_sums[0]), line(edge_sums[1]), line(norms[0]), line(late_ref[0]), line(late_ref[2]),
         line(norms[1]), line(late_ref[1]), line(late_ref[3])], axis=0,
    )
    rates = jnp.sum(jnp.sum(rate_ref[...], axis=0), axis=2).reshape(-1, BLOCK)

    if remote:
        final.start(0)
        early.fold(0)
        pieces = width // BLOCK
        for k in range(pieces):
            sums[0, k] = lines[:, k * BLOCK : (k + 1) * BLOCK]
        for k in range(3):
            sums[0, pieces + k] = rates[8 * k : 8 * (k + 1)]
        turns = [
            (sums.at[k], s_land.at[k], k, device)
            for k, device in enumerate((
                place.at(place.z, place.y, 1 - place.core, place.x),
                place.at(place.z, place.y, place.core, 1 - place.x),
                place.at(place.z, 1 - place.y, place.core, place.x),
            ))
        ] + [
            (s_far.at[place.z], s_far.at[place.z], 2 + k, place.at(place.along(k), place.y, place.core, place.x))
            for k in range(1, depth)
        ]
        turns = [
            pltpu.make_async_remote_copy(
                src_ref=source, dst_ref=land, send_sem=s_send.at[slot], recv_sem=s_recv.at[slot],
                device_id=device, device_id_type=pl.DeviceIdType.MESH,
            )
            for source, land, slot, device in turns
        ]
        turns[0].start()
        qkv.fold(2)
        late.fold(1)

    writes = lambda row: pltpu.make_async_copy(one.at[row], input_grad_out.at[row], out_sem.at[row])

    @pl.loop(0, rows)
    def _(row):
        for c in range(chunks):
            part = slice(c * chunk, (c + 1) * chunk)
            mean[row, part, :] = (nt(pre[row, part, :], first_w[:, width : 2 * width]) * cols[row, part, 2:3]).astype(LOW)
        if remote:
            @pl.when(row == 0)
            def _():
                final.fold(0)
                turns[0].wait_recv()
                sums[1] = sums[0] + s_land[0]
                turns[1].start()
        spread(row, mean)
        for c in range(chunks):
            part = slice(c * chunk, (c + 1) * chunk)
            grad = one[row, part, :] + back[REACH + c * chunk : REACH + (c + 1) * chunk, :]
            one[row, part, :] = grad + nt(pre[row, part, :], first_w[:, 0:width])
        writes(row).start()
        if remote:
            @pl.when(row == 0)
            def _():
                early.fold(1)

    if remote:
        turns[1].wait_recv()
        sums[2] = sums[1] + s_land[1]
        turns[2].start()
        late.fold(2)
        final.fold(1)
        early.fold(2)
        turns[2].wait_recv()
        s_far[place.z] = sums[2] + s_land[2]
        for turn in turns[3:]:
            turn.start()
        owned[5][...] = out.finish()
        owned[6][...] = up.finish()
        owned[4][...] = qkv.finish()
        final.fold(2)
        result = late.finish()
        owned[2][...] = result[:, :width]
        owned[3][...] = result[:, width:]
        for turn in turns[3:]:
            turn.wait_recv()
        total = s_far[0]
        for k in range(1, depth):
            total = total + s_far[k]
        for k in range(pieces):
            part = slice(k * BLOCK, (k + 1) * BLOCK)
            edge_out[:, part] = total[k, 0:2]
            gains_out[:, part] = total[k, 2:5]
            shifts_out[:, part] = total[k, 5:8]
        for k in range(3):
            rates_out[8 * k : 8 * (k + 1)] = jnp.sum(total[pieces + k], axis=1, keepdims=True)
        owned[0][...] = early.finish()
        owned[1][...] = final.finish()
        for group in (qkv, late, early, final):
            group.sent()
        for turn in turns:
            turn.wait_send()
    else:
        edge_out[...], gains_out[...], shifts_out[...] = lines[0:2], lines[2:5], lines[5:8]
        rates_out[...] = jnp.sum(rates, axis=1, keepdims=True)
    for row in range(rows):
        writes(row).wait()


def graph_backward(remote, depth, arrays, gains, late, rates, sources):
    dq, two, unit, rstd, slope, hidden, adj, cols = (arrays[k] for k in (0, 3, 4, 5, 6, 7, 11, 12))
    rows, tokens, width = dq.shape
    vmem, hbm = pl.BlockSpec(memory_space=pltpu.VMEM), pl.BlockSpec(memory_space=pl.ANY)
    shape = lambda dtype, *dims: jax.ShapeDtypeStruct(dims, dtype)
    out_shape = [
        shape(F32, rows, tokens, width), shape(F32, 2, width), shape(F32, 3, width), shape(F32, 3, width),
        shape(F32, rates.shape[1] * 4, 1),
    ]
    like = lambda v: pltpu.VMEM(v.shape, v.dtype)
    scratch = [like(v) for v in (dq, dq, dq, two, unit, rstd, slope, hidden, hidden, adj, cols) + tuple(arrays[13:16])]
    scratch += [
        pltpu.VMEM((tokens + 2 * REACH, width), F32),
        pltpu.VMEM((2, 8, width), F32),
        pltpu.VMEM((2, 8, width), F32),
        pltpu.SemaphoreType.DMA((6, rows)),
        pltpu.SemaphoreType.DMA((10,)),
        pltpu.SemaphoreType.DMA((rows,)),
    ]
    more = {}
    if remote:
        share = sources[0].shape[4]
        out_shape += [shape(F32, share, width)] * 4 + [shape(F32, share, s.shape[-1]) for s in sources]
        scratch += scatter_room(depth, share, sources[0].shape[5])
        for cols in (2 * width, width, width):
            scratch += scatter_room(depth, share, cols, (2,))
        lines = (width // BLOCK + 3, 8, BLOCK)
        scratch += [pltpu.VMEM((3,) + lines, F32), pltpu.VMEM((3,) + lines, F32), pltpu.VMEM((depth,) + lines, F32)]
        scratch += [pltpu.SemaphoreType.DMA((6, depth + 3))] * 2 + [pltpu.SemaphoreType.DMA((6,))]
        scratch += [pltpu.SemaphoreType.DMA((depth + 2,))] * 2
        for part in sources[1:]:
            scratch += [pltpu.VMEM((k, share, part.shape[3]), LOW) for k in (depth, depth, depth - 1)]
        more = {"collective_id": CALLS["graph"], "has_side_effects": True}
    else:
        out_shape += [shape(LOW, width, 2 * width)] * 2
    return pl.pallas_call(
        functools.partial(graph_back_kernel, remote),
        in_specs=[hbm] * 16 + [vmem] * 3 + [hbm] * (3 if remote else 0),
        out_specs=[hbm] + [vmem] * (len(out_shape) - 1),
        out_shape=out_shape,
        scratch_shapes=scratch,
        compiler_params=pltpu.CompilerParams(vmem_limit_bytes=VMEM, **more),
        name="graph_backward",
    )(*arrays, gains, late, rates, *(sources if remote else ()))


def local(
    sizes, inputs, coords, neighbours, counts, doc_length, self_one, near_one, self_two, near_two, edge_proj,
    qkv_proj, out_proj, up_proj, down_proj, norm_gains, norm_shifts, distance_rate, order_rate, cotangent,
):
    axes = ("wide", "narrow")
    rows, tokens, width = inputs.shape
    wide_size, narrow_size = sizes
    depth = wide_size // 4
    remote = wide_size % 4 == 0 and narrow_size == 2 and self_one.shape[0] % 8 == 0
    weights, shards = (self_one, near_one, self_two, near_two, qkv_proj), (out_proj, up_proj, down_proj)
    gather = lambda v: lax.all_gather(v, axes, axis=0, tiled=True)
    scatter = lambda v: lax.psum_scatter(v, axes, scatter_dimension=0, tiled=True).astype(F32)
    blocked = lambda v: v.reshape(depth, 2, 2, 2, -1, v.shape[1])
    flat = lambda v: v.reshape(rows * tokens, width)
    tall = lambda v: v.reshape(rows, tokens, width)
    if not remote:
        weights, shards = tuple(map(gather, weights)), tuple(map(gather, shards))
    results = front(
        remote, depth, doc_length[:, 0], distance_rate, order_rate, neighbours, counts[:, None, :], coords, inputs,
        edge_proj, norm_gains, norm_shifts, weights, shards if remote else (),
    )
    (adj, cols, agg1, slope, hidden, agg2, unit, rstd, normed, low, qkv, att, probs, far, order, first_w, second_w, qkv_w) = results[:18]
    out_w, up = (v.reshape(-1, v.shape[-1]) for v in results[18:20]) if remote else shards[:2]
    result, two, grad_att, grad_out, grad_up, grad_down, late = block_both(
        remote, depth, att.reshape(-1, rows * tokens, BLOCK), flat(normed), flat(cotangent), out_w, up, results[20] if remote else shards[2],
        norm_gains, norm_shifts,
    )
    first_sources = (blocked(grad_down), blocked(grad_out), blocked(grad_up)) if remote else ()
    dq, dk, dv, rates, grad_qkv, *summed = attention_backward(
        remote, depth, qkv, tall(grad_att), probs, far, order, low, first_sources
    )
    arrays = (dq, dk, dv, tall(two), unit, rstd, slope, hidden, agg2, agg1, inputs, adj, cols, first_w, second_w, qkv_w)
    sources = (blocked(grad_qkv), summed[1], summed[2]) if remote else ()
    input_grad, edge, gains, shifts, rates, *owned = graph_backward(remote, depth, arrays, norm_gains, late, rates, sources)
    if remote:
        down_own = summed[0]
        self1, near1, self2, near2, qkv_own, out_own, up_own = owned
    else:
        down_own, out_own, up_own, qkv_own = map(scatter, (grad_down, grad_out, grad_up, grad_qkv))
        self1, near1 = jnp.split(scatter(owned[0]), 2, axis=1)
        self2, near2 = jnp.split(scatter(owned[1]), 2, axis=1)
        edge, gains, shifts, rates = lax.psum((edge, gains, shifts, rates), axes)
    rates = rates.reshape(-1, 2, 2)
    return (
        tall(result), input_grad, self1, near1, self2, near2, edge, qkv_own, out_own, up_own, down_own, gains, shifts,
        rates[:, :, 0].reshape(-1), rates[:, :, 1].reshape(-1),
    )


def solution(mesh):
    axes = ("wide", "narrow")
    middle, last = P(None, axes, None), P(None, None, axes)
    count, weight, same = P(None, axes), P(axes, None), P()
    sizes = (mesh.shape["wide"], mesh.shape["narrow"])
    return jax.shard_map(
        functools.partial(local, sizes),
        mesh=mesh,
        in_specs=(middle, last, last, count, count)
        + (weight,) * 4
        + (same,)
        + (weight,) * 4
        + (same,) * 4
        + (middle,),
        out_specs=(middle, middle) + (weight,) * 4 + (same,) + (weight,) * 4 + (same,) * 4,
        check_vma=False,
    )
```
